512 devices in a mesh: seq: 64 (over x, z), track: 8 (over y, core).
Axes of the slice: x: 4, y: 4, z: 16, core: 2. Of those that a mesh axis runs over, the one named last changes fastest.
Arguments:
- embeddings: bfloat16 [768, 131072], P('track', 'seq'), may hold values from -1000 to 1000, as said below
- taps: bfloat16 [5, 768], P(None, 'track'), may hold values from -3 to 3
- head_weight: bfloat16 [768, 768], P('track'), may hold values from -0.21875 to 0.21875
- targets: float32 [768, 131072], P('track', 'seq'), may hold values from 0.04 to 15, as said below
Outputs:
- embed_grad: bfloat16 [768, 131072], P('track', 'seq')
- weight_grad: float32 [768, 768], P('track')
- taps_grad: float32 [5, 768], P(None, 'track')
The draws below stay inside these ranges and needn't reach their ends.
Inputs may be any that keep to these rules, and one draw needn't show every extreme that they name: embeddings are real-valued. targets are positive counts.
All inputs are finite; a program needn't handle non-finite values.
Results may differ from the reference program's by a relative error of at most 0.02.
Values may be sent and summed in bfloat16 or wider, within the bound.
No kernel may reach another device: no remote copies, remote signals or barrier semaphores. Data moves between devices by JAX's collectives and lax.ppermute only.
A program may use at most 64 MiB of HBM per device.

```python
import jax
import jax.numpy as jnp
from jax import lax

D = 768
TR = 768
TAPS = 5
L = 131072
N_TRACK = 8


def draw_embeddings(key, part):
    key = jax.random.fold_in(key, 11)
    first = jax.random.fold_in(key, 0)
    base = jax.random.normal(first, (D, L), jnp.float32)
    base = jnp.clip(base, -6.0, 6.0)
    return base.astype(jnp.bfloat16)


def draw_targets(key, part):
    key = jax.random.fold_in(key, 23)
    level = jax.random.uniform(key, (TR, L), jnp.float32, -3.0, 1.6)
    ramp = 1.0 + 2.0 * jnp.arange(L, dtype=jnp.float32) / L
    return jnp.exp(level) * ramp[None, :]


def level_of(rng, dims, cuts, low, high):
    level = 1.0
    for position, blocks in cuts:
        steps = jax.random.uniform(jax.random.fold_in(jax.random.fold_in(rng, 6), position), (blocks,), jnp.float32, low / len(cuts), high / len(cuts))
        level = level * jnp.repeat(jnp.exp(steps), dims[position] // blocks).reshape((-1,) + (1,) * (len(dims) - 1 - position))
    return level


def noise(stream_key, dims, scale, bound, cuts=(), kind=jnp.bfloat16):
    array = jax.random.normal(stream_key, dims, jnp.float32) * scale
    if len(cuts) > 0:
        array = level_of(stream_key, dims, cuts, -0.22, 0.18) * array
    return jnp.clip(array, min=-bound, max=bound).astype(kind)


def setup_inputs(seed: int = 0) -> dict:
    seeds = jax.random.split(jax.random.key(seed), 5)
    embeddings = draw_embeddings(jax.random.fold_in(seeds[4], 71), 0)
    taps = noise(seeds[1], (TAPS, D), 0.5, 3.0, ((1, 8),))
    head_weight = noise(seeds[2], (TR, D), D ** -0.5, 0.21875, ((0, 8),))
    targets = draw_targets(jax.random.fold_in(seeds[4], 71), 0)
    return dict(embeddings=embeddings, taps=taps, head_weight=head_weight, targets=targets)


def reference(embeddings, taps, head_weight, targets):
    rows_first = embeddings.T
    weight_rows = head_weight.T
    target_rows = targets.T
    length = rows_first.shape[0]
    width = TAPS // 2
    emb32 = rows_first.astype(jnp.float32)
    tap32 = taps.astype(jnp.float32)
    padded = jnp.pad(emb32, ((width, width), (0, 0)))
    conv = jnp.zeros((length, D), jnp.float32)
    for k in range(TAPS):
        conv = conv + tap32[k][None, :] * padded[k:k + length]
    hidden = jax.nn.silu(conv).astype(jnp.bfloat16)
    logits = jnp.dot(hidden, weight_rows, preferred_element_type=jnp.float32)
    peak = jnp.max(logits, axis=0)
    expo = jnp.exp(logits - peak[None, :])
    total = jnp.sum(expo, axis=0)
    counts = jnp.sum(target_rows, axis=0)
    logit_grad = (counts[None, :] * expo / total[None, :] - target_rows).astype(jnp.bfloat16)
    weight_grad = jnp.dot(hidden.T, logit_grad, preferred_element_type=jnp.float32)
    group = TR // N_TRACK
    grad_three = logit_grad.reshape(length, N_TRACK, group)
    weight_three = weight_rows.reshape(D, N_TRACK, group)

    def add_group(j, acc):
        part = jnp.dot(grad_three[:, j, :], weight_three[:, j, :].T, preferred_element_type=jnp.float32)
        part = lax.optimization_barrier(part.astype(jnp.bfloat16))
        return acc + part.astype(jnp.float32)

    hidden_grad = lax.fori_loop(0, N_TRACK, add_group, jnp.zeros((length, D), jnp.float32))
    sig = jax.nn.sigmoid(conv)
    conv_grad = (hidden_grad * sig * (1.0 + conv * (1.0 - sig))).astype(jnp.bfloat16)
    dpad = jnp.pad(conv_grad.astype(jnp.float32), ((width, width), (0, 0)))
    embed_grad = jnp.zeros((length, D), jnp.float32)
    for k in range(TAPS):
        embed_grad = embed_grad + tap32[k][None, :] * dpad[2 * width - k:2 * width - k + length]
    grad32 = conv_grad.astype(jnp.float32)
    taps_grad = jnp.stack([jnp.sum(padded[k:k + length] * grad32, axis=0) for k in range(TAPS)])
    return embed_grad.T.astype(jnp.bfloat16), weight_grad.T, taps_grad
```

```python
import jax
import jax.numpy as jnp
import numpy as np
from jax import lax
from jax.sharding import Mesh
from jax.sharding import PartitionSpec as P

F32 = jnp.float32
BF16 = jnp.bfloat16
SEQ = ("x", "z")


def ring(count, shift):
    return [(i, (i + shift) % count) for i in range(count)]


def along_y(value, shift):
    return lax.ppermute(value, "y", ring(lax.axis_size("y"), shift))


def other_core(value):
    return lax.ppermute(value, "c", [(0, 1), (1, 0)])


def halo(cells, width):
    count = lax.axis_size(SEQ)
    head = cells[:, :width]
    tail = cells[:, -width:]
    left = lax.ppermute(tail, SEQ, [(i, i + 1) for i in range(count - 1)])
    right = lax.ppermute(head, SEQ, [(i + 1, i) for i in range(count - 1)])
    return jnp.concatenate([left, cells, right], axis=1)


def exchange(value, axes):
    count = lax.axis_size(axes)
    copies = jnp.broadcast_to(value[None], (count,) + value.shape)
    return lax.all_to_all(copies, axes, 0, 0, tiled=True)


def gather_track(block):
    half = block.shape[0] // 2
    above = along_y(block, -1)
    below = along_y(block, 1)
    far_low = along_y(below[:half], 1)
    far_high = along_y(above[half:], -1)
    mine = jnp.concatenate([block, above, far_low, far_high, below], axis=0)
    theirs = [other_core(part) for part in (block, above, below)]
    far = other_core(jnp.concatenate([far_low, far_high], axis=0))
    return jnp.concatenate([mine, theirs[0], theirs[1], far, theirs[2]], axis=0)


def scatter_track(kept, sent):
    width = kept.shape[0] // 4
    half = width // 2
    both = (kept.astype(F32) + other_core(sent).astype(F32)).reshape(4, width, -1)
    narrow = both.astype(BF16)
    low = along_y(narrow[2, :half], 1)
    high = along_y(narrow[2, half:], -1)
    up = jnp.concatenate(
        [(both[1, :half] + low.astype(F32)).astype(BF16), narrow[1, half:]], axis=0
    )
    down = jnp.concatenate(
        [narrow[3, :half], (both[3, half:] + high.astype(F32)).astype(BF16)], axis=0
    )
    from_below = along_y(up, 1)
    from_above = along_y(down, -1)
    return both[0] + from_below.astype(F32) + from_above.astype(F32)


def shards(embeddings, taps, head_weight, targets):
    width = embeddings.shape[0]
    count = embeddings.shape[1]
    tracks = head_weight.shape[0]
    ntaps = taps.shape[0]
    reach = ntaps // 2
    y = lax.axis_index("y")
    c = lax.axis_index("c")
    ny = lax.axis_size("y")
    tap = taps.astype(F32)

    blocks = head_weight.reshape(tracks, ny, 2, width)
    twice = jnp.concatenate([blocks, blocks], axis=1)
    turned = lax.dynamic_slice_in_dim(twice, y, ny, axis=1)
    first = jnp.where(c == 0, turned[:, :, 0], turned[:, :, 1]).reshape(tracks, ny * width)
    second = jnp.where(c == 0, turned[:, :, 1], turned[:, :, 0]).reshape(tracks, ny * width)

    padded = halo(embeddings, reach).astype(F32)
    conv = jnp.zeros((width, count), F32)
    for k in range(ntaps):
        conv = conv + tap[k][:, None] * padded[:, k : k + count]
    hidden = gather_track(jax.nn.silu(conv).astype(BF16))

    logits = jnp.dot(
        jnp.concatenate([first, second], axis=1), hidden, preferred_element_type=F32
    )
    top = jnp.max(logits, axis=1)
    expo = jnp.exp(logits - top[:, None])
    stats = jnp.stack([top, jnp.sum(expo, axis=1), jnp.sum(targets, axis=1)])
    every = exchange(stats, SEQ)
    peak = jnp.max(every[:, 0], axis=0)
    total = jnp.sum(every[:, 1] * jnp.exp(every[:, 0] - peak[None]), axis=0)
    counts = jnp.sum(every[:, 2], axis=0)
    scale = counts * jnp.exp(top - peak) / total
    logit_grad = (scale[:, None] * expo - targets).astype(BF16)

    turn = (((0,), (0,)), ((), ()))
    sent = lax.dot_general(second, logit_grad, turn, preferred_element_type=F32).astype(BF16)
    kept = lax.dot_general(first, logit_grad, turn, preferred_element_type=F32).astype(BF16)
    hidden_grad = scatter_track(kept, sent)

    local = lax.dot_general(
        hidden, logit_grad, (((1,), (1,)), ((), ())), preferred_element_type=F32
    ).reshape(2, ny, width, tracks)
    local = jnp.where(c == 0, local, local[::-1])
    local = lax.dynamic_slice_in_dim(
        jnp.concatenate([local, local], axis=1), (ny - y) % ny, ny, axis=1
    )
    local = local.transpose(1, 0, 2, 3).reshape(2 * ny * width, tracks)
    nx, nz = lax.axis_size("x"), lax.axis_size("z")
    part = local.reshape(nx, -1, tracks)
    part = jnp.sum(lax.all_to_all(part, "x", 0, 0, tiled=True), axis=0)
    part = part.reshape(nz, -1, tracks)
    part = jnp.sum(lax.all_to_all(part, "z", 0, 0, tiled=True), axis=0)

    sig = jax.nn.sigmoid(conv)
    conv_grad = (hidden_grad * sig * (1.0 + conv * (1.0 - sig))).astype(BF16)
    grad_float = conv_grad.astype(F32)
    local_taps = jnp.stack(
        [jnp.sum(padded[:, k : k + count] * grad_float, axis=1) for k in range(ntaps)]
    )
    slab = exchange(jnp.concatenate([part, local_taps], axis=0), "z")
    rows = part.shape[0]
    taps_z = jnp.sum(slab[:, rows:], axis=0)
    slab = exchange(
        jnp.concatenate([slab[:, :rows].reshape(-1, tracks), taps_z], axis=0), "x"
    )
    rows = rows * nz
    weight_grad = slab[:, :rows].reshape(-1, tracks).T
    taps_grad = jnp.sum(slab[:, rows:], axis=0)

    grad_pad = halo(conv_grad, reach).astype(F32)
    embed_grad = jnp.zeros((width, count), F32)
    for k in range(ntaps):
        start = 2 * reach - k
        embed_grad = embed_grad + tap[k][:, None] * grad_pad[:, start : start + count]
    return embed_grad.astype(BF16), weight_grad, taps_grad


def solution(mesh):
    fine = Mesh(np.asarray(mesh.devices).reshape(4, 16, 4, 2), ("x", "z", "y", "c"))
    track = ("y", "c")
    return jax.shard_map(
        shards,
        mesh=fine,
        in_specs=(P(track, SEQ), P(None, track), P(track, None), P(track, SEQ)),
        out_specs=(P(track, SEQ), P(track, None), P(None, track)),
        check_vma=False,
    )
```

```python
import jax
import jax.numpy as jnp
import numpy as np
from jax import lax
from jax.sharding import Mesh
from jax.sharding import PartitionSpec as P

F32 = jnp.float32
BF16 = jnp.bfloat16
SEQ = ("x", "z")


def ring(count, shift):
    return [(i, (i + shift) % count) for i in range(count)]


def along_y(value, shift):
    return lax.ppermute(value, "y", ring(lax.axis_size("y"), shift))


def other_core(value):
    return lax.ppermute(value, "c", [(0, 1), (1, 0)])


def halo(cells, width):
    count = lax.axis_size(SEQ)
    head = cells[:, :width]
    tail = cells[:, -width:]
    left = lax.ppermute(tail, SEQ, [(i, i + 1) for i in range(count - 1)])
    right = lax.ppermute(head, SEQ, [(i + 1, i) for i in range(count - 1)])
    return jnp.concatenate([left, cells, right], axis=1)


def share(value, axes):
    count = lax.axis_size(axes)
    copies = jnp.broadcast_to(value.reshape(1, 1, -1), (count, 1, value.size))
    return lax.all_to_all(copies, axes, 0, 0, tiled=True)[:, 0]


def scatter_track(kept, sent):
    width = kept.shape[0] // 4
    half = width // 2
    both = (kept.astype(F32) + other_core(sent).astype(F32)).reshape(4, width, -1)
    narrow = both.astype(BF16)
    low = along_y(narrow[2, :half], 1)
    high = along_y(narrow[2, half:], -1)
    up = jnp.concatenate(
        [(both[1, :half] + low.astype(F32)).astype(BF16), narrow[1, half:]], axis=0
    )
    down = jnp.concatenate(
        [narrow[3, :half], (both[3, half:] + high.astype(F32)).astype(BF16)], axis=0
    )
    from_below = along_y(up, 1)
    from_above = along_y(down, -1)
    return both[0] + from_below.astype(F32) + from_above.astype(F32)


def convolve(cells, tap, offsets, count):
    result = jnp.zeros((cells.shape[0], count), F32)
    for k, start in enumerate(offsets):
        result = result + tap[k][:, None] * cells[:, start : start + count]
    return result


def shards(embeddings, taps, head_weight, targets):
    width = embeddings.shape[0]
    count = embeddings.shape[1]
    tracks = head_weight.shape[0]
    ntaps = taps.shape[0]
    reach = ntaps // 2
    y = lax.axis_index("y")
    c = lax.axis_index("c")
    ny = lax.axis_size("y")
    nseq = lax.axis_size(SEQ)
    me = lax.axis_index(SEQ)
    features = ny * 2 * width
    tap = taps.astype(F32)
    steps = list(range(ntaps))

    bare = jnp.pad(embeddings, ((0, 0), (reach, reach))).astype(F32)
    early = jax.nn.silu(convolve(bare, tap, steps, count)).astype(BF16)
    gathered = lax.all_gather(early, ("y", "c"), axis=0, tiled=True)

    padded = halo(embeddings, reach).astype(F32)
    conv = convolve(padded, tap, steps, count)
    sig = jax.nn.sigmoid(conv)
    slope = sig * (1.0 + conv * (1.0 - sig))
    lanes = 128
    late = conv * sig
    rim = jnp.concatenate([late[:, : lanes // 2], late[:, -lanes // 2 :]], axis=1).astype(BF16)
    rims = lax.all_to_all(
        jnp.broadcast_to(rim[None], (2 * ny, width, lanes)), ("y", "c"), 0, 0, tiled=True
    ).reshape(features, lanes)
    place = jnp.arange(lanes)[None, :]
    hidden = jnp.concatenate(
        [
            jnp.where(place < reach, rims, gathered[:, :lanes]),
            gathered[:, lanes:-lanes],
            jnp.where(place >= lanes - reach, rims, gathered[:, -lanes:]),
        ],
        axis=1,
    )

    blocks = head_weight.reshape(tracks, ny, 2, width)
    twice = jnp.concatenate([blocks, blocks], axis=1)
    turned = lax.dynamic_slice_in_dim(twice, y, ny, axis=1)
    first = jnp.where(c == 0, turned[:, :, 0], turned[:, :, 1]).reshape(tracks, ny * width)
    second = jnp.where(c == 0, turned[:, :, 1], turned[:, :, 0]).reshape(tracks, ny * width)

    logits = jnp.dot(head_weight, hidden, preferred_element_type=F32)
    top = jnp.max(logits, axis=1)
    expo = jnp.exp(logits - top[:, None])
    stats = jnp.concatenate([top, jnp.sum(expo, axis=1), jnp.sum(targets, axis=1)])
    every = share(stats, SEQ)
    tops = every[:, :tracks]
    peak = jnp.max(tops, axis=0)
    total = jnp.sum(every[:, tracks : 2 * tracks] * jnp.exp(tops - peak[None]), axis=0)
    counts = jnp.sum(every[:, 2 * tracks :], axis=0)
    scale = counts * jnp.exp(top - peak) / total
    logit_grad = (scale[:, None] * expo - targets).astype(BF16)

    turn = (((0,), (0,)), ((), ()))
    sent = lax.dot_general(second, logit_grad, turn, preferred_element_type=F32).astype(BF16)
    kept = lax.dot_general(first, logit_grad, turn, preferred_element_type=F32).astype(BF16)
    hidden_grad = scatter_track(kept, sent)

    local = lax.dot_general(
        logit_grad, hidden, (((1,), (1,)), ((), ())), preferred_element_type=F32
    ).reshape(nseq, 1, -1)
    part = jnp.sum(lax.all_to_all(local, SEQ, 0, 0, tiled=True), axis=0).reshape(-1)

    conv_grad = (hidden_grad * slope).astype(BF16)
    grad_float = conv_grad.astype(F32)
    local_taps = jnp.concatenate(
        [jnp.sum(padded[:, k : k + count] * grad_float, axis=1) for k in range(ntaps)]
    )
    row = jnp.arange(nseq)[:, None]
    head = grad_float[:, :reach].T.reshape(1, -1)
    tail = grad_float[:, -reach:].T.reshape(1, -1)
    edge = jnp.where(row == me + 1, tail, jnp.where(row == me - 1, head, 0.0))
    same = jnp.concatenate([part, local_taps])
    message = jnp.concatenate(
        [jnp.broadcast_to(same[None], (nseq, same.size)), edge], axis=1
    )
    slab = lax.all_to_all(message[:, None], SEQ, 0, 0, tiled=True)[:, 0]
    weight_grad = slab[:, : part.size].reshape(tracks, features)
    taps_grad = jnp.sum(slab[:, part.size : same.size], axis=0).reshape(ntaps, width)
    edges = slab[:, same.size :]
    left = jnp.sum(jnp.where(row == me - 1, edges, 0.0), axis=0).reshape(reach, width).T
    right = jnp.sum(jnp.where(row == me + 1, edges, 0.0), axis=0).reshape(reach, width).T

    grad_pad = jnp.concatenate([left, grad_float, right], axis=1)
    embed_grad = convolve(grad_pad, tap, [2 * reach - k for k in steps], count)
    return embed_grad.astype(BF16), weight_grad, taps_grad


def solution(mesh):
    fine = Mesh(np.asarray(mesh.devices).reshape(4, 16, 4, 2), ("x", "z", "y", "c"))
    track = ("y", "c")
    return jax.shard_map(
        shards,
        mesh=fine,
        in_specs=(P(track, SEQ), P(None, track), P(track, None), P(track, SEQ)),
        out_specs=(P(track, SEQ), P(track, None), P(None, track)),
        check_vma=False,
    )
```

```python
import functools

import jax
import jax.numpy as jnp
import numpy as np
from jax import lax
from jax.experimental import pallas as pl
from jax.experimental.pallas import tpu as pltpu
from jax.sharding import Mesh
from jax.sharding import PartitionSpec as P

F32 = jnp.float32
BF16 = jnp.bfloat16
SEQ = ("x", "z")
LANES = 128


def ring(count, shift):
    return [(i, (i + shift) % count) for i in range(count)]


def along_y(value, shift):
    return lax.ppermute(value, "y", ring(lax.axis_size("y"), shift))


def other_core(value):
    return lax.ppermute(value, "c", [(0, 1), (1, 0)])


def outer_columns(cells, width):
    count = lax.axis_size(SEQ)
    left = lax.ppermute(cells[:, -width:], SEQ, [(i, i + 1) for i in range(count - 1)])
    right = lax.ppermute(cells[:, :width], SEQ, [(i + 1, i) for i in range(count - 1)])
    return left, right


def share(value, axes):
    count = lax.axis_size(axes)
    copies = jnp.broadcast_to(value.reshape(1, 1, -1), (count, 1, value.size))
    return lax.all_to_all(copies, axes, 0, 0, tiled=True)[:, 0]


ORDER = ((0, 0), (0, 1), (1, 0), (3, 0), (1, 1), (3, 1), (2, 0), (2, 1))


def gather_track(block):
    half = block.shape[0] // 2
    above = along_y(block, -1)
    below = along_y(block, 1)
    beside = other_core(block)
    far_low = along_y(below[:half], 1)
    far_high = along_y(above[half:], -1)
    above_beside = other_core(above)
    below_beside = other_core(below)
    far = jnp.concatenate([far_low, far_high], axis=0)
    far_beside = other_core(far)
    return jnp.concatenate(
        [block, beside, above, below, above_beside, below_beside, far, far_beside], axis=0
    )


def scatter_sends(kept, sent):
    width = kept.shape[0] // 4
    half = width // 2
    both = (kept.astype(F32) + other_core(sent).astype(F32)).reshape(4, width, -1)
    narrow = both.astype(BF16)
    low = along_y(narrow[2, :half], 1)
    high = along_y(narrow[2, half:], -1)
    up = jnp.concatenate(
        [(both[1, :half] + low.astype(F32)).astype(BF16), narrow[1, half:]], axis=0
    )
    down = jnp.concatenate(
        [narrow[3, :half], (both[3, half:] + high.astype(F32)).astype(BF16)], axis=0
    )
    return both[0], up, down, narrow


def forward_kernel(cells, left, right, tap, hidden, slope, line):
    reach = left.shape[1]
    count = cells.shape[1]
    line[:, :LANES] = jnp.zeros((cells.shape[0], LANES), F32)
    line[:, LANES + count :] = jnp.zeros((cells.shape[0], LANES), F32)
    line[:, LANES - reach : LANES] = left[...].astype(F32)
    line[:, LANES + count : LANES + count + reach] = right[...].astype(F32)
    line[:, LANES : LANES + count] = cells[...].astype(F32)
    rows = 8

    @pl.loop(0, cells.shape[0] // 16)
    def _(block):
        both_hidden = []
        for part in range(2):
            at = pl.ds(pl.multiple_of(block * 16 + part * rows, rows), rows)
            whole = line[at, :]
            taps = tap[at, :]
            conv = jnp.zeros((rows, count), F32)
            for k in range(2 * reach + 1):
                shift = (reach - k) % whole.shape[1]
                moved = pltpu.roll(whole, shift, 1) if shift else whole
                conv = conv + taps[:, k : k + 1] * moved[:, LANES : LANES + count]
            sig = jax.nn.sigmoid(conv)
            both_hidden.append((conv * sig).astype(BF16))
            slope[at, :] = sig * (1.0 + conv * (1.0 - sig))
        out = pl.ds(pl.multiple_of(block * 16, 16), 16)
        hidden[out, :] = jnp.concatenate(both_hidden, axis=0)


def forward(cells, left, right, tap):
    rows, count = cells.shape
    return pl.pallas_call(
        forward_kernel,
        out_shape=(
            jax.ShapeDtypeStruct((rows, count), BF16),
            jax.ShapeDtypeStruct((rows, count), F32),
        ),
        scratch_shapes=[pltpu.VMEM((rows, count + 2 * LANES), F32)],
        compiler_params=pltpu.CompilerParams(vmem_limit_bytes=16 * 2**20),
        cost_estimate=pl.CostEstimate(
            flops=20 * rows * count, bytes_accessed=8 * rows * count, transcendentals=rows * count
        ),
        name="conv_silu",
    )(cells, left, right, tap)


def shards(embeddings, taps, head_weight, targets):
    width = embeddings.shape[0]
    count = embeddings.shape[1]
    tracks = head_weight.shape[0]
    ntaps = taps.shape[0]
    reach = ntaps // 2
    y = lax.axis_index("y")
    c = lax.axis_index("c")
    ny = lax.axis_size("y")
    nseq = lax.axis_size(SEQ)
    me = lax.axis_index(SEQ)
    features = ny * 2 * width
    tap = taps.astype(F32)

    left, right = outer_columns(embeddings, reach)
    block, slope = forward(embeddings, left, right, jnp.pad(tap, ((0, 8 - ntaps), (0, 0))).T)
    hidden = gather_track(block)

    blocks = head_weight.reshape(tracks, ny, 2, width)
    twice = jnp.concatenate([blocks, blocks], axis=1)
    turned = lax.dynamic_slice_in_dim(twice, y, ny, axis=1)
    turned = (
        jnp.where(c == 0, turned[:, :, 0], turned[:, :, 1]),
        jnp.where(c == 0, turned[:, :, 1], turned[:, :, 0]),
    )
    first = turned[0].reshape(tracks, ny * width)
    second = turned[1].reshape(tracks, ny * width)
    ordered = jnp.concatenate([turned[core][:, dy] for dy, core in ORDER], axis=1)

    logits = jnp.dot(ordered, hidden, preferred_element_type=F32)
    top = jnp.max(logits, axis=1)
    expo = jnp.exp(logits - top[:, None])
    stats = jnp.concatenate([top, jnp.sum(expo, axis=1), jnp.sum(targets, axis=1)])
    every = share(stats, SEQ)
    tops = every[:, :tracks]
    peak = jnp.max(tops, axis=0)
    total = jnp.sum(every[:, tracks : 2 * tracks] * jnp.exp(tops - peak[None]), axis=0)
    counts = jnp.sum(every[:, 2 * tracks :], axis=0)
    scale = counts * jnp.exp(top - peak) / total
    logit_grad = (scale[:, None] * expo - targets).astype(BF16)

    turn = (((0,), (0,)), ((), ()))
    sent = lax.dot_general(second, logit_grad, turn, preferred_element_type=F32).astype(BF16)
    kept = lax.dot_general(first, logit_grad, turn, preferred_element_type=F32).astype(BF16)
    mine, up, down, narrow = scatter_sends(kept, sent)

    late_grad, _ = lax.optimization_barrier((logit_grad, narrow))
    local = lax.dot_general(
        hidden, late_grad, (((1,), (1,)), ((), ())), preferred_element_type=F32
    ).reshape(2 * ny, width, tracks)
    sorted_blocks = [
        [local[ORDER.index((dy, core))] for dy in range(ny)] for core in range(2)
    ]
    by_core = jnp.stack([jnp.stack(sorted_blocks[0]), jnp.stack(sorted_blocks[1])], axis=1)
    by_core = jnp.where(c == 0, by_core, by_core[:, ::-1])
    by_core = lax.dynamic_slice_in_dim(
        jnp.concatenate([by_core, by_core], axis=0), (ny - y) % ny, ny, axis=0
    )
    local = by_core.reshape(features, tracks).T.reshape(nseq, 1, -1)
    local, up, down = lax.optimization_barrier((local, up, down))
    from_below = along_y(up, 1)
    from_above = along_y(down, -1)
    part = jnp.sum(lax.all_to_all(local, SEQ, 0, 0, tiled=True), axis=0).reshape(-1)

    hidden_grad = mine + from_below.astype(F32) + from_above.astype(F32)
    conv_grad = (hidden_grad * slope).astype(BF16)
    grad_float = conv_grad.astype(F32)
    padded = jnp.concatenate([left, embeddings, right], axis=1).astype(F32)
    local_taps = jnp.concatenate(
        [jnp.sum(padded[:, k : k + count] * grad_float, axis=1) for k in range(ntaps)]
    )
    high = lax.reduce_precision(local_taps, 8, 7)
    low = local_taps - high
    row = jnp.arange(nseq)[:, None]
    head = conv_grad[:, :reach].T.reshape(1, -1)
    tail = conv_grad[:, -reach:].T.reshape(1, -1)
    zero = jnp.zeros((), BF16)
    edge = jnp.where(row == me + 1, tail, jnp.where(row == me - 1, head, zero))
    same = jnp.concatenate([part, high, low]).astype(BF16)
    message = jnp.concatenate(
        [jnp.broadcast_to(same[None], (nseq, same.size)), edge], axis=1
    )
    slab = lax.all_to_all(message[:, None], SEQ, 0, 0, tiled=True)[:, 0]
    weight_grad = slab[:, : part.size].reshape(tracks, features).astype(F32)
    sums = jnp.sum(slab[:, part.size : same.size].astype(F32), axis=0).reshape(2, ntaps, width)
    taps_grad = sums[0] + sums[1]
    edges = slab[:, same.size :]
    before = jnp.sum(jnp.where(row == me - 1, edges, zero).astype(F32), axis=0)
    after = jnp.sum(jnp.where(row == me + 1, edges, zero).astype(F32), axis=0)

    grad_pad = jnp.concatenate(
        [before.reshape(reach, width).T, grad_float, after.reshape(reach, width).T], axis=1
    )
    embed_grad = jnp.zeros((width, count), F32)
    for k in range(ntaps):
        start = 2 * reach - k
        embed_grad = embed_grad + tap[k][:, None] * grad_pad[:, start : start + count]
    return embed_grad.astype(BF16), weight_grad, taps_grad


def solution(mesh):
    fine = Mesh(np.asarray(mesh.devices).reshape(4, 16, 4, 2), ("x", "z", "y", "c"))
    track = ("y", "c")
    return jax.shard_map(
        shards,
        mesh=fine,
        in_specs=(P(track, SEQ), P(None, track), P(track, None), P(track, SEQ)),
        out_specs=(P(track, SEQ), P(track, None), P(None, track)),
        check_vma=False,
    )
```

```python
import functools

import jax
import jax.numpy as jnp
import numpy as np
from jax import lax
from jax.experimental import pallas as pl
from jax.experimental.pallas import tpu as pltpu
from jax.sharding import Mesh
from jax.sharding import PartitionSpec as P

F32 = jnp.float32
BF16 = jnp.bfloat16
SEQ = ("x", "z")
LANES = 128


def along_y(value, shift):
    count = lax.axis_size("y")
    return lax.ppermute(value, "y", [(i, (i + shift) % count) for i in range(count)])


def other_core(value):
    return lax.ppermute(value, "c", [(0, 1), (1, 0)])


def outer_columns(cells, width):
    count = lax.axis_size(SEQ)
    left = lax.ppermute(cells[:, -width:], SEQ, [(i, i + 1) for i in range(count - 1)])
    right = lax.ppermute(cells[:, :width], SEQ, [(i + 1, i) for i in range(count - 1)])
    return left, right


def share(value, axes):
    count = lax.axis_size(axes)
    copies = jnp.broadcast_to(value.reshape(1, 1, -1), (count, 1, value.size))
    return lax.all_to_all(copies, axes, 0, 0, tiled=True)[:, 0]


def forward_kernel(cells, left, right, tap, hidden, slope, line):
    reach = left.shape[1]
    count = cells.shape[1]
    line[:, :LANES] = jnp.zeros((cells.shape[0], LANES), F32)
    line[:, LANES + count :] = jnp.zeros((cells.shape[0], LANES), F32)
    line[:, LANES - reach : LANES] = left[...].astype(F32)
    line[:, LANES + count : LANES + count + reach] = right[...].astype(F32)
    line[:, LANES : LANES + count] = cells[...].astype(F32)
    rows = 8

    @pl.loop(0, cells.shape[0] // 16)
    def _(block):
        both_hidden = []
        for part in range(2):
            at = pl.ds(pl.multiple_of(block * 16 + part * rows, rows), rows)
            whole = line[at, :]
            taps = tap[at, :]
            conv = jnp.zeros((rows, count), F32)
            for k in range(2 * reach + 1):
                shift = (reach - k) % whole.shape[1]
                moved = pltpu.roll(whole, shift, 1) if shift else whole
                conv = conv + taps[:, k : k + 1] * moved[:, LANES : LANES + count]
            sig = jax.nn.sigmoid(conv)
            both_hidden.append((conv * sig).astype(BF16))
            slope[at, :] = sig * (1.0 + conv * (1.0 - sig))
        out = pl.ds(pl.multiple_of(block * 16, 16), 16)
        hidden[out, :] = jnp.concatenate(both_hidden, axis=0)


def forward(cells, left, right, tap):
    rows, count = cells.shape
    return pl.pallas_call(
        forward_kernel,
        out_shape=(
            jax.ShapeDtypeStruct((rows, count), BF16),
            jax.ShapeDtypeStruct((rows, count), F32),
        ),
        scratch_shapes=[pltpu.VMEM((rows, count + 2 * LANES), F32)],
        compiler_params=pltpu.CompilerParams(vmem_limit_bytes=16 * 2**20),
        cost_estimate=pl.CostEstimate(
            flops=20 * rows * count, bytes_accessed=8 * rows * count, transcendentals=rows * count
        ),
        name="conv_silu",
    )(cells, left, right, tap)


def scatter_kernel(place, weight, grad, received, mine, one, two, three, total):
    width = mine.shape[0]
    chips = weight.shape[0] // width
    chunk = total.shape[1]
    for start in range(0, grad.shape[1], chunk):
        at = pl.ds(start, chunk)
        part = jnp.dot(weight[...], grad[:, at], preferred_element_type=F32)
        total[...] = part + received[:, at].astype(F32)
        for shift, out in enumerate((mine, one, two, three)):
            row = lax.rem(place[0] + shift, chips) * width
            out[:, at] = total[pl.ds(pl.multiple_of(row, 16), width), :].astype(out.dtype)


def scatter_blocks(place, weight, grad, received):
    features, tracks = weight.shape
    count = grad.shape[1]
    width = features // 4
    sent = jax.ShapeDtypeStruct((width, count), BF16)
    return pl.pallas_call(
        scatter_kernel,
        out_shape=(jax.ShapeDtypeStruct((width, count), F32), sent, sent, sent),
        in_specs=[pl.BlockSpec(memory_space=pltpu.SMEM)]
        + [pl.BlockSpec(memory_space=pltpu.VMEM)] * 3,
        scratch_shapes=[pltpu.VMEM((features, 512), F32)],
        compiler_params=pltpu.CompilerParams(vmem_limit_bytes=24 * 2**20),
        cost_estimate=pl.CostEstimate(
            flops=2 * features * tracks * count,
            bytes_accessed=5 * features * count,
            transcendentals=0,
        ),
        name="core_sum",
    )(place, weight, grad, received)


def outer_kernel(core, grad, mine, theirs, out, table):
    tracks = grad.shape[0]
    width = mine.shape[0] // 4
    along = (((1,), (1,)), ((), ()))
    for block, offset in ((mine, core[0]), (theirs, 1 - core[0])):
        part = lax.dot_general(block[...], grad[...], along, preferred_element_type=F32)
        for chip in range(4):
            row = (2 * chip + offset) * width
            at = pl.ds(pl.multiple_of(row, 16), width)
            table[at, :tracks] = part[chip * width : (chip + 1) * width]
    out[...] = table[...].T[:tracks]


def outer_product(core, grad, mine, theirs):
    tracks, count = grad.shape
    features = 2 * mine.shape[0]
    return pl.pallas_call(
        outer_kernel,
        out_shape=jax.ShapeDtypeStruct((tracks, features), F32),
        in_specs=[pl.BlockSpec(memory_space=pltpu.SMEM)]
        + [pl.BlockSpec(memory_space=pltpu.VMEM)] * 3,
        scratch_shapes=[pltpu.VMEM((features, LANES), F32)],
        compiler_params=pltpu.CompilerParams(vmem_limit_bytes=16 * 2**20),
        cost_estimate=pl.CostEstimate(
            flops=2 * features * tracks * count,
            bytes_accessed=2 * features * count,
            transcendentals=0,
        ),
        name="weight_part",
    )(core, grad, mine, theirs)


def backward_kernel(mine, one, two, three, slope, cells, left, right, grad, sums, line, table):
    reach = left.shape[1]
    count = cells.shape[1]
    rows = 16
    lane = lax.broadcasted_iota(jnp.int32, (rows, LANES), 1)
    line[:, :LANES] = jnp.zeros((rows, LANES), F32)
    line[:, LANES + count :] = jnp.zeros((rows, LANES), F32)

    @pl.loop(0, cells.shape[0] // rows)
    def _(block):
        at = pl.ds(pl.multiple_of(block * rows, rows), rows)
        total = mine[at, :] + one[at, :].astype(F32)
        total = total + two[at, :].astype(F32) + three[at, :].astype(F32)
        value = (total * slope[at, :]).astype(BF16)
        grad[at, :] = value
        value = value.astype(F32)
        line[:, LANES - reach : LANES] = left[at, :].astype(F32)
        line[:, LANES + count : LANES + count + reach] = right[at, :].astype(F32)
        line[:, LANES : LANES + count] = cells[at, :].astype(F32)
        whole = line[...]
        found = jnp.zeros((rows, LANES), F32)
        for k in range(2 * reach + 1):
            shift = (reach - k) % whole.shape[1]
            moved = pltpu.roll(whole, shift, 1) if shift else whole
            product = moved[:, LANES : LANES + count] * value
            found = jnp.where(lane == k, jnp.sum(product, axis=1, keepdims=True), found)
        table[at, :] = found

    sums[...] = table[...].T[: sums.shape[0]]


def backward(mine, parts, slope, cells, left, right):
    rows, count = cells.shape
    return pl.pallas_call(
        backward_kernel,
        out_shape=(
            jax.ShapeDtypeStruct((rows, count), BF16),
            jax.ShapeDtypeStruct((8, rows), F32),
        ),
        scratch_shapes=[
            pltpu.VMEM((16, count + 2 * LANES), F32),
            pltpu.VMEM((rows, LANES), F32),
        ],
        compiler_params=pltpu.CompilerParams(vmem_limit_bytes=16 * 2**20),
        cost_estimate=pl.CostEstimate(
            flops=20 * rows * count, bytes_accessed=18 * rows * count, transcendentals=0
        ),
        name="conv_grad",
    )(mine, *parts, slope, cells, left, right)


def shards(embeddings, taps, head_weight, targets):
    width = embeddings.shape[0]
    count = embeddings.shape[1]
    tracks = head_weight.shape[0]
    ntaps = taps.shape[0]
    reach = ntaps // 2
    y = lax.axis_index("y")
    c = lax.axis_index("c")
    ny = lax.axis_size("y")
    nseq = lax.axis_size(SEQ)
    me = lax.axis_index(SEQ)
    features = ny * 2 * width
    tap = taps.astype(F32)

    left, right = outer_columns(embeddings, reach)
    block, slope = forward(embeddings, left, right, jnp.pad(tap, ((0, 8 - ntaps), (0, 0))).T)

    mine = lax.all_to_all(
        jnp.broadcast_to(block[None], (ny, width, count)), "y", 0, 0, tiled=True
    ).reshape(ny * width, count)
    theirs = other_core(mine)
    late_weight, _ = lax.optimization_barrier((head_weight, block))
    blocks = late_weight.reshape(tracks, ny, 2, width)
    halves = blocks[:, :, 0].reshape(tracks, -1), blocks[:, :, 1].reshape(tracks, -1)
    first = jnp.where(c == 0, halves[0], halves[1])
    second = jnp.where(c == 0, halves[1], halves[0])

    logits = jnp.dot(first, mine, preferred_element_type=F32)
    logits = logits + jnp.dot(second, theirs, preferred_element_type=F32)
    top = jnp.max(logits, axis=1)
    expo = jnp.exp(logits - top[:, None])
    stats = jnp.concatenate([top, jnp.sum(expo, axis=1), jnp.sum(targets, axis=1)])
    every = share(stats, SEQ)
    tops = every[:, :tracks]
    peak = jnp.max(tops, axis=0)
    total = jnp.sum(every[:, tracks : 2 * tracks] * jnp.exp(tops - peak[None]), axis=0)
    counts = jnp.sum(every[:, 2 * tracks :], axis=0)
    scale = counts * jnp.exp(top - peak) / total
    logit_grad = (scale[:, None] * expo - targets).astype(BF16)

    sent = jnp.dot(second.T, logit_grad, preferred_element_type=F32).astype(BF16)
    received = other_core(sent)

    nx, nz = lax.axis_size("x"), lax.axis_size("z")
    late_grad, _ = lax.optimization_barrier((logit_grad, sent))
    local = outer_product(c.reshape(1), late_grad, mine, theirs)
    part = lax.all_to_all(local.reshape(nx, tracks // nx, features), "x", 0, 0, tiled=True)

    own, *blocks = scatter_blocks(y.reshape(1), first.T, logit_grad, received)
    parts = [along_y(block, shift) for shift, block in ((2, blocks[1]), (1, blocks[0]), (3, blocks[2]))]
    part = jnp.sum(part, axis=0).reshape(nz, 1, -1)
    part = jnp.sum(lax.all_to_all(part, "z", 0, 0, tiled=True), axis=0).reshape(-1)

    conv_grad, local_taps = backward(own, parts, slope, embeddings, left, right)
    local_taps = local_taps[:ntaps].reshape(-1)
    high = lax.reduce_precision(local_taps, 8, 7)
    low = local_taps - high
    row = jnp.arange(nseq)[:, None]
    head = conv_grad[:, :reach].T.reshape(1, -1)
    tail = conv_grad[:, -reach:].T.reshape(1, -1)
    zero = jnp.zeros((), BF16)
    edge = jnp.where(row == me + 1, tail, jnp.where(row == me - 1, head, zero))
    both = jnp.concatenate([high, low]).astype(BF16)
    both = jnp.broadcast_to(both[None], (nseq, both.size))
    same = jnp.broadcast_to(part.astype(BF16)[None], (nseq, part.size))
    message = jnp.stack([same, jnp.concatenate([both, edge], axis=1)], axis=1)
    slab = lax.all_to_all(message, SEQ, 0, 0, tiled=True)
    weight_grad = slab[:, 0].reshape(tracks, features).astype(F32)
    sums = jnp.sum(slab[:, 1, : both.shape[1]].astype(F32), axis=0).reshape(2, ntaps, width)
    taps_grad = sums[0] + sums[1]
    edges = slab[:, 1, both.shape[1] :]
    before = jnp.sum(jnp.where(row == me - 1, edges, zero).astype(F32), axis=0)
    after = jnp.sum(jnp.where(row == me + 1, edges, zero).astype(F32), axis=0)

    grad_pad = jnp.concatenate(
        [before.reshape(reach, width).T, conv_grad.astype(F32), after.reshape(reach, width).T], axis=1
    )
    embed_grad = jnp.zeros((width, count), F32)
    for k in range(ntaps):
        start = 2 * reach - k
        embed_grad = embed_grad + tap[k][:, None] * grad_pad[:, start : start + count]
    return embed_grad.astype(BF16), weight_grad, taps_grad


def solution(mesh):
    fine = Mesh(np.asarray(mesh.devices).reshape(4, 16, 4, 2), ("x", "z", "y", "c"))
    track = ("y", "c")
    return jax.shard_map(
        shards,
        mesh=fine,
        in_specs=(P(track, SEQ), P(None, track), P(track, None), P(track, SEQ)),
        out_specs=(P(track, SEQ), P(track, None), P(None, track)),
        check_vma=False,
    )
```

```python
import functools

import jax
import jax.numpy as jnp
import numpy as np
from jax import lax
from jax.experimental import pallas as pl
from jax.experimental.pallas import tpu as pltpu
from jax.sharding import Mesh
from jax.sharding import PartitionSpec as P

F32 = jnp.float32
BF16 = jnp.bfloat16
SEQ = ("x", "z")
LANES = 128


def along_y(value, shift):
    count = lax.axis_size("y")
    return lax.ppermute(value, "y", [(i, (i + shift) % count) for i in range(count)])


def other_core(value):
    return lax.ppermute(value, "c", [(0, 1), (1, 0)])


def outer_columns(cells, width):
    count = lax.axis_size(SEQ)
    left = lax.ppermute(cells[:, -width:], SEQ, [(i, i + 1) for i in range(count - 1)])
    right = lax.ppermute(cells[:, :width], SEQ, [(i + 1, i) for i in range(count - 1)])
    return left, right


def share(value, axes):
    count = lax.axis_size(axes)
    copies = jnp.broadcast_to(value.reshape(1, 1, -1), (count, 1, value.size))
    return lax.all_to_all(copies, axes, 0, 0, tiled=True)[:, 0]


def tap_columns(tap, square):
    count, features = tap.shape
    square[:, :] = jnp.zeros(square.shape, F32)
    square[:count, :features] = tap[...].astype(F32)
    return square[...].T


def forward_kernel(
    cells_hbm, left, right, tap_hbm, hidden, line, square, columns, cells, tap, sems
):
    reads = [
        pltpu.make_async_copy(tap_hbm, tap, sems.at[0]),
        pltpu.make_async_copy(cells_hbm, cells, sems.at[1]),
    ]
    for read in reads:
        read.start()
    reach = left.shape[1]
    count = cells.shape[1]
    line[:, :LANES] = jnp.zeros((cells.shape[0], LANES), F32)
    line[:, LANES + count :] = jnp.zeros((cells.shape[0], LANES), F32)
    line[:, LANES - reach : LANES] = left[...].astype(F32)
    line[:, LANES + count : LANES + count + reach] = right[...].astype(F32)
    rows = 8
    reads[0].wait()
    columns[...] = tap_columns(tap, square)
    reads[1].wait()
    line[:, LANES : LANES + count] = cells[...].astype(F32)

    @pl.loop(0, cells.shape[0] // 16)
    def _(block):
        both_hidden = []
        for part in range(2):
            at = pl.ds(pl.multiple_of(block * 16 + part * rows, rows), rows)
            whole = line[at, :]
            taps = columns[at, :]
            conv = jnp.zeros((rows, count), F32)
            for k in range(2 * reach + 1):
                shift = (reach - k) % whole.shape[1]
                moved = pltpu.roll(whole, shift, 1) if shift else whole
                conv = conv + taps[:, k : k + 1] * moved[:, LANES : LANES + count]
            sig = jax.nn.sigmoid(conv)
            both_hidden.append((conv * sig).astype(BF16))
        out = pl.ds(pl.multiple_of(block * 16, 16), 16)
        hidden[out, :] = jnp.concatenate(both_hidden, axis=0)


def forward(cells, left, right, tap):
    rows, count = cells.shape
    return pl.pallas_call(
        forward_kernel,
        out_shape=jax.ShapeDtypeStruct((rows, count), BF16),
        in_specs=[
            pl.BlockSpec(memory_space=pl.ANY),
            pl.BlockSpec(memory_space=pltpu.VMEM),
            pl.BlockSpec(memory_space=pltpu.VMEM),
            pl.BlockSpec(memory_space=pl.ANY),
        ],
        scratch_shapes=[
            pltpu.VMEM((rows, count + 2 * LANES), F32),
            pltpu.VMEM((8, LANES), F32),
            pltpu.VMEM((LANES, 8), F32),
            pltpu.VMEM(cells.shape, cells.dtype),
            pltpu.VMEM(tap.shape, tap.dtype),
            pltpu.SemaphoreType.DMA((2,)),
        ],
        compiler_params=pltpu.CompilerParams(vmem_limit_bytes=8 * 2**20),
        cost_estimate=pl.CostEstimate(
            flops=20 * rows * count, bytes_accessed=4 * rows * count, transcendentals=rows * count
        ),
        name="conv_silu",
    )(cells, left, right, tap)


def pick_rows(weight, picked, blocks):
    width = picked.shape[0] // 4
    for chip, block in enumerate(blocks):
        at = pl.ds(pl.multiple_of(block * width, 16), width)
        picked[chip * width : (chip + 1) * width, :] = weight[at, :]


TURN = (((0,), (0,)), ((), ()))


def near_kernel(place, weight, hidden, targets, logits, counts, picked):
    pick_rows(weight, picked, [2 * chip + place[1] for chip in range(4)])
    logits[...] = lax.dot_general(picked[...], hidden[...], TURN, preferred_element_type=F32)
    counts[...] = jnp.broadcast_to(jnp.sum(targets[...], axis=1, keepdims=True), counts.shape)


def far_kernel(place, weight, hidden, near, counts, expo, stats, picked, table):
    tracks = near.shape[0]
    pick_rows(weight, picked, [2 * chip + 1 - place[1] for chip in range(4)])
    logits = lax.dot_general(picked[...], hidden[...], TURN, preferred_element_type=F32)
    logits = logits + near[...]
    top = jnp.max(logits, axis=1, keepdims=True)
    value = jnp.exp(logits - top)
    expo[...] = value
    total = jnp.sum(value, axis=1, keepdims=True)
    lane = lax.broadcasted_iota(jnp.int32, (tracks, LANES), 1)
    table[...] = jnp.zeros(table.shape, F32)
    table[:tracks, :] = jnp.where(lane == 0, top, jnp.where(lane == 1, total, counts[...]))
    stats[...] = table[...].T[: stats.shape[0]]


def kernel_call(body, name, outs, scratch, place, *operands, flops=0):
    size = sum(o.size * o.dtype.itemsize for o in operands)
    size += sum(o.size * o.dtype.itemsize for o in outs)
    return pl.pallas_call(
        body,
        out_shape=outs,
        in_specs=[pl.BlockSpec(memory_space=pltpu.SMEM)]
        + [pl.BlockSpec(memory_space=pltpu.VMEM)] * len(operands),
        scratch_shapes=scratch,
        compiler_params=pltpu.CompilerParams(vmem_limit_bytes=size + 4 * 2**20),
        cost_estimate=pl.CostEstimate(flops=flops, bytes_accessed=size, transcendentals=0),
        name=name,
    )(place, *operands)


def near_logits(place, weight, hidden, targets):
    tracks, count = targets.shape
    outs = (
        jax.ShapeDtypeStruct((tracks, count), F32),
        jax.ShapeDtypeStruct((tracks, LANES), F32),
    )
    scratch = [pltpu.VMEM((hidden.shape[0], tracks), BF16)]
    return kernel_call(
        near_kernel, "near_logits", outs, scratch, place, weight, hidden, targets,
        flops=2 * hidden.size * tracks,
    )


def far_logits(place, weight, hidden, near, counts):
    tracks = near.shape[0]
    outs = (
        jax.ShapeDtypeStruct(near.shape, F32),
        jax.ShapeDtypeStruct((8, LANES), F32),
    )
    scratch = [
        pltpu.VMEM((hidden.shape[0], tracks), BF16),
        pltpu.VMEM((LANES, LANES), F32),
    ]
    return kernel_call(
        far_kernel, "far_logits", outs, scratch, place, weight, hidden, near, counts,
        flops=2 * hidden.size * tracks,
    )


def grad_kernel(place, weight, scale, expo, targets, grad, sent, picked):
    tracks = expo.shape[0]
    column = scale[...].T[:tracks, 0:1]
    value = (column * expo[...] - targets[...]).astype(BF16)
    grad[...] = value
    blocks = [2 * lax.rem(place[0] + shift, 4) + 1 - place[1] for shift in range(4)]
    pick_rows(weight, picked, blocks)
    sent[...] = jnp.dot(picked[...], value, preferred_element_type=F32).astype(BF16)


def logit_gradient(place, weight, scale, expo, targets):
    tracks, count = expo.shape
    outs = (
        jax.ShapeDtypeStruct((tracks, count), BF16),
        jax.ShapeDtypeStruct((weight.shape[0] // 2, count), BF16),
    )
    scratch = [pltpu.VMEM((weight.shape[0] // 2, tracks), BF16)]
    return kernel_call(
        grad_kernel, "logit_grad", outs, scratch, place, weight, scale, expo, targets,
        flops=weight.size * count,
    )


def scatter_kernel(place, weight, grad, received, mine, one, two, three, picked):
    width = mine.shape[0]
    blocks = [2 * lax.rem(place[0] + shift, 4) + place[1] for shift in range(4)]
    pick_rows(weight, picked, blocks)
    part = jnp.dot(picked[...], grad[...], preferred_element_type=F32)
    for shift, out in enumerate((mine, one, two, three)):
        at = slice(shift * width, (shift + 1) * width)
        out[...] = (part[at] + received[at, :].astype(F32)).astype(out.dtype)


def scatter_blocks(place, weight, grad, received):
    tracks, count = grad.shape
    width = received.shape[0] // 4
    block = jax.ShapeDtypeStruct((width, count), BF16)
    outs = (jax.ShapeDtypeStruct((width, count), F32), block, block, block)
    scratch = [pltpu.VMEM((received.shape[0], tracks), BF16)]
    return kernel_call(
        scatter_kernel, "core_sum", outs, scratch, place, weight, grad, received,
        flops=weight.size * count,
    )


def outer_kernel(place, grad, mine, theirs, out, table):
    tracks = grad.shape[0]
    width = mine.shape[0] // 4
    along = (((1,), (1,)), ((), ()))
    for block, offset in ((mine, place[1]), (theirs, 1 - place[1])):
        part = lax.dot_general(block[...], grad[...], along, preferred_element_type=F32)
        for chip in range(4):
            row = (2 * chip + offset) * width
            at = pl.ds(pl.multiple_of(row, 16), width)
            table[at, :tracks] = part[chip * width : (chip + 1) * width]
    out[...] = table[...].T[:tracks]


def outer_product(place, grad, mine, theirs):
    tracks = grad.shape[0]
    features = 2 * mine.shape[0]
    return kernel_call(
        outer_kernel, "weight_part", (jax.ShapeDtypeStruct((tracks, features), F32),),
        [pltpu.VMEM((features, LANES), F32)], place, grad, mine, theirs,
        flops=2 * features * grad.size,
    )[0]


def rows_kernel(parts, out):
    wide = parts.shape[2] // LANES
    tiles = out.shape[2] // LANES
    for tile in range(parts.shape[1] // 8 * wide):
        row, lane = tile // wide * 8, tile % wide * LANES
        group, spot = tile // tiles, tile % tiles * LANES
        total = jnp.sum(parts[:, row : row + 8, lane : lane + LANES], axis=0)
        out[group * 8 : group * 8 + 8, 0, spot : spot + LANES] = total


def sum_to_rows(parts, rows):
    size = parts.shape[1] * parts.shape[2]
    return pl.pallas_call(
        rows_kernel,
        out_shape=jax.ShapeDtypeStruct((rows, 1, size // rows), F32),
        compiler_params=pltpu.CompilerParams(vmem_limit_bytes=8 * 2**20),
        cost_estimate=pl.CostEstimate(flops=4 * size, bytes_accessed=20 * size, transcendentals=0),
        name="sum_to_rows",
    )(parts)


def from_rows(rows, tracks, features):
    tiles = rows.reshape(-1, 8, rows.shape[1] // LANES, LANES).transpose(0, 2, 1, 3)
    tiles = tiles.reshape(tracks // 8, features // LANES, 8, LANES).transpose(0, 2, 1, 3)
    return tiles.reshape(tracks, features)


def backward_kernel(
    mine, one, two, three, cells, left, right, tap, grad, rows_out, line, table, sides, sems,
    square, columns,
):
    reach = left.shape[1]
    count = cells.shape[1]
    rows = 16
    copies = [
        pltpu.make_async_copy(side, sides.at[i], sems.at[i])
        for i, side in enumerate((left, right))
    ]
    for copy in copies:
        copy.start()
    lane = lax.broadcasted_iota(jnp.int32, (rows, LANES), 1)
    columns[...] = tap_columns(tap, square)
    line[:, :LANES] = jnp.zeros((rows, LANES), F32)
    line[:, LANES + count :] = jnp.zeros((rows, LANES), F32)
    for copy in copies:
        copy.wait()

    @pl.loop(0, cells.shape[0] // rows)
    def _(block):
        at = pl.ds(pl.multiple_of(block * rows, rows), rows)
        line[:, LANES - reach : LANES] = sides[0, at, :].astype(F32)
        line[:, LANES + count : LANES + count + reach] = sides[1, at, :].astype(F32)
        line[:, LANES : LANES + count] = cells[at, :].astype(F32)
        whole = line[...]
        taps = columns[at, :]
        moved = []
        conv = jnp.zeros((rows, count), F32)
        for k in range(2 * reach + 1):
            shift = (reach - k) % whole.shape[1]
            turned = pltpu.roll(whole, shift, 1) if shift else whole
            moved.append(turned[:, LANES : LANES + count])
            conv = conv + taps[:, k : k + 1] * moved[k]
        sig = jax.nn.sigmoid(conv)
        total = mine[at, :] + one[at, :].astype(F32)
        total = total + two[at, :].astype(F32) + three[at, :].astype(F32)
        value = (total * (sig * (1.0 + conv * (1.0 - sig)))).astype(BF16)
        grad[at, :] = value
        value = value.astype(F32)
        found = jnp.zeros((rows, LANES), F32)
        for k in range(2 * reach + 1):
            found = jnp.where(lane == k, jnp.sum(moved[k] * value, axis=1, keepdims=True), found)
        for k in range(reach):
            found = jnp.where(lane == 8 + k, value[:, k : k + 1], found)
            last = count - reach + k
            found = jnp.where(lane == 8 + reach + k, value[:, last : last + 1], found)
        table[at, :] = found

    rows_out[...] = table[...].T[: rows_out.shape[0]]


def backward(mine, parts, cells, left, right, tap):
    rows, count = cells.shape
    return pl.pallas_call(
        backward_kernel,
        out_shape=(
            jax.ShapeDtypeStruct((rows, count), BF16),
            jax.ShapeDtypeStruct((16, rows), F32),
        ),
        in_specs=[pl.BlockSpec(memory_space=pltpu.VMEM)] * 5
        + [pl.BlockSpec(memory_space=pl.ANY)] * 2
        + [pl.BlockSpec(memory_space=pltpu.VMEM)],
        scratch_shapes=[
            pltpu.VMEM((16, count + 2 * LANES), F32),
            pltpu.VMEM((rows, LANES), F32),
            pltpu.VMEM((2,) + left.shape, left.dtype),
            pltpu.SemaphoreType.DMA((2,)),
            pltpu.VMEM((8, LANES), F32),
            pltpu.VMEM((LANES, 8), F32),
        ],
        compiler_params=pltpu.CompilerParams(vmem_limit_bytes=8 * 2**20),
        cost_estimate=pl.CostEstimate(
            flops=40 * rows * count, bytes_accessed=14 * rows * count, transcendentals=0
        ),
        name="conv_grad",
    )(mine, *parts, cells, left, right, tap)


def spread_kernel(grad, tap, embed, ends, line, square, columns):
    count = grad.shape[1]
    rows = 16
    reach = tap.shape[0] // 2
    columns[...] = tap_columns(tap, square)
    line[:, :LANES] = jnp.zeros((rows, LANES), F32)
    line[:, LANES + count :] = jnp.zeros((rows, LANES), F32)

    @pl.loop(0, grad.shape[0] // rows)
    def _(block):
        at = pl.ds(pl.multiple_of(block * rows, rows), rows)
        line[:, LANES : LANES + count] = grad[at, :].astype(F32)
        whole = line[...]
        taps = columns[at, :]
        total = jnp.zeros((rows, count), F32)
        for k in range(2 * reach + 1):
            shift = (k - reach) % whole.shape[1]
            moved = pltpu.roll(whole, shift, 1) if shift else whole
            total = total + taps[:, k : k + 1] * moved[:, LANES : LANES + count]
        embed[at, :] = total.astype(BF16)
        ends[at, :LANES] = total[:, :LANES]
        ends[at, LANES:] = total[:, count - LANES :]


def spread(grad, tap):
    rows, count = grad.shape
    return pl.pallas_call(
        spread_kernel,
        out_shape=(
            jax.ShapeDtypeStruct((rows, count), BF16),
            jax.ShapeDtypeStruct((rows, 2 * LANES), F32),
        ),
        scratch_shapes=[
            pltpu.VMEM((16, count + 2 * LANES), F32),
            pltpu.VMEM((8, LANES), F32),
            pltpu.VMEM((LANES, 8), F32),
        ],
        compiler_params=pltpu.CompilerParams(vmem_limit_bytes=8 * 2**20),
        cost_estimate=pl.CostEstimate(
            flops=10 * rows * count, bytes_accessed=4 * rows * count, transcendentals=0
        ),
        name="embed_grad",
    )(grad, tap)


def finish_kernel(
    place, slab, ends, tap, given, embed, sums, square, columns, edges, tiles, sems
):
    del given
    ntaps, width = tap.shape
    reach = ntaps // 2
    devices = slab.shape[0]
    me = place[0]
    columns[...] = tap_columns(tap, square)

    edges[...] = jnp.zeros(edges.shape, F32)
    start = 2 * ntaps * width
    for side, other in enumerate((me - 1, me + 1)):
        row = slab[pl.ds(jnp.clip(other, 0, devices - 1), 1), :]
        row = jnp.where((other >= 0) & (other < devices), row, 0.0)
        for k in range(reach):
            turned = pltpu.roll(row, row.shape[1] - start - k * width, 1)
            edges[side * reach + k : side * reach + k + 1, :] = turned[:, :LANES]
    outer = edges[...].T[:width]

    lane = lax.broadcasted_iota(jnp.int32, (width, LANES), 1)
    first, last = ends[:, :LANES], ends[:, LANES:]
    for column in range(reach):
        for k in range(ntaps):
            source = column - k + reach
            if source < 0:
                mirror = ntaps - 1 - k
                before = outer[:, reach + source : reach + source + 1]
                after = outer[:, reach - 1 - source : reach - source]
                value = columns[:width, k : k + 1] * before
                first = first + jnp.where(lane == column, value, 0.0)
                value = columns[:width, mirror : mirror + 1] * after
                last = last + jnp.where(lane == LANES - 1 - column, value, 0.0)
    count = embed.shape[1]
    writes = []
    for n, (tile, at) in enumerate(((first, 0), (last, count - LANES))):
        tiles[n] = tile.astype(BF16)
        writes.append(
            pltpu.make_async_copy(tiles.at[n], embed.at[:, pl.ds(at, LANES)], sems.at[n])
        )
        writes[n].start()

    total = jnp.sum(slab[...], axis=0, keepdims=True)
    for k in range(ntaps):
        high = pltpu.roll(total, total.shape[1] - k * width, 1) if k else total
        low = pltpu.roll(total, total.shape[1] - (ntaps + k) * width, 1)
        sums[k : k + 1, :] = (high + low)[:, :width]
    for write in writes:
        write.wait()


def finish(place, slab, ends, tap, embed):
    ntaps, width = tap.shape
    return pl.pallas_call(
        finish_kernel,
        out_shape=(
            jax.ShapeDtypeStruct(embed.shape, embed.dtype),
            jax.ShapeDtypeStruct((ntaps, width), F32),
        ),
        in_specs=[pl.BlockSpec(memory_space=pltpu.SMEM)]
        + [pl.BlockSpec(memory_space=pltpu.VMEM)] * 3
        + [pl.BlockSpec(memory_space=pl.ANY)],
        out_specs=(
            pl.BlockSpec(memory_space=pl.ANY),
            pl.BlockSpec(memory_space=pltpu.VMEM),
        ),
        input_output_aliases={4: 0},
        scratch_shapes=[
            pltpu.VMEM((8, LANES), F32),
            pltpu.VMEM((LANES, 8), F32),
            pltpu.VMEM((8, LANES), F32),
            pltpu.VMEM((2, width, LANES), BF16),
            pltpu.SemaphoreType.DMA((2,)),
        ],
        compiler_params=pltpu.CompilerParams(vmem_limit_bytes=8 * 2**20),
        cost_estimate=pl.CostEstimate(
            flops=slab.size, bytes_accessed=8 * slab.size, transcendentals=0
        ),
        name="finish",
    )(place, slab, ends, tap, embed)


def shards(embeddings, taps, head_weight, targets):
    width = embeddings.shape[0]
    count = embeddings.shape[1]
    tracks = head_weight.shape[0]
    ntaps = taps.shape[0]
    reach = ntaps // 2
    y = lax.axis_index("y")
    c = lax.axis_index("c")
    ny = lax.axis_size("y")
    nseq = lax.axis_size(SEQ)
    me = lax.axis_index(SEQ)
    features = ny * 2 * width

    place = jnp.stack([y, c])
    left, right = outer_columns(embeddings, reach)
    block = forward(embeddings, left, right, taps)

    mine = lax.all_to_all(
        jnp.broadcast_to(block[None], (ny, width, count)), "y", 0, 0, tiled=True
    ).reshape(ny * width, count)
    theirs = other_core(mine)
    weight = head_weight.T
    near, counts = near_logits(place, weight, mine, targets)
    expo, stats = far_logits(place, weight, theirs, near, counts)
    every = share(stats[:3].reshape(-1), SEQ)
    tops = every[:, :LANES]
    peak = jnp.max(tops, axis=0)
    total = jnp.sum(every[:, LANES : 2 * LANES] * jnp.exp(tops - peak[None]), axis=0)
    counts = jnp.sum(every[:, 2 * LANES :], axis=0)
    scale = counts * jnp.exp(stats[0] - peak) / jnp.where(total > 0.0, total, 1.0)
    logit_grad, sent = logit_gradient(
        place, weight, jnp.broadcast_to(scale[None], (8, LANES)), expo, targets
    )
    received = other_core(sent)

    nx, nz = lax.axis_size("x"), lax.axis_size("z")
    late_grad, _ = lax.optimization_barrier((logit_grad, sent))
    local = outer_product(place, late_grad, mine, theirs)
    part = lax.all_to_all(local.reshape(nx, tracks // nx, features), "x", 0, 0, tiled=True)

    own, *blocks = scatter_blocks(place, weight, logit_grad, received)
    parts = [along_y(blocks[shift - 1], shift) for shift in (2, 1, 3)]
    part = lax.all_to_all(sum_to_rows(part, nz), "z", 0, 0, tiled=True)

    conv_grad, found = backward(own, parts, embeddings, left, right, taps)
    part, found = lax.optimization_barrier((part, found))
    part = jnp.sum(part, axis=0).reshape(-1)
    local_taps = found[:ntaps].reshape(-1)
    head = found[8 : 8 + reach].reshape(1, -1).astype(BF16)
    tail = found[8 + reach : 8 + 2 * reach].reshape(1, -1).astype(BF16)

    high = lax.reduce_precision(local_taps, 8, 7)
    low = local_taps - high
    row = jnp.arange(nseq)[:, None]
    zero = jnp.zeros((), BF16)
    edge = jnp.where(row == me + 1, tail, jnp.where(row == me - 1, head, zero))
    both = jnp.concatenate([high, low]).astype(BF16)
    both = jnp.broadcast_to(both[None], (nseq, both.size))
    same = jnp.broadcast_to(part.astype(BF16)[None], (nseq, part.size))
    message = jnp.stack([same, jnp.concatenate([both, edge], axis=1)], axis=1)
    slab = lax.all_to_all(message, SEQ, 0, 0, tiled=True)
    weight_grad = from_rows(slab[:, 0], tracks, features).astype(F32)
    embed_grad, ends = spread(conv_grad, taps)
    embed_grad, taps_grad = finish(
        me.reshape(1), slab[:, 1].astype(F32), ends, taps, embed_grad
    )
    return embed_grad, weight_grad, taps_grad


def solution(mesh):
    fine = Mesh(np.asarray(mesh.devices).reshape(4, 16, 4, 2), ("x", "z", "y", "c"))
    track = ("y", "c")
    return jax.shard_map(
        shards,
        mesh=fine,
        in_specs=(P(track, SEQ), P(None, track), P(track, None), P(track, SEQ)),
        out_specs=(P(track, SEQ), P(track, None), P(None, track)),
        check_vma=False,
    )
```

```python
import functools

import jax
import jax.numpy as jnp
import numpy as np
from jax import lax
from jax.experimental import pallas as pl
from jax.experimental.pallas import tpu as pltpu
from jax.sharding import Mesh
from jax.sharding import PartitionSpec as P

F32 = jnp.float32
BF16 = jnp.bfloat16
SEQ = ("x", "z")
LANES = 128


def along_y(value, shift):
    count = lax.axis_size("y")
    return lax.ppermute(value, "y", [(i, (i + shift) % count) for i in range(count)])


def other_core(value):
    return lax.ppermute(value, "c", [(0, 1), (1, 0)])


def outer_columns(cells, width):
    count = lax.axis_size(SEQ)
    left = lax.ppermute(cells[:, -width:], SEQ, [(i, i + 1) for i in range(count - 1)])
    right = lax.ppermute(cells[:, :width], SEQ, [(i + 1, i) for i in range(count - 1)])
    return left, right


def share(value, axes):
    count = lax.axis_size(axes)
    copies = jnp.broadcast_to(value.reshape(1, 1, -1), (count, 1, value.size))
    return lax.all_to_all(copies, axes, 0, 0, tiled=True)[:, 0]


def tap_columns(tap, square):
    count, features = tap.shape
    square[:, :] = jnp.zeros(square.shape, F32)
    square[:count, :features] = tap[...].astype(F32)
    return square[...].T


def forward_kernel(cells, tap, hidden, line, square, columns):
    rows = 16
    count = cells.shape[1]
    reach = tap.shape[0] // 2
    columns[...] = tap_columns(tap, square)
    line[:, :LANES] = jnp.zeros((rows, LANES), F32)
    line[:, LANES + count :] = jnp.zeros((rows, LANES), F32)

    @pl.loop(0, cells.shape[0] // rows)
    def _(block):
        at = pl.ds(pl.multiple_of(block * rows, rows), rows)
        line[:, LANES : LANES + count] = cells[at, :].astype(F32)
        whole = line[...]
        taps = columns[at, :]
        conv = jnp.zeros((rows, count), F32)
        for k in range(2 * reach + 1):
            shift = (reach - k) % whole.shape[1]
            moved = pltpu.roll(whole, shift, 1) if shift else whole
            conv = conv + taps[:, k : k + 1] * moved[:, LANES : LANES + count]
        hidden[at, :] = (conv * jax.nn.sigmoid(conv)).astype(BF16)


def forward(cells, tap):
    rows, count = cells.shape
    return pl.pallas_call(
        forward_kernel,
        out_shape=jax.ShapeDtypeStruct((rows, count), BF16),
        scratch_shapes=[
            pltpu.VMEM((16, count + 2 * LANES), F32),
            pltpu.VMEM((8, LANES), F32),
            pltpu.VMEM((LANES, 8), F32),
        ],
        compiler_params=pltpu.CompilerParams(vmem_limit_bytes=4 * 2**20),
        cost_estimate=pl.CostEstimate(
            flops=20 * rows * count, bytes_accessed=4 * rows * count, transcendentals=rows * count
        ),
        name="conv_silu",
    )(cells, tap)


def rim_kernel(cells, left, right, tap, given, hidden, line, square, columns, tiles, sems):
    del given
    width, count = cells.shape
    reach = left.shape[1]
    columns[...] = tap_columns(tap, square)
    taps = columns[:width, :]
    line[...] = jnp.zeros(line.shape, F32)
    writes = []
    for side, at in enumerate((0, count - LANES)):
        line[:, LANES : 2 * LANES] = cells[:, at : at + LANES].astype(F32)
        if side == 0:
            line[:, LANES - reach : LANES] = left[...].astype(F32)
            line[:, 2 * LANES :] = cells[:, at + LANES : at + 2 * LANES].astype(F32)
        else:
            line[:, :LANES] = cells[:, at - LANES : at].astype(F32)
            line[:, 2 * LANES : 2 * LANES + reach] = right[...].astype(F32)
        whole = line[...]
        conv = jnp.zeros((width, LANES), F32)
        for k in range(2 * reach + 1):
            shift = (reach - k) % whole.shape[1]
            moved = pltpu.roll(whole, shift, 1) if shift else whole
            conv = conv + taps[:, k : k + 1] * moved[:, LANES : 2 * LANES]
        tiles[side] = (conv * jax.nn.sigmoid(conv)).astype(BF16)
        spot = hidden.at[:, pl.ds(at, LANES)]
        writes.append(pltpu.make_async_copy(tiles.at[side], spot, sems.at[side]))
        writes[side].start()
    for write in writes:
        write.wait()


def with_rim(cells, left, right, tap, hidden):
    width, _ = cells.shape
    return pl.pallas_call(
        rim_kernel,
        out_shape=jax.ShapeDtypeStruct(hidden.shape, hidden.dtype),
        in_specs=[pl.BlockSpec(memory_space=pltpu.VMEM)] * 4
        + [pl.BlockSpec(memory_space=pl.ANY)],
        out_specs=pl.BlockSpec(memory_space=pl.ANY),
        input_output_aliases={4: 0},
        scratch_shapes=[
            pltpu.VMEM((width, 3 * LANES), F32),
            pltpu.VMEM((8, LANES), F32),
            pltpu.VMEM((LANES, 8), F32),
            pltpu.VMEM((2, width, LANES), BF16),
            pltpu.SemaphoreType.DMA((2,)),
        ],
        compiler_params=pltpu.CompilerParams(vmem_limit_bytes=4 * 2**20),
        cost_estimate=pl.CostEstimate(
            flops=40 * width * LANES, bytes_accessed=8 * width * LANES, transcendentals=0
        ),
        name="outer_columns",
    )(cells, left, right, tap, hidden)


def pick_rows(weight, picked, blocks):
    width = picked.shape[0] // 4
    for chip, block in enumerate(blocks):
        at = pl.ds(pl.multiple_of(block * width, 16), width)
        picked[chip * width : (chip + 1) * width, :] = weight[at, :]


TURN = (((0,), (0,)), ((), ()))


def near_kernel(place, weight, hidden, targets, logits, counts, picked):
    pick_rows(weight, picked, [2 * chip + place[1] for chip in range(4)])
    logits[...] = lax.dot_general(picked[...], hidden[...], TURN, preferred_element_type=F32)
    counts[...] = jnp.broadcast_to(jnp.sum(targets[...], axis=1, keepdims=True), counts.shape)


def far_kernel(place, weight, hidden, near, counts, expo, stats, picked, table):
    tracks = near.shape[0]
    pick_rows(weight, picked, [2 * chip + 1 - place[1] for chip in range(4)])
    logits = lax.dot_general(picked[...], hidden[...], TURN, preferred_element_type=F32)
    logits = logits + near[...]
    top = jnp.max(logits, axis=1, keepdims=True)
    value = jnp.exp(logits - top)
    expo[...] = value
    total = jnp.sum(value, axis=1, keepdims=True)
    lane = lax.broadcasted_iota(jnp.int32, (tracks, LANES), 1)
    table[...] = jnp.zeros(table.shape, F32)
    table[:tracks, :] = jnp.where(lane == 0, top, jnp.where(lane == 1, total, counts[...]))
    stats[...] = table[...].T[: stats.shape[0]]


def kernel_call(body, name, outs, scratch, place, *operands, flops=0):
    size = sum(o.size * o.dtype.itemsize for o in operands)
    size += sum(o.size * o.dtype.itemsize for o in outs)
    return pl.pallas_call(
        body,
        out_shape=outs,
        in_specs=[pl.BlockSpec(memory_space=pltpu.SMEM)]
        + [pl.BlockSpec(memory_space=pltpu.VMEM)] * len(operands),
        scratch_shapes=scratch,
        compiler_params=pltpu.CompilerParams(vmem_limit_bytes=size + 4 * 2**20),
        cost_estimate=pl.CostEstimate(flops=flops, bytes_accessed=size, transcendentals=0),
        name=name,
    )(place, *operands)


def near_logits(place, weight, hidden, targets):
    tracks, count = targets.shape
    outs = (
        jax.ShapeDtypeStruct((tracks, count), F32),
        jax.ShapeDtypeStruct((tracks, LANES), F32),
    )
    scratch = [pltpu.VMEM((hidden.shape[0], tracks), BF16)]
    return kernel_call(
        near_kernel, "near_logits", outs, scratch, place, weight, hidden, targets,
        flops=2 * hidden.size * tracks,
    )


def far_logits(place, weight, hidden, near, counts):
    tracks = near.shape[0]
    outs = (
        jax.ShapeDtypeStruct(near.shape, F32),
        jax.ShapeDtypeStruct((8, LANES), F32),
    )
    scratch = [
        pltpu.VMEM((hidden.shape[0], tracks), BF16),
        pltpu.VMEM((LANES, LANES), F32),
    ]
    return kernel_call(
        far_kernel, "far_logits", outs, scratch, place, weight, hidden, near, counts,
        flops=2 * hidden.size * tracks,
    )


def grad_kernel(place, weight, scale, expo, targets, grad, sent, picked):
    tracks = expo.shape[0]
    column = scale[...].T[:tracks, 0:1]
    value = (column * expo[...] - targets[...]).astype(BF16)
    grad[...] = value
    blocks = [2 * lax.rem(place[0] + shift, 4) + 1 - place[1] for shift in range(4)]
    pick_rows(weight, picked, blocks)
    sent[...] = jnp.dot(picked[...], value, preferred_element_type=F32).astype(BF16)


def logit_gradient(place, weight, scale, expo, targets):
    tracks, count = expo.shape
    outs = (
        jax.ShapeDtypeStruct((tracks, count), BF16),
        jax.ShapeDtypeStruct((weight.shape[0] // 2, count), BF16),
    )
    scratch = [pltpu.VMEM((weight.shape[0] // 2, tracks), BF16)]
    return kernel_call(
        grad_kernel, "logit_grad", outs, scratch, place, weight, scale, expo, targets,
        flops=weight.size * count,
    )


def scatter_kernel(place, weight, grad, received, mine, one, two, three, picked):
    width = mine.shape[0]
    blocks = [2 * lax.rem(place[0] + shift, 4) + place[1] for shift in range(4)]
    pick_rows(weight, picked, blocks)
    part = jnp.dot(picked[...], grad[...], preferred_element_type=F32)
    for shift, out in enumerate((mine, one, two, three)):
        at = slice(shift * width, (shift + 1) * width)
        out[...] = (part[at] + received[at, :].astype(F32)).astype(out.dtype)


def scatter_blocks(place, weight, grad, received):
    tracks, count = grad.shape
    width = received.shape[0] // 4
    block = jax.ShapeDtypeStruct((width, count), BF16)
    outs = (jax.ShapeDtypeStruct((width, count), F32), block, block, block)
    scratch = [pltpu.VMEM((received.shape[0], tracks), BF16)]
    return kernel_call(
        scatter_kernel, "core_sum", outs, scratch, place, weight, grad, received,
        flops=weight.size * count,
    )


def outer_kernel(place, grad, mine, theirs, out, table):
    tracks = grad.shape[0]
    width = mine.shape[0] // 4
    along = (((1,), (1,)), ((), ()))
    for block, offset in ((mine, place[1]), (theirs, 1 - place[1])):
        part = lax.dot_general(block[...], grad[...], along, preferred_element_type=F32)
        for chip in range(4):
            row = (2 * chip + offset) * width
            at = pl.ds(pl.multiple_of(row, 16), width)
            table[at, :tracks] = part[chip * width : (chip + 1) * width]
    out[...] = table[...].T[:tracks]


def outer_product(place, grad, mine, theirs):
    tracks = grad.shape[0]
    features = 2 * mine.shape[0]
    return kernel_call(
        outer_kernel, "weight_part", (jax.ShapeDtypeStruct((tracks, features), F32),),
        [pltpu.VMEM((features, LANES), F32)], place, grad, mine, theirs,
        flops=2 * features * grad.size,
    )[0]


def rows_kernel(parts, out):
    wide = parts.shape[2] // LANES
    tiles = out.shape[2] // LANES
    for tile in range(parts.shape[1] // 8 * wide):
        row, lane = tile // wide * 8, tile % wide * LANES
        group, spot = tile // tiles, tile % tiles * LANES
        total = jnp.sum(parts[:, row : row + 8, lane : lane + LANES], axis=0)
        out[group * 8 : group * 8 + 8, 0, spot : spot + LANES] = total


def sum_to_rows(parts, rows):
    size = parts.shape[1] * parts.shape[2]
    return pl.pallas_call(
        rows_kernel,
        out_shape=jax.ShapeDtypeStruct((rows, 1, size // rows), F32),
        compiler_params=pltpu.CompilerParams(vmem_limit_bytes=8 * 2**20),
        cost_estimate=pl.CostEstimate(flops=4 * size, bytes_accessed=20 * size, transcendentals=0),
        name="sum_to_rows",
    )(parts)


def from_rows(rows, tracks, features):
    tiles = rows.reshape(-1, 8, rows.shape[1] // LANES, LANES).transpose(0, 2, 1, 3)
    tiles = tiles.reshape(tracks // 8, features // LANES, 8, LANES).transpose(0, 2, 1, 3)
    return tiles.reshape(tracks, features)


def backward_kernel(
    mine, one, two, three, cells, left, right, tap, grad, rows_out, line, table, sides, sems,
    square, columns,
):
    reach = left.shape[1]
    count = cells.shape[1]
    rows = 16
    copies = [
        pltpu.make_async_copy(side, sides.at[i], sems.at[i])
        for i, side in enumerate((left, right))
    ]
    for copy in copies:
        copy.start()
    lane = lax.broadcasted_iota(jnp.int32, (rows, LANES), 1)
    columns[...] = tap_columns(tap, square)
    line[:, :LANES] = jnp.zeros((rows, LANES), F32)
    line[:, LANES + count :] = jnp.zeros((rows, LANES), F32)
    for copy in copies:
        copy.wait()

    @pl.loop(0, cells.shape[0] // rows)
    def _(block):
        at = pl.ds(pl.multiple_of(block * rows, rows), rows)
        line[:, LANES - reach : LANES] = sides[0, at, :].astype(F32)
        line[:, LANES + count : LANES + count + reach] = sides[1, at, :].astype(F32)
        line[:, LANES : LANES + count] = cells[at, :].astype(F32)
        whole = line[...]
        taps = columns[at, :]
        moved = []
        conv = jnp.zeros((rows, count), F32)
        for k in range(2 * reach + 1):
            shift = (reach - k) % whole.shape[1]
            turned = pltpu.roll(whole, shift, 1) if shift else whole
            moved.append(turned[:, LANES : LANES + count])
            conv = conv + taps[:, k : k + 1] * moved[k]
        sig = jax.nn.sigmoid(conv)
        total = mine[at, :] + one[at, :].astype(F32)
        total = total + two[at, :].astype(F32) + three[at, :].astype(F32)
        value = (total * (sig * (1.0 + conv * (1.0 - sig)))).astype(BF16)
        grad[at, :] = value
        value = value.astype(F32)
        found = jnp.zeros((rows, LANES), F32)
        for k in range(2 * reach + 1):
            found = jnp.where(lane == k, jnp.sum(moved[k] * value, axis=1, keepdims=True), found)
        for k in range(reach):
            found = jnp.where(lane == 8 + k, value[:, k : k + 1], found)
            last = count - reach + k
            found = jnp.where(lane == 8 + reach + k, value[:, last : last + 1], found)
        table[at, :] = found

    rows_out[...] = table[...].T[: rows_out.shape[0]]


def backward(mine, parts, cells, left, right, tap):
    rows, count = cells.shape
    return pl.pallas_call(
        backward_kernel,
        out_shape=(
            jax.ShapeDtypeStruct((rows, count), BF16),
            jax.ShapeDtypeStruct((16, rows), F32),
        ),
        in_specs=[pl.BlockSpec(memory_space=pltpu.VMEM)] * 5
        + [pl.BlockSpec(memory_space=pl.ANY)] * 2
        + [pl.BlockSpec(memory_space=pltpu.VMEM)],
        scratch_shapes=[
            pltpu.VMEM((16, count + 2 * LANES), F32),
            pltpu.VMEM((rows, LANES), F32),
            pltpu.VMEM((2,) + left.shape, left.dtype),
            pltpu.SemaphoreType.DMA((2,)),
            pltpu.VMEM((8, LANES), F32),
            pltpu.VMEM((LANES, 8), F32),
        ],
        compiler_params=pltpu.CompilerParams(vmem_limit_bytes=8 * 2**20),
        cost_estimate=pl.CostEstimate(
            flops=40 * rows * count, bytes_accessed=14 * rows * count, transcendentals=0
        ),
        name="conv_grad",
    )(mine, *parts, cells, left, right, tap)


def spread_kernel(grad, tap, embed, ends, line, square, columns):
    count = grad.shape[1]
    rows = 16
    reach = tap.shape[0] // 2
    columns[...] = tap_columns(tap, square)
    line[:, :LANES] = jnp.zeros((rows, LANES), F32)
    line[:, LANES + count :] = jnp.zeros((rows, LANES), F32)

    @pl.loop(0, grad.shape[0] // rows)
    def _(block):
        at = pl.ds(pl.multiple_of(block * rows, rows), rows)
        line[:, LANES : LANES + count] = grad[at, :].astype(F32)
        whole = line[...]
        taps = columns[at, :]
        total = jnp.zeros((rows, count), F32)
        for k in range(2 * reach + 1):
            shift = (k - reach) % whole.shape[1]
            moved = pltpu.roll(whole, shift, 1) if shift else whole
            total = total + taps[:, k : k + 1] * moved[:, LANES : LANES + count]
        embed[at, :] = total.astype(BF16)
        ends[at, :LANES] = total[:, :LANES]
        ends[at, LANES:] = total[:, count - LANES :]


def spread(grad, tap):
    rows, count = grad.shape
    return pl.pallas_call(
        spread_kernel,
        out_shape=(
            jax.ShapeDtypeStruct((rows, count), BF16),
            jax.ShapeDtypeStruct((rows, 2 * LANES), F32),
        ),
        scratch_shapes=[
            pltpu.VMEM((16, count + 2 * LANES), F32),
            pltpu.VMEM((8, LANES), F32),
            pltpu.VMEM((LANES, 8), F32),
        ],
        compiler_params=pltpu.CompilerParams(vmem_limit_bytes=8 * 2**20),
        cost_estimate=pl.CostEstimate(
            flops=10 * rows * count, bytes_accessed=4 * rows * count, transcendentals=0
        ),
        name="embed_grad",
    )(grad, tap)


def finish_kernel(
    place, slab, ends, tap, given, embed, sums, square, columns, edges, tiles, sems
):
    del given
    ntaps, width = tap.shape
    reach = ntaps // 2
    devices = slab.shape[0]
    me = place[0]
    columns[...] = tap_columns(tap, square)

    edges[...] = jnp.zeros(edges.shape, F32)
    start = 2 * ntaps * width
    for side, other in enumerate((me - 1, me + 1)):
        row = slab[pl.ds(jnp.clip(other, 0, devices - 1), 1), :]
        row = jnp.where((other >= 0) & (other < devices), row, 0.0)
        for k in range(reach):
            turned = pltpu.roll(row, row.shape[1] - start - k * width, 1)
            edges[side * reach + k : side * reach + k + 1, :] = turned[:, :LANES]
    outer = edges[...].T[:width]

    lane = lax.broadcasted_iota(jnp.int32, (width, LANES), 1)
    first, last = ends[:, :LANES], ends[:, LANES:]
    for column in range(reach):
        for k in range(ntaps):
            source = column - k + reach
            if source < 0:
                mirror = ntaps - 1 - k
                before = outer[:, reach + source : reach + source + 1]
                after = outer[:, reach - 1 - source : reach - source]
                value = columns[:width, k : k + 1] * before
                first = first + jnp.where(lane == column, value, 0.0)
                value = columns[:width, mirror : mirror + 1] * after
                last = last + jnp.where(lane == LANES - 1 - column, value, 0.0)
    count = embed.shape[1]
    writes = []
    for n, (tile, at) in enumerate(((first, 0), (last, count - LANES))):
        tiles[n] = tile.astype(BF16)
        writes.append(
            pltpu.make_async_copy(tiles.at[n], embed.at[:, pl.ds(at, LANES)], sems.at[n])
        )
        writes[n].start()

    total = jnp.sum(slab[...], axis=0, keepdims=True)
    for k in range(ntaps):
        high = pltpu.roll(total, total.shape[1] - k * width, 1) if k else total
        low = pltpu.roll(total, total.shape[1] - (ntaps + k) * width, 1)
        sums[k : k + 1, :] = (high + low)[:, :width]
    for write in writes:
        write.wait()


def finish(place, slab, ends, tap, embed):
    ntaps, width = tap.shape
    return pl.pallas_call(
        finish_kernel,
        out_shape=(
            jax.ShapeDtypeStruct(embed.shape, embed.dtype),
            jax.ShapeDtypeStruct((ntaps, width), F32),
        ),
        in_specs=[pl.BlockSpec(memory_space=pltpu.SMEM)]
        + [pl.BlockSpec(memory_space=pltpu.VMEM)] * 3
        + [pl.BlockSpec(memory_space=pl.ANY)],
        out_specs=(
            pl.BlockSpec(memory_space=pl.ANY),
            pl.BlockSpec(memory_space=pltpu.VMEM),
        ),
        input_output_aliases={4: 0},
        scratch_shapes=[
            pltpu.VMEM((8, LANES), F32),
            pltpu.VMEM((LANES, 8), F32),
            pltpu.VMEM((8, LANES), F32),
            pltpu.VMEM((2, width, LANES), BF16),
            pltpu.SemaphoreType.DMA((2,)),
        ],
        compiler_params=pltpu.CompilerParams(vmem_limit_bytes=8 * 2**20),
        cost_estimate=pl.CostEstimate(
            flops=slab.size, bytes_accessed=8 * slab.size, transcendentals=0
        ),
        name="finish",
    )(place, slab, ends, tap, embed)


def shards(embeddings, taps, head_weight, targets):
    width = embeddings.shape[0]
    count = embeddings.shape[1]
    tracks = head_weight.shape[0]
    ntaps = taps.shape[0]
    reach = ntaps // 2
    y = lax.axis_index("y")
    c = lax.axis_index("c")
    ny = lax.axis_size("y")
    nseq = lax.axis_size(SEQ)
    me = lax.axis_index(SEQ)
    features = ny * 2 * width

    place = jnp.stack([y, c])
    left, right = outer_columns(embeddings, reach)
    block = with_rim(embeddings, left, right, taps, forward(embeddings, taps))

    mine = lax.all_to_all(
        jnp.broadcast_to(block[None], (ny, width, count)), "y", 0, 0, tiled=True
    ).reshape(ny * width, count)
    theirs = other_core(mine)
    weight = head_weight.T
    near, counts = near_logits(place, weight, mine, targets)
    expo, stats = far_logits(place, weight, theirs, near, counts)
    every = share(stats[:3].reshape(-1), SEQ)
    tops = every[:, :LANES]
    peak = jnp.max(tops, axis=0)
    total = jnp.sum(every[:, LANES : 2 * LANES] * jnp.exp(tops - peak[None]), axis=0)
    counts = jnp.sum(every[:, 2 * LANES :], axis=0)
    scale = counts * jnp.exp(stats[0] - peak) / jnp.where(total > 0.0, total, 1.0)
    logit_grad, sent = logit_gradient(
        place, weight, jnp.broadcast_to(scale[None], (8, LANES)), expo, targets
    )
    received = other_core(sent)

    nx, nz = lax.axis_size("x"), lax.axis_size("z")
    late_grad, _ = lax.optimization_barrier((logit_grad, sent))
    local = outer_product(place, late_grad, mine, theirs)
    own, *blocks = scatter_blocks(place, weight, logit_grad, received)
    parts = [along_y(blocks[shift - 1], shift) for shift in (2, 1, 3)]

    local, own = lax.optimization_barrier((local, own))
    part = lax.all_to_all(local.reshape(nx, tracks // nx, features), "x", 0, 0, tiled=True)
    part, own = lax.optimization_barrier((sum_to_rows(part, nz), own))
    part = lax.all_to_all(part, "z", 0, 0, tiled=True)
    conv_grad, found = backward(own, parts, embeddings, left, right, taps)
    part, found = lax.optimization_barrier((part, found))
    part = jnp.sum(part, axis=0).reshape(-1)
    local_taps = found[:ntaps].reshape(-1)
    head = found[8 : 8 + reach].reshape(1, -1).astype(BF16)
    tail = found[8 + reach : 8 + 2 * reach].reshape(1, -1).astype(BF16)

    high = lax.reduce_precision(local_taps, 8, 7)
    low = local_taps - high
    row = jnp.arange(nseq)[:, None]
    zero = jnp.zeros((), BF16)
    edge = jnp.where(row == me + 1, tail, jnp.where(row == me - 1, head, zero))
    both = jnp.concatenate([high, low]).astype(BF16)
    both = jnp.broadcast_to(both[None], (nseq, both.size))
    same = jnp.broadcast_to(part.astype(BF16)[None], (nseq, part.size))
    message = jnp.stack([same, jnp.concatenate([both, edge], axis=1)], axis=1)
    slab = lax.all_to_all(message, SEQ, 0, 0, tiled=True)
    weight_grad = from_rows(slab[:, 0], tracks, features).astype(F32)
    embed_grad, ends = spread(conv_grad, taps)
    embed_grad, taps_grad = finish(
        me.reshape(1), slab[:, 1].astype(F32), ends, taps, embed_grad
    )
    return embed_grad, weight_grad, taps_grad


def solution(mesh):
    fine = Mesh(np.asarray(mesh.devices).reshape(4, 16, 4, 2), ("x", "z", "y", "c"))
    track = ("y", "c")
    return jax.shard_map(
        shards,
        mesh=fine,
        in_specs=(P(track, SEQ), P(None, track), P(track, None), P(track, SEQ)),
        out_specs=(P(track, SEQ), P(track, None), P(None, track)),
        check_vma=False,
    )
```

```python
import functools

import jax
import jax.numpy as jnp
import numpy as np
from jax import lax
from jax.experimental import pallas as pl
from jax.experimental.pallas import tpu as pltpu
from jax.sharding import Mesh
from jax.sharding import PartitionSpec as P

F32 = jnp.float32
BF16 = jnp.bfloat16
SEQ = ("x", "z")
LANES = 128


def along_y(value, shift):
    count = lax.axis_size("y")
    return lax.ppermute(value, "y", [(i, (i + shift) % count) for i in range(count)])


def other_core(value):
    return lax.ppermute(value, "c", [(0, 1), (1, 0)])


def outer_columns(cells, width):
    count = lax.axis_size(SEQ)
    left = lax.ppermute(cells[:, -width:], SEQ, [(i, i + 1) for i in range(count - 1)])
    right = lax.ppermute(cells[:, :width], SEQ, [(i + 1, i) for i in range(count - 1)])
    return left, right


def share(value, axes):
    count = lax.axis_size(axes)
    copies = jnp.broadcast_to(value.reshape(1, 1, -1), (count, 1, value.size))
    return lax.all_to_all(copies, axes, 0, 0, tiled=True)[:, 0]


def tap_columns(tap, square):
    count, features = tap.shape
    square[:, :] = jnp.zeros(square.shape, F32)
    square[:count, :features] = tap[...].astype(F32)
    return square[...].T


def forward_kernel(cells, tap, hidden, line, square, columns):
    rows = 16
    count = cells.shape[1]
    reach = tap.shape[0] // 2
    columns[...] = tap_columns(tap, square)
    line[:, :LANES] = jnp.zeros((rows, LANES), F32)
    line[:, LANES + count :] = jnp.zeros((rows, LANES), F32)

    @pl.loop(0, cells.shape[0] // rows)
    def _(block):
        at = pl.ds(pl.multiple_of(block * rows, rows), rows)
        line[:, LANES : LANES + count] = cells[at, :].astype(F32)
        whole = line[...]
        taps = columns[at, :]
        conv = jnp.zeros((rows, count), F32)
        for k in range(2 * reach + 1):
            shift = (reach - k) % whole.shape[1]
            moved = pltpu.roll(whole, shift, 1) if shift else whole
            conv = conv + taps[:, k : k + 1] * moved[:, LANES : LANES + count]
        hidden[at, :] = (conv * jax.nn.sigmoid(conv)).astype(BF16)


def forward(cells, tap):
    rows, count = cells.shape
    return pl.pallas_call(
        forward_kernel,
        out_shape=jax.ShapeDtypeStruct((rows, count), BF16),
        scratch_shapes=[
            pltpu.VMEM((16, count + 2 * LANES), F32),
            pltpu.VMEM((8, LANES), F32),
            pltpu.VMEM((LANES, 8), F32),
        ],
        compiler_params=pltpu.CompilerParams(vmem_limit_bytes=4 * 2**20),
        cost_estimate=pl.CostEstimate(
            flops=20 * rows * count, bytes_accessed=4 * rows * count, transcendentals=rows * count
        ),
        name="conv_silu",
    )(cells, tap)


def rim_kernel(cells, left, right, tap, given, hidden, line, square, columns, tiles, sems):
    del given
    width, count = cells.shape
    reach = left.shape[1]
    columns[...] = tap_columns(tap, square)
    taps = columns[:width, :]
    line[...] = jnp.zeros(line.shape, F32)
    writes = []
    for side, at in enumerate((0, count - LANES)):
        line[:, LANES : 2 * LANES] = cells[:, at : at + LANES].astype(F32)
        if side == 0:
            line[:, LANES - reach : LANES] = left[...].astype(F32)
            line[:, 2 * LANES :] = cells[:, at + LANES : at + 2 * LANES].astype(F32)
        else:
            line[:, :LANES] = cells[:, at - LANES : at].astype(F32)
            line[:, 2 * LANES : 2 * LANES + reach] = right[...].astype(F32)
        whole = line[...]
        conv = jnp.zeros((width, LANES), F32)
        for k in range(2 * reach + 1):
            shift = (reach - k) % whole.shape[1]
            moved = pltpu.roll(whole, shift, 1) if shift else whole
            conv = conv + taps[:, k : k + 1] * moved[:, LANES : 2 * LANES]
        tiles[side] = (conv * jax.nn.sigmoid(conv)).astype(BF16)
        spot = hidden.at[:, pl.ds(at, LANES)]
        writes.append(pltpu.make_async_copy(tiles.at[side], spot, sems.at[side]))
        writes[side].start()
    for write in writes:
        write.wait()


def with_rim(cells, left, right, tap, hidden):
    width, _ = cells.shape
    return pl.pallas_call(
        rim_kernel,
        out_shape=jax.ShapeDtypeStruct(hidden.shape, hidden.dtype),
        in_specs=[pl.BlockSpec(memory_space=pltpu.VMEM)] * 4
        + [pl.BlockSpec(memory_space=pl.ANY)],
        out_specs=pl.BlockSpec(memory_space=pl.ANY),
        input_output_aliases={4: 0},
        scratch_shapes=[
            pltpu.VMEM((width, 3 * LANES), F32),
            pltpu.VMEM((8, LANES), F32),
            pltpu.VMEM((LANES, 8), F32),
            pltpu.VMEM((2, width, LANES), BF16),
            pltpu.SemaphoreType.DMA((2,)),
        ],
        compiler_params=pltpu.CompilerParams(vmem_limit_bytes=4 * 2**20),
        cost_estimate=pl.CostEstimate(
            flops=40 * width * LANES, bytes_accessed=8 * width * LANES, transcendentals=0
        ),
        name="outer_columns",
    )(cells, left, right, tap, hidden)


def pick_rows(weight, picked, blocks):
    width = picked.shape[0] // 4
    for chip, block in enumerate(blocks):
        at = pl.ds(pl.multiple_of(block * width, 16), width)
        picked[chip * width : (chip + 1) * width, :] = weight[at, :]


TURN = (((0,), (0,)), ((), ()))


def near_kernel(place, weight, hidden, targets, logits, counts, picked):
    pick_rows(weight, picked, [2 * chip + place[1] for chip in range(4)])
    logits[...] = lax.dot_general(picked[...], hidden[...], TURN, preferred_element_type=F32)
    counts[...] = jnp.broadcast_to(jnp.sum(targets[...], axis=1, keepdims=True), counts.shape)


def far_kernel(place, weight, hidden, near, counts, expo, stats, picked, table):
    tracks = near.shape[0]
    pick_rows(weight, picked, [2 * chip + 1 - place[1] for chip in range(4)])
    logits = lax.dot_general(picked[...], hidden[...], TURN, preferred_element_type=F32)
    logits = logits + near[...]
    top = jnp.max(logits, axis=1, keepdims=True)
    value = jnp.exp(logits - top)
    expo[...] = value
    total = jnp.sum(value, axis=1, keepdims=True)
    lane = lax.broadcasted_iota(jnp.int32, (tracks, LANES), 1)
    table[...] = jnp.zeros(table.shape, F32)
    table[:tracks, :] = jnp.where(lane == 0, top, jnp.where(lane == 1, total, counts[...]))
    stats[...] = table[...].T[: stats.shape[0]]


def kernel_call(body, name, outs, scratch, place, *operands, flops=0):
    size = sum(o.size * o.dtype.itemsize for o in operands)
    size += sum(o.size * o.dtype.itemsize for o in outs)
    return pl.pallas_call(
        body,
        out_shape=outs,
        in_specs=[pl.BlockSpec(memory_space=pltpu.SMEM)]
        + [pl.BlockSpec(memory_space=pltpu.VMEM)] * len(operands),
        scratch_shapes=scratch,
        compiler_params=pltpu.CompilerParams(vmem_limit_bytes=size + 4 * 2**20),
        cost_estimate=pl.CostEstimate(flops=flops, bytes_accessed=size, transcendentals=0),
        name=name,
    )(place, *operands)


def near_logits(place, weight, hidden, targets):
    tracks, count = targets.shape
    outs = (
        jax.ShapeDtypeStruct((tracks, count), F32),
        jax.ShapeDtypeStruct((tracks, LANES), F32),
    )
    scratch = [pltpu.VMEM((hidden.shape[0], tracks), BF16)]
    return kernel_call(
        near_kernel, "near_logits", outs, scratch, place, weight, hidden, targets,
        flops=2 * hidden.size * tracks,
    )


def far_logits(place, weight, hidden, near, counts):
    tracks = near.shape[0]
    outs = (
        jax.ShapeDtypeStruct(near.shape, F32),
        jax.ShapeDtypeStruct((8, LANES), F32),
    )
    scratch = [
        pltpu.VMEM((hidden.shape[0], tracks), BF16),
        pltpu.VMEM((LANES, LANES), F32),
    ]
    return kernel_call(
        far_kernel, "far_logits", outs, scratch, place, weight, hidden, near, counts,
        flops=2 * hidden.size * tracks,
    )


def grad_kernel(place, weight, scale, expo, targets, grad, sent, picked):
    tracks = expo.shape[0]
    column = scale[...].T[:tracks, 0:1]
    value = (column * expo[...] - targets[...]).astype(BF16)
    grad[...] = value
    blocks = [2 * lax.rem(place[0] + shift, 4) + 1 - place[1] for shift in range(4)]
    pick_rows(weight, picked, blocks)
    sent[...] = jnp.dot(picked[...], value, preferred_element_type=F32).astype(BF16)


def logit_gradient(place, weight, scale, expo, targets):
    tracks, count = expo.shape
    outs = (
        jax.ShapeDtypeStruct((tracks, count), BF16),
        jax.ShapeDtypeStruct((weight.shape[0] // 2, count), BF16),
    )
    scratch = [pltpu.VMEM((weight.shape[0] // 2, tracks), BF16)]
    return kernel_call(
        grad_kernel, "logit_grad", outs, scratch, place, weight, scale, expo, targets,
        flops=weight.size * count,
    )


def scatter_kernel(place, weight, grad, received, mine, one, two, three, picked):
    width = mine.shape[0]
    blocks = [2 * lax.rem(place[0] + shift, 4) + place[1] for shift in range(4)]
    pick_rows(weight, picked, blocks)
    part = jnp.dot(picked[...], grad[...], preferred_element_type=F32)
    for shift, out in enumerate((mine, one, two, three)):
        at = slice(shift * width, (shift + 1) * width)
        out[...] = (part[at] + received[at, :].astype(F32)).astype(out.dtype)


def scatter_blocks(place, weight, grad, received):
    tracks, count = grad.shape
    width = received.shape[0] // 4
    block = jax.ShapeDtypeStruct((width, count), BF16)
    outs = (jax.ShapeDtypeStruct((width, count), F32), block, block, block)
    scratch = [pltpu.VMEM((received.shape[0], tracks), BF16)]
    return kernel_call(
        scatter_kernel, "core_sum", outs, scratch, place, weight, grad, received,
        flops=weight.size * count,
    )


def outer_kernel(place, grad, mine, theirs, out, table):
    tracks = grad.shape[0]
    width = mine.shape[0] // 4
    along = (((1,), (1,)), ((), ()))
    for block, offset in ((mine, place[1]), (theirs, 1 - place[1])):
        part = lax.dot_general(block[...], grad[...], along, preferred_element_type=F32)
        for chip in range(4):
            row = (2 * chip + offset) * width
            at = pl.ds(pl.multiple_of(row, 16), width)
            table[at, :tracks] = part[chip * width : (chip + 1) * width]
    out[...] = table[...].T[:tracks]


def outer_product(place, grad, mine, theirs):
    tracks = grad.shape[0]
    features = 2 * mine.shape[0]
    return kernel_call(
        outer_kernel, "weight_part", (jax.ShapeDtypeStruct((tracks, features), F32),),
        [pltpu.VMEM((features, LANES), F32)], place, grad, mine, theirs,
        flops=2 * features * grad.size,
    )[0]


def rows_kernel(parts, out):
    wide = parts.shape[2] // LANES
    tiles = out.shape[2] // LANES
    for tile in range(parts.shape[1] // 8 * wide):
        row, lane = tile // wide * 8, tile % wide * LANES
        group, spot = tile // tiles, tile % tiles * LANES
        total = jnp.sum(parts[:, row : row + 8, lane : lane + LANES], axis=0)
        out[group * 8 : group * 8 + 8, 0, spot : spot + LANES] = total


def sum_to_rows(parts, rows):
    size = parts.shape[1] * parts.shape[2]
    return pl.pallas_call(
        rows_kernel,
        out_shape=jax.ShapeDtypeStruct((rows, 1, size // rows), F32),
        compiler_params=pltpu.CompilerParams(vmem_limit_bytes=8 * 2**20),
        cost_estimate=pl.CostEstimate(flops=4 * size, bytes_accessed=20 * size, transcendentals=0),
        name="sum_to_rows",
    )(parts)


def backward_kernel(
    mine, one, two, three, cells, left, right, tap, grad, rows_out, line, table, sides, sems,
    square, columns,
):
    reach = left.shape[1]
    count = cells.shape[1]
    rows = 16
    copies = [
        pltpu.make_async_copy(side, sides.at[i], sems.at[i])
        for i, side in enumerate((left, right))
    ]
    for copy in copies:
        copy.start()
    lane = lax.broadcasted_iota(jnp.int32, (rows, LANES), 1)
    columns[...] = tap_columns(tap, square)
    line[:, :LANES] = jnp.zeros((rows, LANES), F32)
    line[:, LANES + count :] = jnp.zeros((rows, LANES), F32)
    for copy in copies:
        copy.wait()

    @pl.loop(0, cells.shape[0] // rows)
    def _(block):
        at = pl.ds(pl.multiple_of(block * rows, rows), rows)
        line[:, LANES - reach : LANES] = sides[0, at, :].astype(F32)
        line[:, LANES + count : LANES + count + reach] = sides[1, at, :].astype(F32)
        line[:, LANES : LANES + count] = cells[at, :].astype(F32)
        whole = line[...]
        taps = columns[at, :]
        moved = []
        conv = jnp.zeros((rows, count), F32)
        for k in range(2 * reach + 1):
            shift = (reach - k) % whole.shape[1]
            turned = pltpu.roll(whole, shift, 1) if shift else whole
            moved.append(turned[:, LANES : LANES + count])
            conv = conv + taps[:, k : k + 1] * moved[k]
        sig = jax.nn.sigmoid(conv)
        total = mine[at, :] + one[at, :].astype(F32)
        total = total + two[at, :].astype(F32) + three[at, :].astype(F32)
        value = (total * (sig * (1.0 + conv * (1.0 - sig)))).astype(BF16)
        grad[at, :] = value
        value = value.astype(F32)
        found = jnp.zeros((rows, LANES), F32)
        for k in range(2 * reach + 1):
            found = jnp.where(lane == k, jnp.sum(moved[k] * value, axis=1, keepdims=True), found)
        for k in range(reach):
            found = jnp.where(lane == 8 + k, value[:, k : k + 1], found)
            last = count - reach + k
            found = jnp.where(lane == 8 + reach + k, value[:, last : last + 1], found)
        table[at, :] = found

    rows_out[...] = table[...].T[: rows_out.shape[0]]


def backward(mine, parts, cells, left, right, tap):
    rows, count = cells.shape
    return pl.pallas_call(
        backward_kernel,
        out_shape=(
            jax.ShapeDtypeStruct((rows, count), BF16),
            jax.ShapeDtypeStruct((16, rows), F32),
        ),
        in_specs=[pl.BlockSpec(memory_space=pltpu.VMEM)] * 5
        + [pl.BlockSpec(memory_space=pl.ANY)] * 2
        + [pl.BlockSpec(memory_space=pltpu.VMEM)],
        scratch_shapes=[
            pltpu.VMEM((16, count + 2 * LANES), F32),
            pltpu.VMEM((rows, LANES), F32),
            pltpu.VMEM((2,) + left.shape, left.dtype),
            pltpu.SemaphoreType.DMA((2,)),
            pltpu.VMEM((8, LANES), F32),
            pltpu.VMEM((LANES, 8), F32),
        ],
        compiler_params=pltpu.CompilerParams(vmem_limit_bytes=8 * 2**20),
        cost_estimate=pl.CostEstimate(
            flops=40 * rows * count, bytes_accessed=14 * rows * count, transcendentals=0
        ),
        name="conv_grad",
    )(mine, *parts, cells, left, right, tap)


def spread_kernel(grad, tap, embed, ends, line, square, columns):
    count = grad.shape[1]
    rows = 16
    reach = tap.shape[0] // 2
    columns[...] = tap_columns(tap, square)
    line[:, :LANES] = jnp.zeros((rows, LANES), F32)
    line[:, LANES + count :] = jnp.zeros((rows, LANES), F32)

    @pl.loop(0, grad.shape[0] // rows)
    def _(block):
        at = pl.ds(pl.multiple_of(block * rows, rows), rows)
        line[:, LANES : LANES + count] = grad[at, :].astype(F32)
        whole = line[...]
        taps = columns[at, :]
        total = jnp.zeros((rows, count), F32)
        for k in range(2 * reach + 1):
            shift = (k - reach) % whole.shape[1]
            moved = pltpu.roll(whole, shift, 1) if shift else whole
            total = total + taps[:, k : k + 1] * moved[:, LANES : LANES + count]
        embed[at, :] = total.astype(BF16)
        ends[at, :LANES] = total[:, :LANES]
        ends[at, LANES:] = total[:, count - LANES :]


def spread(grad, tap):
    rows, count = grad.shape
    return pl.pallas_call(
        spread_kernel,
        out_shape=(
            jax.ShapeDtypeStruct((rows, count), BF16),
            jax.ShapeDtypeStruct((rows, 2 * LANES), F32),
        ),
        scratch_shapes=[
            pltpu.VMEM((16, count + 2 * LANES), F32),
            pltpu.VMEM((8, LANES), F32),
            pltpu.VMEM((LANES, 8), F32),
        ],
        compiler_params=pltpu.CompilerParams(vmem_limit_bytes=8 * 2**20),
        cost_estimate=pl.CostEstimate(
            flops=10 * rows * count, bytes_accessed=4 * rows * count, transcendentals=0
        ),
        name="embed_grad",
    )(grad, tap)


def message_kernel(place, slices, found, out, rows, mixed):
    me = place[0]
    devices, _, size = out.shape
    width = found.shape[1]
    ntaps, reach = place_taps(size, width)
    rows[...] = jnp.zeros(rows.shape, F32)
    rows[:, :width] = found[...]
    taps = rows[0:8, :]
    high = taps.astype(BF16).astype(F32)
    low = taps - high
    parts = [high[k : k + 1] for k in range(ntaps)] + [low[k : k + 1] for k in range(ntaps)]
    sides = [rows[8 + k : 9 + k, :] for k in range(2 * reach)]

    def line(pieces, first):
        total = jnp.zeros((1, size), F32)
        for n, piece in enumerate(pieces):
            total = total + (pltpu.roll(piece, (first + n) * width, 1) if first + n else piece)
        return total

    row = lax.broadcasted_iota(jnp.int32, (devices, size), 0)
    value = jnp.broadcast_to(line(parts, 0), (devices, size))
    value = jnp.where(row == me - 1, value + line(sides[:reach], 2 * ntaps), value)
    value = jnp.where(row == me + 1, value + line(sides[reach:], 2 * ntaps), value)
    part = jnp.sum(slices[:, 0, :], axis=0, keepdims=True)
    mixed[:, 0, :] = jnp.broadcast_to(part, (devices, size))
    mixed[:, 1, :] = value
    out[...] = mixed[...].astype(BF16)


def place_taps(size, width):
    reach = (size // width - 2) // 5
    return 2 * reach + 1, reach


def last_message(place, slices, found, devices):
    size = slices.shape[2]
    return pl.pallas_call(
        message_kernel,
        out_shape=jax.ShapeDtypeStruct((devices, 2, size), BF16),
        in_specs=[pl.BlockSpec(memory_space=pltpu.SMEM)]
        + [pl.BlockSpec(memory_space=pltpu.VMEM)] * 2,
        scratch_shapes=[
            pltpu.VMEM((found.shape[0], size), F32),
            pltpu.VMEM((devices, 2, size), F32),
        ],
        compiler_params=pltpu.CompilerParams(vmem_limit_bytes=6 * 2**20),
        cost_estimate=pl.CostEstimate(
            flops=4 * devices * size, bytes_accessed=8 * devices * size, transcendentals=0
        ),
        name="message",
    )(place, slices, found)


def finish_kernel(
    place, slab, ends, tap, given, embed, weight, sums,
    square, columns, edges, tiles, plain, sems,
):
    del given
    ntaps, width = tap.shape
    reach = ntaps // 2
    devices, _, size = slab.shape
    me = place[0]
    plain[...] = slab[...].astype(F32)
    columns[...] = tap_columns(tap, square)

    edges[...] = jnp.zeros(edges.shape, F32)
    start = 2 * ntaps * width
    for side, other in enumerate((me - 1, me + 1)):
        row = plain[jnp.clip(other, 0, devices - 1), 1:2, :]
        row = jnp.where((other >= 0) & (other < devices), row, 0.0)
        for k in range(reach):
            turned = pltpu.roll(row, size - start - k * width, 1)
            edges[side * reach + k : side * reach + k + 1, :] = turned[:, :LANES]
    outer = edges[...].T[:width]

    lane = lax.broadcasted_iota(jnp.int32, (width, LANES), 1)
    first, last = ends[:, :LANES], ends[:, LANES:]
    for column in range(reach):
        for k in range(ntaps):
            source = column - k + reach
            if source < 0:
                mirror = ntaps - 1 - k
                before = outer[:, reach + source : reach + source + 1]
                after = outer[:, reach - 1 - source : reach - source]
                value = columns[:width, k : k + 1] * before
                first = first + jnp.where(lane == column, value, 0.0)
                value = columns[:width, mirror : mirror + 1] * after
                last = last + jnp.where(lane == LANES - 1 - column, value, 0.0)
    count = embed.shape[1]
    writes = []
    for n, (tile, at) in enumerate(((first, 0), (last, count - LANES))):
        tiles[n] = tile.astype(BF16)
        writes.append(
            pltpu.make_async_copy(tiles.at[n], embed.at[:, pl.ds(at, LANES)], sems.at[n])
        )
        writes[n].start()

    per_row, wide = size // LANES, weight.shape[1] // LANES
    for tile in range(devices // 8 * per_row):
        group, spot = tile // per_row, tile % per_row * LANES
        row, col = tile // wide * 8, tile % wide * LANES
        weight[row : row + 8, col : col + LANES] = plain[
            group * 8 : group * 8 + 8, 0, spot : spot + LANES
        ]

    total = jnp.sum(plain[:, 1, :], axis=0, keepdims=True)
    for k in range(ntaps):
        high = pltpu.roll(total, size - k * width, 1) if k else total
        low = pltpu.roll(total, size - (ntaps + k) * width, 1)
        sums[k : k + 1, :] = (high + low)[:, :width]
    for write in writes:
        write.wait()


def finish(place, slab, ends, tap, embed, weight_shape):
    ntaps, width = tap.shape
    return pl.pallas_call(
        finish_kernel,
        out_shape=(
            jax.ShapeDtypeStruct(embed.shape, embed.dtype),
            jax.ShapeDtypeStruct(weight_shape, F32),
            jax.ShapeDtypeStruct((ntaps, width), F32),
        ),
        in_specs=[pl.BlockSpec(memory_space=pltpu.SMEM)]
        + [pl.BlockSpec(memory_space=pltpu.VMEM)] * 3
        + [pl.BlockSpec(memory_space=pl.ANY)],
        out_specs=(
            pl.BlockSpec(memory_space=pl.ANY),
            pl.BlockSpec(memory_space=pltpu.VMEM),
            pl.BlockSpec(memory_space=pltpu.VMEM),
        ),
        input_output_aliases={4: 0},
        scratch_shapes=[
            pltpu.VMEM((8, LANES), F32),
            pltpu.VMEM((LANES, 8), F32),
            pltpu.VMEM((8, LANES), F32),
            pltpu.VMEM((2, width, LANES), BF16),
            pltpu.VMEM(slab.shape, F32),
            pltpu.SemaphoreType.DMA((2,)),
        ],
        compiler_params=pltpu.CompilerParams(vmem_limit_bytes=8 * 2**20),
        cost_estimate=pl.CostEstimate(
            flops=slab.size, bytes_accessed=8 * slab.size, transcendentals=0
        ),
        name="finish",
    )(place, slab, ends, tap, embed)


def shards(embeddings, taps, head_weight, targets):
    width = embeddings.shape[0]
    count = embeddings.shape[1]
    tracks = head_weight.shape[0]
    ntaps = taps.shape[0]
    reach = ntaps // 2
    y = lax.axis_index("y")
    c = lax.axis_index("c")
    ny = lax.axis_size("y")
    nseq = lax.axis_size(SEQ)
    me = lax.axis_index(SEQ)
    features = ny * 2 * width

    place = jnp.stack([y, c])
    left, right = outer_columns(embeddings, reach)
    block = with_rim(embeddings, left, right, taps, forward(embeddings, taps))

    mine = lax.all_to_all(
        jnp.broadcast_to(block[None], (ny, width, count)), "y", 0, 0, tiled=True
    ).reshape(ny * width, count)
    theirs = other_core(mine)
    weight = head_weight.T
    near, counts = near_logits(place, weight, mine, targets)
    expo, stats = far_logits(place, weight, theirs, near, counts)
    every = share(stats[:3].reshape(-1), SEQ)
    tops = every[:, :LANES]
    peak = jnp.max(tops, axis=0)
    total = jnp.sum(every[:, LANES : 2 * LANES] * jnp.exp(tops - peak[None]), axis=0)
    counts = jnp.sum(every[:, 2 * LANES :], axis=0)
    scale = counts * jnp.exp(stats[0] - peak) / jnp.where(total > 0.0, total, 1.0)
    logit_grad, sent = logit_gradient(
        place, weight, jnp.broadcast_to(scale[None], (8, LANES)), expo, targets
    )
    received = other_core(sent)

    nx, nz = lax.axis_size("x"), lax.axis_size("z")
    late_grad, _ = lax.optimization_barrier((logit_grad, sent))
    local = outer_product(place, late_grad, mine, theirs)
    own, *blocks = scatter_blocks(place, weight, logit_grad, received)
    parts = [along_y(blocks[shift - 1], shift) for shift in (2, 1, 3)]

    local, own = lax.optimization_barrier((local, own))
    part = lax.all_to_all(local.reshape(nx, tracks // nx, features), "x", 0, 0, tiled=True)
    part, own = lax.optimization_barrier((sum_to_rows(part, nz), own))
    part = lax.all_to_all(part, "z", 0, 0, tiled=True)
    conv_grad, found = backward(own, parts, embeddings, left, right, taps)

    message = last_message(me.reshape(1), part, found, nseq)
    slab = lax.all_to_all(message, SEQ, 0, 0, tiled=True)
    embed_grad, ends = spread(conv_grad, taps)
    embed_grad, weight_grad, taps_grad = finish(
        me.reshape(1), slab, ends, taps, embed_grad, (tracks, features)
    )
    return embed_grad, weight_grad, taps_grad


def solution(mesh):
    fine = Mesh(np.asarray(mesh.devices).reshape(4, 16, 4, 2), ("x", "z", "y", "c"))
    track = ("y", "c")
    return jax.shard_map(
        shards,
        mesh=fine,
        in_specs=(P(track, SEQ), P(None, track), P(track, None), P(track, SEQ)),
        out_specs=(P(track, SEQ), P(track, None), P(None, track)),
        check_vma=False,
    )
```

```python
import functools

import jax
import jax.numpy as jnp
import numpy as np
from jax import lax
from jax.experimental import pallas as pl
from jax.experimental.pallas import tpu as pltpu
from jax.sharding import Mesh
from jax.sharding import PartitionSpec as P

F32 = jnp.float32
BF16 = jnp.bfloat16
SEQ = ("x", "z")
LANES = 128


def along_y(value, shift):
    count = lax.axis_size("y")
    return lax.ppermute(value, "y", [(i, (i + shift) % count) for i in range(count)])


def other_core(value):
    return lax.ppermute(value, "c", [(0, 1), (1, 0)])


def outer_columns(cells, width):
    count = lax.axis_size(SEQ)
    left = lax.ppermute(cells[:, -width:], SEQ, [(i, i + 1) for i in range(count - 1)])
    right = lax.ppermute(cells[:, :width], SEQ, [(i + 1, i) for i in range(count - 1)])
    return left, right


def share(value, axes):
    count = lax.axis_size(axes)
    copies = jnp.broadcast_to(value.reshape(1, 1, -1), (count, 1, value.size))
    return lax.all_to_all(copies, axes, 0, 0, tiled=True)[:, 0]


def tap_columns(tap, square):
    count, features = tap.shape
    square[:, :] = jnp.zeros(square.shape, F32)
    square[:count, :features] = tap[...].astype(F32)
    return square[...].T


def forward_kernel(cells, tap, hidden, line, square, columns):
    rows = 16
    count = cells.shape[1]
    reach = tap.shape[0] // 2
    columns[...] = tap_columns(tap, square)
    line[:, :LANES] = jnp.zeros((rows, LANES), F32)
    line[:, LANES + count :] = jnp.zeros((rows, LANES), F32)

    @pl.loop(0, cells.shape[0] // rows)
    def _(block):
        at = pl.ds(pl.multiple_of(block * rows, rows), rows)
        line[:, LANES : LANES + count] = cells[at, :].astype(F32)
        whole = line[...]
        taps = columns[at, :]
        conv = jnp.zeros((rows, count), F32)
        for k in range(2 * reach + 1):
            shift = (reach - k) % whole.shape[1]
            moved = pltpu.roll(whole, shift, 1) if shift else whole
            conv = conv + taps[:, k : k + 1] * moved[:, LANES : LANES + count]
        hidden[at, :] = (conv * jax.nn.sigmoid(conv)).astype(BF16)


def forward(cells, tap):
    rows, count = cells.shape
    return pl.pallas_call(
        forward_kernel,
        out_shape=jax.ShapeDtypeStruct((rows, count), BF16),
        scratch_shapes=[
            pltpu.VMEM((16, count + 2 * LANES), F32),
            pltpu.VMEM((8, LANES), F32),
            pltpu.VMEM((LANES, 8), F32),
        ],
        compiler_params=pltpu.CompilerParams(vmem_limit_bytes=4 * 2**20),
        cost_estimate=pl.CostEstimate(
            flops=20 * rows * count, bytes_accessed=4 * rows * count, transcendentals=rows * count
        ),
        name="conv_silu",
    )(cells, tap)


def rim_kernel(cells, left, right, tap, given, hidden, line, square, columns, tiles, sems):
    del given
    width, count = cells.shape
    reach = left.shape[1]
    columns[...] = tap_columns(tap, square)
    taps = columns[:width, :]
    line[...] = jnp.zeros(line.shape, F32)
    writes = []
    for side, at in enumerate((0, count - LANES)):
        line[:, LANES : 2 * LANES] = cells[:, at : at + LANES].astype(F32)
        if side == 0:
            line[:, LANES - reach : LANES] = left[...].astype(F32)
            line[:, 2 * LANES :] = cells[:, at + LANES : at + 2 * LANES].astype(F32)
        else:
            line[:, :LANES] = cells[:, at - LANES : at].astype(F32)
            line[:, 2 * LANES : 2 * LANES + reach] = right[...].astype(F32)
        whole = line[...]
        conv = jnp.zeros((width, LANES), F32)
        for k in range(2 * reach + 1):
            shift = (reach - k) % whole.shape[1]
            moved = pltpu.roll(whole, shift, 1) if shift else whole
            conv = conv + taps[:, k : k + 1] * moved[:, LANES : 2 * LANES]
        tiles[side] = (conv * jax.nn.sigmoid(conv)).astype(BF16)
        spot = hidden.at[:, pl.ds(at, LANES)]
        writes.append(pltpu.make_async_copy(tiles.at[side], spot, sems.at[side]))
        writes[side].start()
    for write in writes:
        write.wait()


def with_rim(cells, left, right, tap, hidden):
    width, _ = cells.shape
    return pl.pallas_call(
        rim_kernel,
        out_shape=jax.ShapeDtypeStruct(hidden.shape, hidden.dtype),
        in_specs=[pl.BlockSpec(memory_space=pltpu.VMEM)] * 4
        + [pl.BlockSpec(memory_space=pl.ANY)],
        out_specs=pl.BlockSpec(memory_space=pl.ANY),
        input_output_aliases={4: 0},
        scratch_shapes=[
            pltpu.VMEM((width, 3 * LANES), F32),
            pltpu.VMEM((8, LANES), F32),
            pltpu.VMEM((LANES, 8), F32),
            pltpu.VMEM((2, width, LANES), BF16),
            pltpu.SemaphoreType.DMA((2,)),
        ],
        compiler_params=pltpu.CompilerParams(vmem_limit_bytes=4 * 2**20),
        cost_estimate=pl.CostEstimate(
            flops=40 * width * LANES, bytes_accessed=8 * width * LANES, transcendentals=0
        ),
        name="outer_columns",
    )(cells, left, right, tap, hidden)


def pick_rows(weight, picked, blocks):
    width = picked.shape[0] // 4
    for chip, block in enumerate(blocks):
        at = pl.ds(pl.multiple_of(block * width, 16), width)
        picked[chip * width : (chip + 1) * width, :] = weight[at, :]


TURN = (((0,), (0,)), ((), ()))


def near_kernel(place, weight, hidden, targets, logits, counts, picked):
    pick_rows(weight, picked, [2 * chip + place[1] for chip in range(4)])
    logits[...] = lax.dot_general(picked[...], hidden[...], TURN, preferred_element_type=F32)
    counts[...] = jnp.broadcast_to(jnp.sum(targets[...], axis=1, keepdims=True), counts.shape)


def far_kernel(place, weight, hidden, near, counts, expo, stats, picked, table):
    tracks = near.shape[0]
    pick_rows(weight, picked, [2 * chip + 1 - place[1] for chip in range(4)])
    logits = lax.dot_general(picked[...], hidden[...], TURN, preferred_element_type=F32)
    logits = logits + near[...]
    top = jnp.max(logits, axis=1, keepdims=True)
    value = jnp.exp(logits - top)
    expo[...] = value
    total = jnp.sum(value, axis=1, keepdims=True)
    lane = lax.broadcasted_iota(jnp.int32, (tracks, LANES), 1)
    table[...] = jnp.zeros(table.shape, F32)
    table[:tracks, :] = jnp.where(lane == 0, top, jnp.where(lane == 1, total, counts[...]))
    stats[...] = table[...].T[: stats.shape[0]]


def kernel_call(body, name, outs, scratch, place, *operands, flops=0):
    size = sum(o.size * o.dtype.itemsize for o in operands)
    size += sum(o.size * o.dtype.itemsize for o in outs)
    return pl.pallas_call(
        body,
        out_shape=outs,
        in_specs=[pl.BlockSpec(memory_space=pltpu.SMEM)]
        + [pl.BlockSpec(memory_space=pltpu.VMEM)] * len(operands),
        scratch_shapes=scratch,
        compiler_params=pltpu.CompilerParams(vmem_limit_bytes=size + 4 * 2**20),
        cost_estimate=pl.CostEstimate(flops=flops, bytes_accessed=size, transcendentals=0),
        name=name,
    )(place, *operands)


def near_logits(place, weight, hidden, targets):
    tracks, count = targets.shape
    outs = (
        jax.ShapeDtypeStruct((tracks, count), F32),
        jax.ShapeDtypeStruct((tracks, LANES), F32),
    )
    scratch = [pltpu.VMEM((hidden.shape[0], tracks), BF16)]
    return kernel_call(
        near_kernel, "near_logits", outs, scratch, place, weight, hidden, targets,
        flops=2 * hidden.size * tracks,
    )


def far_logits(place, weight, hidden, near, counts):
    tracks = near.shape[0]
    outs = (
        jax.ShapeDtypeStruct(near.shape, F32),
        jax.ShapeDtypeStruct((8, LANES), F32),
    )
    scratch = [
        pltpu.VMEM((hidden.shape[0], tracks), BF16),
        pltpu.VMEM((LANES, LANES), F32),
    ]
    return kernel_call(
        far_kernel, "far_logits", outs, scratch, place, weight, hidden, near, counts,
        flops=2 * hidden.size * tracks,
    )


def grad_kernel(place, weight, scale, expo, targets, grad, sent, picked):
    tracks = expo.shape[0]
    column = scale[...].T[:tracks, 0:1]
    value = (column * expo[...] - targets[...]).astype(BF16)
    grad[...] = value
    blocks = [2 * lax.rem(place[0] + shift, 4) + 1 - place[1] for shift in range(4)]
    pick_rows(weight, picked, blocks)
    sent[...] = jnp.dot(picked[...], value, preferred_element_type=F32).astype(BF16)


def logit_gradient(place, weight, scale, expo, targets):
    tracks, count = expo.shape
    outs = (
        jax.ShapeDtypeStruct((tracks, count), BF16),
        jax.ShapeDtypeStruct((weight.shape[0] // 2, count), BF16),
    )
    scratch = [pltpu.VMEM((weight.shape[0] // 2, tracks), BF16)]
    return kernel_call(
        grad_kernel, "logit_grad", outs, scratch, place, weight, scale, expo, targets,
        flops=weight.size * count,
    )


def scatter_kernel(place, weight, grad, received, mine, one, two, three, picked):
    width = mine.shape[0]
    blocks = [2 * lax.rem(place[0] + shift, 4) + place[1] for shift in range(4)]
    pick_rows(weight, picked, blocks)
    part = jnp.dot(picked[...], grad[...], preferred_element_type=F32)
    for shift, out in enumerate((mine, one, two, three)):
        at = slice(shift * width, (shift + 1) * width)
        out[...] = (part[at] + received[at, :].astype(F32)).astype(out.dtype)


def scatter_blocks(place, weight, grad, received):
    tracks, count = grad.shape
    width = received.shape[0] // 4
    block = jax.ShapeDtypeStruct((width, count), BF16)
    outs = (jax.ShapeDtypeStruct((width, count), F32), block, block, block)
    scratch = [pltpu.VMEM((received.shape[0], tracks), BF16)]
    return kernel_call(
        scatter_kernel, "core_sum", outs, scratch, place, weight, grad, received,
        flops=weight.size * count,
    )


def outer_kernel(place, grad, mine, theirs, out, table):
    tracks = grad.shape[0]
    width = mine.shape[0] // 4
    along = (((1,), (1,)), ((), ()))
    for block, offset in ((mine, place[1]), (theirs, 1 - place[1])):
        part = lax.dot_general(block[...], grad[...], along, preferred_element_type=F32)
        for chip in range(4):
            row = (2 * chip + offset) * width
            at = pl.ds(pl.multiple_of(row, 16), width)
            table[at, :tracks] = part[chip * width : (chip + 1) * width]
    out[...] = table[...].T[:tracks]


def outer_product(place, grad, mine, theirs):
    tracks = grad.shape[0]
    features = 2 * mine.shape[0]
    return kernel_call(
        outer_kernel, "weight_part", (jax.ShapeDtypeStruct((tracks, features), F32),),
        [pltpu.VMEM((features, LANES), F32)], place, grad, mine, theirs,
        flops=2 * features * grad.size,
    )[0]


def rows_kernel(parts, out):
    wide = parts.shape[2] // LANES
    tiles = out.shape[2] // LANES
    for tile in range(parts.shape[1] // 8 * wide):
        row, lane = tile // wide * 8, tile % wide * LANES
        group, spot = tile // tiles, tile % tiles * LANES
        total = jnp.sum(parts[:, row : row + 8, lane : lane + LANES], axis=0)
        out[group * 8 : group * 8 + 8, 0, spot : spot + LANES] = total


def sum_to_rows(parts, rows):
    size = parts.shape[1] * parts.shape[2]
    return pl.pallas_call(
        rows_kernel,
        out_shape=jax.ShapeDtypeStruct((rows, 1, size // rows), F32),
        compiler_params=pltpu.CompilerParams(vmem_limit_bytes=8 * 2**20),
        cost_estimate=pl.CostEstimate(flops=4 * size, bytes_accessed=20 * size, transcendentals=0),
        name="sum_to_rows",
    )(parts)


def backward_kernel(
    mine, one, two, three, cells, left, right, tap, grad, rows_out, line, table, sides, sems,
    square, columns,
):
    reach = left.shape[1]
    count = cells.shape[1]
    rows = 16
    copies = [
        pltpu.make_async_copy(side, sides.at[i], sems.at[i])
        for i, side in enumerate((left, right))
    ]
    for copy in copies:
        copy.start()
    lane = lax.broadcasted_iota(jnp.int32, (rows, LANES), 1)
    columns[...] = tap_columns(tap, square)
    line[:, :LANES] = jnp.zeros((rows, LANES), F32)
    line[:, LANES + count :] = jnp.zeros((rows, LANES), F32)
    for copy in copies:
        copy.wait()

    @pl.loop(0, cells.shape[0] // rows)
    def _(block):
        at = pl.ds(pl.multiple_of(block * rows, rows), rows)
        line[:, LANES - reach : LANES] = sides[0, at, :].astype(F32)
        line[:, LANES + count : LANES + count + reach] = sides[1, at, :].astype(F32)
        line[:, LANES : LANES + count] = cells[at, :].astype(F32)
        whole = line[...]
        taps = columns[at, :]
        moved = []
        conv = jnp.zeros((rows, count), F32)
        for k in range(2 * reach + 1):
            shift = (reach - k) % whole.shape[1]
            turned = pltpu.roll(whole, shift, 1) if shift else whole
            moved.append(turned[:, LANES : LANES + count])
            conv = conv + taps[:, k : k + 1] * moved[k]
        sig = jax.nn.sigmoid(conv)
        total = mine[at, :] + one[at, :].astype(F32)
        total = total + two[at, :].astype(F32) + three[at, :].astype(F32)
        value = (total * (sig * (1.0 + conv * (1.0 - sig)))).astype(BF16)
        grad[at, :] = value
        value = value.astype(F32)
        found = jnp.zeros((rows, LANES), F32)
        for k in range(2 * reach + 1):
            found = jnp.where(lane == k, jnp.sum(moved[k] * value, axis=1, keepdims=True), found)
        for k in range(reach):
            found = jnp.where(lane == 8 + k, value[:, k : k + 1], found)
            last = count - reach + k
            found = jnp.where(lane == 8 + reach + k, value[:, last : last + 1], found)
        table[at, :] = found

    rows_out[...] = table[...].T[: rows_out.shape[0]]


def backward(mine, parts, cells, left, right, tap):
    rows, count = cells.shape
    return pl.pallas_call(
        backward_kernel,
        out_shape=(
            jax.ShapeDtypeStruct((rows, count), BF16),
            jax.ShapeDtypeStruct((16, rows), F32),
        ),
        in_specs=[pl.BlockSpec(memory_space=pltpu.VMEM)] * 5
        + [pl.BlockSpec(memory_space=pl.ANY)] * 2
        + [pl.BlockSpec(memory_space=pltpu.VMEM)],
        scratch_shapes=[
            pltpu.VMEM((16, count + 2 * LANES), F32),
            pltpu.VMEM((rows, LANES), F32),
            pltpu.VMEM((2,) + left.shape, left.dtype),
            pltpu.SemaphoreType.DMA((2,)),
            pltpu.VMEM((8, LANES), F32),
            pltpu.VMEM((LANES, 8), F32),
        ],
        compiler_params=pltpu.CompilerParams(vmem_limit_bytes=8 * 2**20),
        cost_estimate=pl.CostEstimate(
            flops=40 * rows * count, bytes_accessed=14 * rows * count, transcendentals=0
        ),
        name="conv_grad",
    )(mine, *parts, cells, left, right, tap)


def spread_kernel(grad, tap, embed, ends, line, square, columns):
    count = grad.shape[1]
    rows = 16
    reach = tap.shape[0] // 2
    columns[...] = tap_columns(tap, square)
    line[:, :LANES] = jnp.zeros((rows, LANES), F32)
    line[:, LANES + count :] = jnp.zeros((rows, LANES), F32)

    @pl.loop(0, grad.shape[0] // rows)
    def _(block):
        at = pl.ds(pl.multiple_of(block * rows, rows), rows)
        line[:, LANES : LANES + count] = grad[at, :].astype(F32)
        whole = line[...]
        taps = columns[at, :]
        total = jnp.zeros((rows, count), F32)
        for k in range(2 * reach + 1):
            shift = (k - reach) % whole.shape[1]
            moved = pltpu.roll(whole, shift, 1) if shift else whole
            total = total + taps[:, k : k + 1] * moved[:, LANES : LANES + count]
        embed[at, :] = total.astype(BF16)
        ends[at, :LANES] = total[:, :LANES]
        ends[at, LANES:] = total[:, count - LANES :]


def spread(grad, tap):
    rows, count = grad.shape
    return pl.pallas_call(
        spread_kernel,
        out_shape=(
            jax.ShapeDtypeStruct((rows, count), BF16),
            jax.ShapeDtypeStruct((rows, 2 * LANES), F32),
        ),
        scratch_shapes=[
            pltpu.VMEM((16, count + 2 * LANES), F32),
            pltpu.VMEM((8, LANES), F32),
            pltpu.VMEM((LANES, 8), F32),
        ],
        compiler_params=pltpu.CompilerParams(vmem_limit_bytes=8 * 2**20),
        cost_estimate=pl.CostEstimate(
            flops=10 * rows * count, bytes_accessed=4 * rows * count, transcendentals=0
        ),
        name="embed_grad",
    )(grad, tap)


def in_line(pieces, width, size, first=0):
    total = jnp.zeros((1, size), F32)
    for n, piece in enumerate(pieces):
        total = total + (pltpu.roll(piece, (first + n) * width, 1) if first + n else piece)
    return total


def high_and_low(line, ntaps, width):
    taps = lax.broadcasted_iota(jnp.int32, line.shape, 1) < ntaps * width
    line = jnp.where(taps, line, 0.0)
    high = line.astype(BF16).astype(F32)
    return high + pltpu.roll(line - high, ntaps * width, 1)


def message_kernel(place, slices, found, out, rows, mixed):
    z = place[0]
    devices, _, size = out.shape
    width = found.shape[1]
    ntaps, reach = place_taps(size, width)
    rows[...] = jnp.zeros(rows.shape, F32)
    rows[:, :width] = found[...]
    sides = [rows[8 + k : 9 + k, :] for k in range(2 * reach)]
    row = lax.broadcasted_iota(jnp.int32, (devices, size), 0)
    taps = in_line([rows[k : k + 1, :] for k in range(ntaps)], width, size)
    value = jnp.broadcast_to(high_and_low(taps, ntaps, width), (devices, size))
    head = in_line(sides[:reach], width, size, 2 * ntaps)
    tail = in_line(sides[reach:], width, size, 2 * ntaps)
    value = jnp.where(row == lax.rem(z + devices - 1, devices), value + head, value)
    value = jnp.where(row == lax.rem(z + 1, devices), value + tail, value)
    part = jnp.sum(slices[:, 0, :], axis=0, keepdims=True)
    mixed[:, 0, :] = jnp.broadcast_to(part, (devices, size))
    mixed[:, 1, :] = value
    out[...] = mixed[...].astype(BF16)


def place_taps(size, width):
    reach = (size // width - 2) // 5
    return 2 * reach + 1, reach


def last_message(place, slices, found, devices):
    size = slices.shape[2]
    return pl.pallas_call(
        message_kernel,
        out_shape=jax.ShapeDtypeStruct((devices, 2, size), BF16),
        in_specs=[pl.BlockSpec(memory_space=pltpu.SMEM)]
        + [pl.BlockSpec(memory_space=pltpu.VMEM)] * 2,
        scratch_shapes=[
            pltpu.VMEM((found.shape[0], size), F32),
            pltpu.VMEM((devices, 2, size), F32),
        ],
        compiler_params=pltpu.CompilerParams(vmem_limit_bytes=6 * 2**20),
        cost_estimate=pl.CostEstimate(
            flops=4 * devices * size, bytes_accessed=8 * devices * size, transcendentals=0
        ),
        name="message",
    )(place, slices, found)


def tap_line(total, ntaps, width):
    return total + pltpu.roll(total, total.shape[1] - ntaps * width, 1)


def onward_kernel(width, place, slab, out, plain, last):
    z, nz, x = place[0], place[1], place[2]
    devices, _, size = out.shape
    ntaps, _ = place_taps(size, width)
    count = slab.shape[0]
    plain[...] = slab[...].astype(F32)
    total = jnp.sum(plain[:, 1, :], axis=0, keepdims=True)
    value = high_and_low(tap_line(total, ntaps, width), ntaps, width)
    halo = lax.broadcasted_iota(jnp.int32, (1, size), 1) >= 2 * ntaps * width
    up = jnp.where(halo & (z == 0), plain[count - 1, 1:2, :], 0.0)
    down = jnp.where(halo & (z == nz - 1), plain[0, 1:2, :], 0.0)
    slices = plain[:, 0, :].astype(BF16)
    last[...] = jnp.zeros(last.shape, F32)
    for other in range(devices):
        out[other, :count, :] = slices
        passed = jnp.where(x + 1 == other, up, 0.0) + jnp.where(x - 1 == other, down, 0.0)
        last[0:1, :] = value + passed
        out[other, count:, :] = last[...].astype(BF16)


def onward(place, slab, devices, width):
    count, _, size = slab.shape
    return pl.pallas_call(
        functools.partial(onward_kernel, width),
        out_shape=jax.ShapeDtypeStruct((devices, count + 16, size), BF16),
        in_specs=[
            pl.BlockSpec(memory_space=pltpu.SMEM),
            pl.BlockSpec(memory_space=pltpu.VMEM),
        ],
        scratch_shapes=[
            pltpu.VMEM(slab.shape, F32),
            pltpu.VMEM((16, size), F32),
        ],
        compiler_params=pltpu.CompilerParams(vmem_limit_bytes=6 * 2**20),
        cost_estimate=pl.CostEstimate(
            flops=2 * slab.size, bytes_accessed=12 * slab.size, transcendentals=0
        ),
        name="onward",
    )(place, slab)


def finish_kernel(
    place, slab, wide, ends, tap, given, embed, weight, sums,
    square, columns, edges, tiles, plain, sems,
):
    del given
    ntaps, width = tap.shape
    reach = ntaps // 2
    nz, _, size = slab.shape
    nx = wide.shape[0]
    z, x = place[0], place[2]
    plain[...] = slab[...].astype(F32)
    columns[...] = tap_columns(tap, square)

    edges[...] = jnp.zeros(edges.shape, F32)
    start = 2 * ntaps * width
    lasts = [wide[n, nz:, :].astype(F32)[0:1, :] for n in range(nx)]
    for side, step in enumerate((-1, 1)):
        inner = (z + step >= 0) & (z + step < nz)
        row = jnp.zeros((1, size), F32)
        for n in range(nx):
            row = jnp.where(x + step == n, lasts[n], row)
        row = jnp.where(inner, plain[jnp.clip(z + step, 0, nz - 1), 1:2, :], row)
        for k in range(reach):
            turned = pltpu.roll(row, size - start - k * width, 1)
            edges[side * reach + k : side * reach + k + 1, :] = turned[:, :LANES]
    outer = edges[...].T[:width]

    lane = lax.broadcasted_iota(jnp.int32, (width, LANES), 1)
    first, last = ends[:, :LANES], ends[:, LANES:]
    for column in range(reach):
        for k in range(ntaps):
            source = column - k + reach
            if source < 0:
                mirror = ntaps - 1 - k
                before = outer[:, reach + source : reach + source + 1]
                after = outer[:, reach - 1 - source : reach - source]
                value = columns[:width, k : k + 1] * before
                first = first + jnp.where(lane == column, value, 0.0)
                value = columns[:width, mirror : mirror + 1] * after
                last = last + jnp.where(lane == LANES - 1 - column, value, 0.0)
    count = embed.shape[1]
    writes = []
    for n, (tile, at) in enumerate(((first, 0), (last, count - LANES))):
        tiles[n] = tile.astype(BF16)
        writes.append(
            pltpu.make_async_copy(tiles.at[n], embed.at[:, pl.ds(at, LANES)], sems.at[n])
        )
        writes[n].start()

    per_row, across = size // LANES, weight.shape[1] // LANES
    for n in range(nx):
        block = wide[n, :nz, :].astype(F32)
        for tile in range(nz // 8 * per_row):
            group, spot = tile // per_row, tile % per_row * LANES
            number = n * (nz // 8 * per_row) + tile
            row, col = number // across * 8, number % across * LANES
            weight[row : row + 8, col : col + LANES] = block[
                group * 8 : group * 8 + 8, spot : spot + LANES
            ]

    line = tap_line(sum(lasts), ntaps, width)
    for k in range(ntaps):
        found = pltpu.roll(line, size - k * width, 1) if k else line
        sums[k : k + 1, :] = found[:, :width]
    for write in writes:
        write.wait()


def finish(place, slab, wide, ends, tap, embed, weight_shape):
    ntaps, width = tap.shape
    return pl.pallas_call(
        finish_kernel,
        out_shape=(
            jax.ShapeDtypeStruct(embed.shape, embed.dtype),
            jax.ShapeDtypeStruct(weight_shape, F32),
            jax.ShapeDtypeStruct((ntaps, width), F32),
        ),
        in_specs=[pl.BlockSpec(memory_space=pltpu.SMEM)]
        + [pl.BlockSpec(memory_space=pltpu.VMEM)] * 4
        + [pl.BlockSpec(memory_space=pl.ANY)],
        out_specs=(
            pl.BlockSpec(memory_space=pl.ANY),
            pl.BlockSpec(memory_space=pltpu.VMEM),
            pl.BlockSpec(memory_space=pltpu.VMEM),
        ),
        input_output_aliases={5: 0},
        scratch_shapes=[
            pltpu.VMEM((8, LANES), F32),
            pltpu.VMEM((LANES, 8), F32),
            pltpu.VMEM((8, LANES), F32),
            pltpu.VMEM((2, width, LANES), BF16),
            pltpu.VMEM(slab.shape, F32),
            pltpu.SemaphoreType.DMA((2,)),
        ],
        compiler_params=pltpu.CompilerParams(vmem_limit_bytes=8 * 2**20),
        cost_estimate=pl.CostEstimate(
            flops=slab.size, bytes_accessed=8 * slab.size, transcendentals=0
        ),
        name="finish",
    )(place, slab, wide, ends, tap, embed)


def shards(embeddings, taps, head_weight, targets):
    width = embeddings.shape[0]
    count = embeddings.shape[1]
    tracks = head_weight.shape[0]
    ntaps = taps.shape[0]
    reach = ntaps // 2
    y = lax.axis_index("y")
    c = lax.axis_index("c")
    ny = lax.axis_size("y")
    features = ny * 2 * width

    place = jnp.stack([y, c])
    left, right = outer_columns(embeddings, reach)
    block = with_rim(embeddings, left, right, taps, forward(embeddings, taps))

    mine = lax.all_to_all(
        jnp.broadcast_to(block[None], (ny, width, count)), "y", 0, 0, tiled=True
    ).reshape(ny * width, count)
    theirs = other_core(mine)
    weight = head_weight.T
    near, counts = near_logits(place, weight, mine, targets)
    expo, stats = far_logits(place, weight, theirs, near, counts)
    every = share(stats[:3].reshape(-1), SEQ)
    tops = every[:, :LANES]
    peak = jnp.max(tops, axis=0)
    total = jnp.sum(every[:, LANES : 2 * LANES] * jnp.exp(tops - peak[None]), axis=0)
    counts = jnp.sum(every[:, 2 * LANES :], axis=0)
    scale = counts * jnp.exp(stats[0] - peak) / jnp.where(total > 0.0, total, 1.0)
    logit_grad, sent = logit_gradient(
        place, weight, jnp.broadcast_to(scale[None], (8, LANES)), expo, targets
    )
    received = other_core(sent)

    nx, nz = lax.axis_size("x"), lax.axis_size("z")
    late_grad, _ = lax.optimization_barrier((logit_grad, sent))
    local = outer_product(place, late_grad, mine, theirs)
    own, *blocks = scatter_blocks(place, weight, logit_grad, received)
    parts = [along_y(blocks[shift - 1], shift) for shift in (2, 1, 3)]

    local, own = lax.optimization_barrier((local, own))
    part = lax.all_to_all(local.reshape(nx, tracks // nx, features), "x", 0, 0, tiled=True)
    part, own = lax.optimization_barrier((sum_to_rows(part, nz), own))
    part = lax.all_to_all(part, "z", 0, 0, tiled=True)
    conv_grad, found = backward(own, parts, embeddings, left, right, taps)

    spot = jnp.stack([lax.axis_index("z"), nz, lax.axis_index("x")])
    message = last_message(spot, part, found, nz)
    slab = lax.all_to_all(message, "z", 0, 0, tiled=True)
    wide = lax.all_to_all(onward(spot, slab, nx, width), "x", 0, 0, tiled=True)
    embed_grad, ends = spread(conv_grad, taps)
    embed_grad, weight_grad, taps_grad = finish(
        spot, slab, wide, ends, taps, embed_grad, (tracks, features)
    )
    return embed_grad, weight_grad, taps_grad


def solution(mesh):
    fine = Mesh(np.asarray(mesh.devices).reshape(4, 16, 4, 2), ("x", "z", "y", "c"))
    track = ("y", "c")
    return jax.shard_map(
        shards,
        mesh=fine,
        in_specs=(P(track, SEQ), P(None, track), P(track, None), P(track, SEQ)),
        out_specs=(P(track, SEQ), P(track, None), P(None, track)),
        check_vma=False,
    )
```

```python
import functools

import jax
import jax.numpy as jnp
import numpy as np
from jax import lax
from jax.experimental import pallas as pl
from jax.experimental.pallas import tpu as pltpu
from jax.sharding import Mesh
from jax.sharding import PartitionSpec as P

F32 = jnp.float32
BF16 = jnp.bfloat16
SEQ = ("x", "z")
LANES = 128


def along_y(value, shift):
    count = lax.axis_size("y")
    return lax.ppermute(value, "y", [(i, (i + shift) % count) for i in range(count)])


def other_core(value):
    return lax.ppermute(value, "c", [(0, 1), (1, 0)])


def outer_columns(cells, width):
    count = lax.axis_size(SEQ)
    left = lax.ppermute(cells[:, -width:], SEQ, [(i, i + 1) for i in range(count - 1)])
    right = lax.ppermute(cells[:, :width], SEQ, [(i + 1, i) for i in range(count - 1)])
    return left, right


def share(value, axes):
    count = lax.axis_size(axes)
    copies = jnp.broadcast_to(value.reshape(1, 1, -1), (count, 1, value.size))
    return lax.all_to_all(copies, axes, 0, 0, tiled=True)[:, 0]


def tap_columns(tap, square):
    count, features = tap.shape
    square[:, :] = jnp.zeros(square.shape, F32)
    square[:count, :features] = tap[...].astype(F32)
    return square[...].T


def forward_kernel(cells, tap, hidden, line, square, columns):
    rows = 16
    count = cells.shape[1]
    reach = tap.shape[0] // 2
    columns[...] = tap_columns(tap, square)
    line[:, :LANES] = jnp.zeros((rows, LANES), F32)
    line[:, LANES + count :] = jnp.zeros((rows, LANES), F32)

    @pl.loop(0, cells.shape[0] // rows)
    def _(block):
        at = pl.ds(pl.multiple_of(block * rows, rows), rows)
        line[:, LANES : LANES + count] = cells[at, :].astype(F32)
        whole = line[...]
        taps = columns[at, :]
        conv = jnp.zeros((rows, count), F32)
        for k in range(2 * reach + 1):
            shift = (reach - k) % whole.shape[1]
            moved = pltpu.roll(whole, shift, 1) if shift else whole
            conv = conv + taps[:, k : k + 1] * moved[:, LANES : LANES + count]
        value = (conv * jax.nn.sigmoid(conv)).astype(BF16)
        for chip in range(hidden.shape[0]):
            hidden[chip, at, :] = value


def forward(cells, tap, chips):
    rows, count = cells.shape
    return pl.pallas_call(
        forward_kernel,
        out_shape=jax.ShapeDtypeStruct((chips, rows, count), BF16),
        scratch_shapes=[
            pltpu.VMEM((16, count + 2 * LANES), F32),
            pltpu.VMEM((8, LANES), F32),
            pltpu.VMEM((LANES, 8), F32),
        ],
        compiler_params=pltpu.CompilerParams(vmem_limit_bytes=4 * 2**20),
        cost_estimate=pl.CostEstimate(
            flops=20 * rows * count, bytes_accessed=4 * rows * count, transcendentals=rows * count
        ),
        name="conv_silu",
    )(cells, tap)


def rim_kernel(cells, left, right, tap, given, hidden, line, square, columns, tiles, sems):
    del given
    width, count = cells.shape
    reach = left.shape[1]
    columns[...] = tap_columns(tap, square)
    taps = columns[:width, :]
    line[...] = jnp.zeros(line.shape, F32)
    writes = []
    for side, at in enumerate((0, count - LANES)):
        line[:, LANES : 2 * LANES] = cells[:, at : at + LANES].astype(F32)
        if side == 0:
            line[:, LANES - reach : LANES] = left[...].astype(F32)
            line[:, 2 * LANES :] = cells[:, at + LANES : at + 2 * LANES].astype(F32)
        else:
            line[:, :LANES] = cells[:, at - LANES : at].astype(F32)
            line[:, 2 * LANES : 2 * LANES + reach] = right[...].astype(F32)
        whole = line[...]
        conv = jnp.zeros((width, LANES), F32)
        for k in range(2 * reach + 1):
            shift = (reach - k) % whole.shape[1]
            moved = pltpu.roll(whole, shift, 1) if shift else whole
            conv = conv + taps[:, k : k + 1] * moved[:, LANES : 2 * LANES]
        tiles[side] = (conv * jax.nn.sigmoid(conv)).astype(BF16)
        for chip in range(hidden.shape[0]):
            spot = hidden.at[chip, :, pl.ds(at, LANES)]
            sem = sems.at[2 * chip + side]
            writes.append(pltpu.make_async_copy(tiles.at[side], spot, sem))
            writes[-1].start()
    for write in writes:
        write.wait()


def with_rim(cells, left, right, tap, hidden):
    width, _ = cells.shape
    return pl.pallas_call(
        rim_kernel,
        out_shape=jax.ShapeDtypeStruct(hidden.shape, hidden.dtype),
        in_specs=[pl.BlockSpec(memory_space=pltpu.VMEM)] * 4
        + [pl.BlockSpec(memory_space=pl.ANY)],
        out_specs=pl.BlockSpec(memory_space=pl.ANY),
        input_output_aliases={4: 0},
        scratch_shapes=[
            pltpu.VMEM((width, 3 * LANES), F32),
            pltpu.VMEM((8, LANES), F32),
            pltpu.VMEM((LANES, 8), F32),
            pltpu.VMEM((2, width, LANES), BF16),
            pltpu.SemaphoreType.DMA((2 * hidden.shape[0],)),
        ],
        compiler_params=pltpu.CompilerParams(vmem_limit_bytes=4 * 2**20),
        cost_estimate=pl.CostEstimate(
            flops=40 * width * LANES, bytes_accessed=8 * width * LANES, transcendentals=0
        ),
        name="outer_columns",
    )(cells, left, right, tap, hidden)


def pick_rows(weight, picked, blocks):
    width = picked.shape[0] // 4
    for chip, block in enumerate(blocks):
        at = pl.ds(pl.multiple_of(block * width, 16), width)
        picked[chip * width : (chip + 1) * width, :] = weight[at, :]


TURN = (((0,), (0,)), ((), ()))


def near_kernel(place, weight, hidden, targets, logits, counts, picked):
    pick_rows(weight, picked, [2 * chip + place[1] for chip in range(4)])
    logits[...] = lax.dot_general(picked[...], hidden[...], TURN, preferred_element_type=F32)
    counts[...] = jnp.broadcast_to(jnp.sum(targets[...], axis=1, keepdims=True), counts.shape)


def far_kernel(place, weight, hidden, near, counts, expo, stats, picked, table):
    tracks = near.shape[0]
    pick_rows(weight, picked, [2 * chip + 1 - place[1] for chip in range(4)])
    logits = lax.dot_general(picked[...], hidden[...], TURN, preferred_element_type=F32)
    logits = logits + near[...]
    top = jnp.max(logits, axis=1, keepdims=True)
    value = jnp.exp(logits - top)
    expo[...] = value
    total = jnp.sum(value, axis=1, keepdims=True)
    lane = lax.broadcasted_iota(jnp.int32, (tracks, LANES), 1)
    table[...] = jnp.zeros(table.shape, F32)
    table[:tracks, :] = jnp.where(lane == 0, top, jnp.where(lane == 1, total, counts[...]))
    stats[...] = table[...].T[: stats.shape[0]]


def kernel_call(body, name, outs, scratch, place, *operands, flops=0):
    size = sum(o.size * o.dtype.itemsize for o in operands)
    size += sum(o.size * o.dtype.itemsize for o in outs)
    return pl.pallas_call(
        body,
        out_shape=outs,
        in_specs=[pl.BlockSpec(memory_space=pltpu.SMEM)]
        + [pl.BlockSpec(memory_space=pltpu.VMEM)] * len(operands),
        scratch_shapes=scratch,
        compiler_params=pltpu.CompilerParams(vmem_limit_bytes=size + 4 * 2**20),
        cost_estimate=pl.CostEstimate(flops=flops, bytes_accessed=size, transcendentals=0),
        name=name,
    )(place, *operands)


def near_logits(place, weight, hidden, targets):
    tracks, count = targets.shape
    outs = (
        jax.ShapeDtypeStruct((tracks, count), F32),
        jax.ShapeDtypeStruct((tracks, LANES), F32),
    )
    scratch = [pltpu.VMEM((hidden.shape[0], tracks), BF16)]
    return kernel_call(
        near_kernel, "near_logits", outs, scratch, place, weight, hidden, targets,
        flops=2 * hidden.size * tracks,
    )


def far_logits(place, weight, hidden, near, counts):
    tracks = near.shape[0]
    outs = (
        jax.ShapeDtypeStruct(near.shape, F32),
        jax.ShapeDtypeStruct((8, LANES), F32),
    )
    scratch = [
        pltpu.VMEM((hidden.shape[0], tracks), BF16),
        pltpu.VMEM((LANES, LANES), F32),
    ]
    return kernel_call(
        far_kernel, "far_logits", outs, scratch, place, weight, hidden, near, counts,
        flops=2 * hidden.size * tracks,
    )


def grad_kernel(place, weight, scale, expo, targets, grad, sent, picked):
    tracks = expo.shape[0]
    column = scale[...].T[:tracks, 0:1]
    value = (column * expo[...] - targets[...]).astype(BF16)
    grad[...] = value
    blocks = [2 * lax.rem(place[0] + shift, 4) + 1 - place[1] for shift in range(4)]
    pick_rows(weight, picked, blocks)
    sent[...] = jnp.dot(picked[...], value, preferred_element_type=F32).astype(BF16)


def logit_gradient(place, weight, scale, expo, targets):
    tracks, count = expo.shape
    outs = (
        jax.ShapeDtypeStruct((tracks, count), BF16),
        jax.ShapeDtypeStruct((weight.shape[0] // 2, count), BF16),
    )
    scratch = [pltpu.VMEM((weight.shape[0] // 2, tracks), BF16)]
    return kernel_call(
        grad_kernel, "logit_grad", outs, scratch, place, weight, scale, expo, targets,
        flops=weight.size * count,
    )


def scatter_kernel(place, weight, grad, received, mine, one, two, three, picked):
    width = mine.shape[0]
    blocks = [2 * lax.rem(place[0] + shift, 4) + place[1] for shift in range(4)]
    pick_rows(weight, picked, blocks)
    part = jnp.dot(picked[...], grad[...], preferred_element_type=F32)
    for shift, out in enumerate((mine, one, two, three)):
        at = slice(shift * width, (shift + 1) * width)
        out[...] = (part[at] + received[at, :].astype(F32)).astype(out.dtype)


def scatter_blocks(place, weight, grad, received):
    tracks, count = grad.shape
    width = received.shape[0] // 4
    block = jax.ShapeDtypeStruct((width, count), BF16)
    outs = (jax.ShapeDtypeStruct((width, count), F32), block, block, block)
    scratch = [pltpu.VMEM((received.shape[0], tracks), BF16)]
    return kernel_call(
        scatter_kernel, "core_sum", outs, scratch, place, weight, grad, received,
        flops=weight.size * count,
    )


def outer_kernel(place, grad, mine, theirs, out, table):
    tracks = grad.shape[0]
    width = mine.shape[0] // 4
    along = (((1,), (1,)), ((), ()))
    for block, offset in ((mine, place[1]), (theirs, 1 - place[1])):
        part = lax.dot_general(block[...], grad[...], along, preferred_element_type=F32)
        for chip in range(4):
            row = (2 * chip + offset) * width
            at = pl.ds(pl.multiple_of(row, 16), width)
            table[at, :tracks] = part[chip * width : (chip + 1) * width]
    out[...] = table[...].T[:tracks]


def outer_product(place, grad, mine, theirs):
    tracks = grad.shape[0]
    features = 2 * mine.shape[0]
    return kernel_call(
        outer_kernel, "weight_part", (jax.ShapeDtypeStruct((tracks, features), F32),),
        [pltpu.VMEM((features, LANES), F32)], place, grad, mine, theirs,
        flops=2 * features * grad.size,
    )[0]


def rows_kernel(parts, out):
    wide = parts.shape[2] // LANES
    tiles = out.shape[2] // LANES
    for tile in range(parts.shape[1] // 8 * wide):
        row, lane = tile // wide * 8, tile % wide * LANES
        group, spot = tile // tiles, tile % tiles * LANES
        total = jnp.sum(parts[:, row : row + 8, lane : lane + LANES], axis=0)
        out[group * 8 : group * 8 + 8, 0, spot : spot + LANES] = total


def sum_to_rows(parts, rows):
    size = parts.shape[1] * parts.shape[2]
    return pl.pallas_call(
        rows_kernel,
        out_shape=jax.ShapeDtypeStruct((rows, 1, size // rows), F32),
        compiler_params=pltpu.CompilerParams(vmem_limit_bytes=8 * 2**20),
        cost_estimate=pl.CostEstimate(flops=4 * size, bytes_accessed=20 * size, transcendentals=0),
        name="sum_to_rows",
    )(parts)


def backward_kernel(
    mine, one, two, three, cells, left, right, tap, grad, rows_out, line, table, sides, sems,
    square, columns,
):
    reach = left.shape[1]
    count = cells.shape[1]
    rows = 16
    copies = [
        pltpu.make_async_copy(side, sides.at[i], sems.at[i])
        for i, side in enumerate((left, right))
    ]
    for copy in copies:
        copy.start()
    lane = lax.broadcasted_iota(jnp.int32, (rows, LANES), 1)
    columns[...] = tap_columns(tap, square)
    line[:, :LANES] = jnp.zeros((rows, LANES), F32)
    line[:, LANES + count :] = jnp.zeros((rows, LANES), F32)
    for copy in copies:
        copy.wait()

    @pl.loop(0, cells.shape[0] // rows)
    def _(block):
        at = pl.ds(pl.multiple_of(block * rows, rows), rows)
        line[:, LANES - reach : LANES] = sides[0, at, :].astype(F32)
        line[:, LANES + count : LANES + count + reach] = sides[1, at, :].astype(F32)
        line[:, LANES : LANES + count] = cells[at, :].astype(F32)
        whole = line[...]
        taps = columns[at, :]
        moved = []
        conv = jnp.zeros((rows, count), F32)
        for k in range(2 * reach + 1):
            shift = (reach - k) % whole.shape[1]
            turned = pltpu.roll(whole, shift, 1) if shift else whole
            moved.append(turned[:, LANES : LANES + count])
            conv = conv + taps[:, k : k + 1] * moved[k]
        sig = jax.nn.sigmoid(conv)
        total = mine[at, :] + one[at, :].astype(F32)
        total = total + two[at, :].astype(F32) + three[at, :].astype(F32)
        value = (total * (sig * (1.0 + conv * (1.0 - sig)))).astype(BF16)
        grad[at, :] = value
        value = value.astype(F32)
        found = jnp.zeros((rows, LANES), F32)
        for k in range(2 * reach + 1):
            found = jnp.where(lane == k, jnp.sum(moved[k] * value, axis=1, keepdims=True), found)
        for k in range(reach):
            found = jnp.where(lane == 8 + k, value[:, k : k + 1], found)
            last = count - reach + k
            found = jnp.where(lane == 8 + reach + k, value[:, last : last + 1], found)
        table[at, :] = found

    rows_out[...] = table[...].T[: rows_out.shape[0]]


def backward(mine, parts, cells, left, right, tap):
    rows, count = cells.shape
    return pl.pallas_call(
        backward_kernel,
        out_shape=(
            jax.ShapeDtypeStruct((rows, count), BF16),
            jax.ShapeDtypeStruct((16, rows), F32),
        ),
        in_specs=[pl.BlockSpec(memory_space=pltpu.VMEM)] * 5
        + [pl.BlockSpec(memory_space=pl.ANY)] * 2
        + [pl.BlockSpec(memory_space=pltpu.VMEM)],
        scratch_shapes=[
            pltpu.VMEM((16, count + 2 * LANES), F32),
            pltpu.VMEM((rows, LANES), F32),
            pltpu.VMEM((2,) + left.shape, left.dtype),
            pltpu.SemaphoreType.DMA((2,)),
            pltpu.VMEM((8, LANES), F32),
            pltpu.VMEM((LANES, 8), F32),
        ],
        compiler_params=pltpu.CompilerParams(vmem_limit_bytes=8 * 2**20),
        cost_estimate=pl.CostEstimate(
            flops=40 * rows * count, bytes_accessed=14 * rows * count, transcendentals=0
        ),
        name="conv_grad",
    )(mine, *parts, cells, left, right, tap)


def spread_kernel(grad, tap, embed, ends, line, square, columns):
    count = grad.shape[1]
    rows = 16
    reach = tap.shape[0] // 2
    columns[...] = tap_columns(tap, square)
    line[:, :LANES] = jnp.zeros((rows, LANES), F32)
    line[:, LANES + count :] = jnp.zeros((rows, LANES), F32)

    @pl.loop(0, grad.shape[0] // rows)
    def _(block):
        at = pl.ds(pl.multiple_of(block * rows, rows), rows)
        line[:, LANES : LANES + count] = grad[at, :].astype(F32)
        whole = line[...]
        taps = columns[at, :]
        total = jnp.zeros((rows, count), F32)
        for k in range(2 * reach + 1):
            shift = (k - reach) % whole.shape[1]
            moved = pltpu.roll(whole, shift, 1) if shift else whole
            total = total + taps[:, k : k + 1] * moved[:, LANES : LANES + count]
        embed[at, :] = total.astype(BF16)
        ends[at, :LANES] = total[:, :LANES]
        ends[at, LANES:] = total[:, count - LANES :]


def spread(grad, tap):
    rows, count = grad.shape
    return pl.pallas_call(
        spread_kernel,
        out_shape=(
            jax.ShapeDtypeStruct((rows, count), BF16),
            jax.ShapeDtypeStruct((rows, 2 * LANES), F32),
        ),
        scratch_shapes=[
            pltpu.VMEM((16, count + 2 * LANES), F32),
            pltpu.VMEM((8, LANES), F32),
            pltpu.VMEM((LANES, 8), F32),
        ],
        compiler_params=pltpu.CompilerParams(vmem_limit_bytes=8 * 2**20),
        cost_estimate=pl.CostEstimate(
            flops=10 * rows * count, bytes_accessed=4 * rows * count, transcendentals=0
        ),
        name="embed_grad",
    )(grad, tap)


def in_line(pieces, width, size, first=0):
    total = jnp.zeros((1, size), F32)
    for n, piece in enumerate(pieces):
        total = total + (pltpu.roll(piece, (first + n) * width, 1) if first + n else piece)
    return total


def high_and_low(line, ntaps, width):
    taps = lax.broadcasted_iota(jnp.int32, line.shape, 1) < ntaps * width
    line = jnp.where(taps, line, 0.0)
    high = line.astype(BF16).astype(F32)
    return high + pltpu.roll(line - high, ntaps * width, 1)


def message_kernel(place, slices, found, out, rows, mixed):
    z = place[0]
    devices, _, size = out.shape
    width = found.shape[1]
    ntaps, reach = place_taps(size, width)
    rows[...] = jnp.zeros(rows.shape, F32)
    rows[:, :width] = found[...]
    sides = [rows[8 + k : 9 + k, :] for k in range(2 * reach)]
    row = lax.broadcasted_iota(jnp.int32, (devices, size), 0)
    taps = in_line([rows[k : k + 1, :] for k in range(ntaps)], width, size)
    value = jnp.broadcast_to(high_and_low(taps, ntaps, width), (devices, size))
    head = in_line(sides[:reach], width, size, 2 * ntaps)
    tail = in_line(sides[reach:], width, size, 2 * ntaps)
    value = jnp.where(row == lax.rem(z + devices - 1, devices), value + head, value)
    value = jnp.where(row == lax.rem(z + 1, devices), value + tail, value)
    part = jnp.sum(slices[:, 0, :], axis=0, keepdims=True)
    mixed[:, 0, :] = jnp.broadcast_to(part, (devices, size))
    mixed[:, 1, :] = value
    out[...] = mixed[...].astype(BF16)


def place_taps(size, width):
    reach = (size // width - 2) // 5
    return 2 * reach + 1, reach


def last_message(place, slices, found, devices):
    size = slices.shape[2]
    return pl.pallas_call(
        message_kernel,
        out_shape=jax.ShapeDtypeStruct((devices, 2, size), BF16),
        in_specs=[pl.BlockSpec(memory_space=pltpu.SMEM)]
        + [pl.BlockSpec(memory_space=pltpu.VMEM)] * 2,
        scratch_shapes=[
            pltpu.VMEM((found.shape[0], size), F32),
            pltpu.VMEM((devices, 2, size), F32),
        ],
        compiler_params=pltpu.CompilerParams(vmem_limit_bytes=6 * 2**20),
        cost_estimate=pl.CostEstimate(
            flops=4 * devices * size, bytes_accessed=8 * devices * size, transcendentals=0
        ),
        name="message",
    )(place, slices, found)


def tap_line(total, ntaps, width):
    return total + pltpu.roll(total, total.shape[1] - ntaps * width, 1)


def onward_kernel(width, place, slab, out, plain, last):
    z, nz, x = place[0], place[1], place[2]
    devices, _, size = out.shape
    ntaps, _ = place_taps(size, width)
    count = slab.shape[0]
    plain[...] = slab[...].astype(F32)
    total = jnp.sum(plain[:, 1, :], axis=0, keepdims=True)
    value = high_and_low(tap_line(total, ntaps, width), ntaps, width)
    halo = lax.broadcasted_iota(jnp.int32, (1, size), 1) >= 2 * ntaps * width
    up = jnp.where(halo & (z == 0), plain[count - 1, 1:2, :], 0.0)
    down = jnp.where(halo & (z == nz - 1), plain[0, 1:2, :], 0.0)
    slices = plain[:, 0, :].astype(BF16)
    last[...] = jnp.zeros(last.shape, F32)
    for other in range(devices):
        out[other, :count, :] = slices
        passed = jnp.where(x + 1 == other, up, 0.0) + jnp.where(x - 1 == other, down, 0.0)
        last[0:1, :] = value + passed
        out[other, count:, :] = last[...].astype(BF16)


def onward(place, slab, devices, width):
    count, _, size = slab.shape
    return pl.pallas_call(
        functools.partial(onward_kernel, width),
        out_shape=jax.ShapeDtypeStruct((devices, count + 16, size), BF16),
        in_specs=[
            pl.BlockSpec(memory_space=pltpu.SMEM),
            pl.BlockSpec(memory_space=pltpu.VMEM),
        ],
        scratch_shapes=[
            pltpu.VMEM(slab.shape, F32),
            pltpu.VMEM((16, size), F32),
        ],
        compiler_params=pltpu.CompilerParams(vmem_limit_bytes=6 * 2**20),
        cost_estimate=pl.CostEstimate(
            flops=2 * slab.size, bytes_accessed=12 * slab.size, transcendentals=0
        ),
        name="onward",
    )(place, slab)


def finish_kernel(
    place, slab, wide, ends, tap, given, embed, weight, sums,
    square, columns, edges, tiles, plain, sems,
):
    del given
    ntaps, width = tap.shape
    reach = ntaps // 2
    nz, _, size = slab.shape
    nx = wide.shape[0]
    z, x = place[0], place[2]
    plain[...] = slab[...].astype(F32)
    columns[...] = tap_columns(tap, square)

    edges[...] = jnp.zeros(edges.shape, F32)
    start = 2 * ntaps * width
    lasts = [wide[n, nz:, :].astype(F32)[0:1, :] for n in range(nx)]
    for side, step in enumerate((-1, 1)):
        inner = (z + step >= 0) & (z + step < nz)
        row = jnp.zeros((1, size), F32)
        for n in range(nx):
            row = jnp.where(x + step == n, lasts[n], row)
        row = jnp.where(inner, plain[jnp.clip(z + step, 0, nz - 1), 1:2, :], row)
        for k in range(reach):
            turned = pltpu.roll(row, size - start - k * width, 1)
            edges[side * reach + k : side * reach + k + 1, :] = turned[:, :LANES]
    outer = edges[...].T[:width]

    lane = lax.broadcasted_iota(jnp.int32, (width, LANES), 1)
    first, last = ends[:, :LANES], ends[:, LANES:]
    for column in range(reach):
        for k in range(ntaps):
            source = column - k + reach
            if source < 0:
                mirror = ntaps - 1 - k
                before = outer[:, reach + source : reach + source + 1]
                after = outer[:, reach - 1 - source : reach - source]
                value = columns[:width, k : k + 1] * before
                first = first + jnp.where(lane == column, value, 0.0)
                value = columns[:width, mirror : mirror + 1] * after
                last = last + jnp.where(lane == LANES - 1 - column, value, 0.0)
    count = embed.shape[1]
    writes = []
    for n, (tile, at) in enumerate(((first, 0), (last, count - LANES))):
        tiles[n] = tile.astype(BF16)
        writes.append(
            pltpu.make_async_copy(tiles.at[n], embed.at[:, pl.ds(at, LANES)], sems.at[n])
        )
        writes[n].start()

    per_row, across = size // LANES, weight.shape[1] // LANES
    for n in range(nx):
        block = wide[n, :nz, :].astype(F32)
        for tile in range(nz // 8 * per_row):
            group, spot = tile // per_row, tile % per_row * LANES
            number = n * (nz // 8 * per_row) + tile
            row, col = number // across * 8, number % across * LANES
            weight[row : row + 8, col : col + LANES] = block[
                group * 8 : group * 8 + 8, spot : spot + LANES
            ]

    line = tap_line(sum(lasts), ntaps, width)
    for k in range(ntaps):
        found = pltpu.roll(line, size - k * width, 1) if k else line
        sums[k : k + 1, :] = found[:, :width]
    for write in writes:
        write.wait()


def finish(place, slab, wide, ends, tap, embed, weight_shape):
    ntaps, width = tap.shape
    return pl.pallas_call(
        finish_kernel,
        out_shape=(
            jax.ShapeDtypeStruct(embed.shape, embed.dtype),
            jax.ShapeDtypeStruct(weight_shape, F32),
            jax.ShapeDtypeStruct((ntaps, width), F32),
        ),
        in_specs=[pl.BlockSpec(memory_space=pltpu.SMEM)]
        + [pl.BlockSpec(memory_space=pltpu.VMEM)] * 4
        + [pl.BlockSpec(memory_space=pl.ANY)],
        out_specs=(
            pl.BlockSpec(memory_space=pl.ANY),
            pl.BlockSpec(memory_space=pltpu.VMEM),
            pl.BlockSpec(memory_space=pltpu.VMEM),
        ),
        input_output_aliases={5: 0},
        scratch_shapes=[
            pltpu.VMEM((8, LANES), F32),
            pltpu.VMEM((LANES, 8), F32),
            pltpu.VMEM((8, LANES), F32),
            pltpu.VMEM((2, width, LANES), BF16),
            pltpu.VMEM(slab.shape, F32),
            pltpu.SemaphoreType.DMA((2,)),
        ],
        compiler_params=pltpu.CompilerParams(vmem_limit_bytes=8 * 2**20),
        cost_estimate=pl.CostEstimate(
            flops=slab.size, bytes_accessed=8 * slab.size, transcendentals=0
        ),
        name="finish",
    )(place, slab, wide, ends, tap, embed)


def shards(embeddings, taps, head_weight, targets):
    width = embeddings.shape[0]
    count = embeddings.shape[1]
    tracks = head_weight.shape[0]
    ntaps = taps.shape[0]
    reach = ntaps // 2
    y = lax.axis_index("y")
    c = lax.axis_index("c")
    ny = lax.axis_size("y")
    features = ny * 2 * width

    place = jnp.stack([y, c])
    left, right = outer_columns(embeddings, reach)
    blocks = with_rim(embeddings, left, right, taps, forward(embeddings, taps, ny))

    mine = lax.all_to_all(blocks, "y", 0, 0, tiled=True).reshape(ny * width, count)
    theirs = other_core(mine)
    weight = head_weight.T
    near, counts = near_logits(place, weight, mine, targets)
    expo, stats = far_logits(place, weight, theirs, near, counts)
    every = share(stats[:3].reshape(-1), SEQ)
    tops = every[:, :LANES]
    peak = jnp.max(tops, axis=0)
    total = jnp.sum(every[:, LANES : 2 * LANES] * jnp.exp(tops - peak[None]), axis=0)
    counts = jnp.sum(every[:, 2 * LANES :], axis=0)
    scale = counts * jnp.exp(stats[0] - peak) / jnp.where(total > 0.0, total, 1.0)
    logit_grad, sent = logit_gradient(
        place, weight, jnp.broadcast_to(scale[None], (8, LANES)), expo, targets
    )
    received = other_core(sent)

    nx, nz = lax.axis_size("x"), lax.axis_size("z")
    late_grad, _ = lax.optimization_barrier((logit_grad, sent))
    local = outer_product(place, late_grad, mine, theirs)
    own, *blocks = scatter_blocks(place, weight, logit_grad, received)
    parts = [along_y(blocks[shift - 1], shift) for shift in (2, 1, 3)]

    local, own = lax.optimization_barrier((local, own))
    part = lax.all_to_all(local.reshape(nx, tracks // nx, features), "x", 0, 0, tiled=True)
    part, own = lax.optimization_barrier((sum_to_rows(part, nz), own))
    part = lax.all_to_all(part, "z", 0, 0, tiled=True)
    conv_grad, found = backward(own, parts, embeddings, left, right, taps)

    spot = jnp.stack([lax.axis_index("z"), nz, lax.axis_index("x")])
    message = last_message(spot, part, found, nz)
    slab = lax.all_to_all(message, "z", 0, 0, tiled=True)
    wide = lax.all_to_all(onward(spot, slab, nx, width), "x", 0, 0, tiled=True)
    embed_grad, ends = spread(conv_grad, taps)
    embed_grad, weight_grad, taps_grad = finish(
        spot, slab, wide, ends, taps, embed_grad, (tracks, features)
    )
    return embed_grad, weight_grad, taps_grad


def solution(mesh):
    fine = Mesh(np.asarray(mesh.devices).reshape(4, 16, 4, 2), ("x", "z", "y", "c"))
    track = ("y", "c")
    return jax.shard_map(
        shards,
        mesh=fine,
        in_specs=(P(track, SEQ), P(None, track), P(track, None), P(track, SEQ)),
        out_specs=(P(track, SEQ), P(track, None), P(None, track)),
        check_vma=False,
    )
```

```python
import functools

import jax
import jax.numpy as jnp
import numpy as np
from jax import lax
from jax.experimental import pallas as pl
from jax.experimental.pallas import tpu as pltpu
from jax.sharding import Mesh
from jax.sharding import PartitionSpec as P

F32 = jnp.float32
BF16 = jnp.bfloat16
SEQ = ("x", "z")
LANES = 128


def along_y(value, shift):
    count = lax.axis_size("y")
    return lax.ppermute(value, "y", [(i, (i + shift) % count) for i in range(count)])


def other_core(value):
    return lax.ppermute(value, "c", [(0, 1), (1, 0)])


def outer_columns(cells, width):
    count = lax.axis_size(SEQ)
    left = lax.ppermute(cells[:, -width:], SEQ, [(i, i + 1) for i in range(count - 1)])
    right = lax.ppermute(cells[:, :width], SEQ, [(i + 1, i) for i in range(count - 1)])
    return left, right


def share(value, axes):
    count = lax.axis_size(axes)
    copies = jnp.broadcast_to(value.reshape(1, 1, -1), (count, 1, value.size))
    return lax.all_to_all(copies, axes, 0, 0, tiled=True)[:, 0]


def tap_columns(tap, square):
    count, features = tap.shape
    square[:, :] = jnp.zeros(square.shape, F32)
    square[:count, :features] = tap[...].astype(F32)
    return square[...].T


def forward_kernel(cells, tap, hidden, line, square, columns):
    rows = 16
    count = cells.shape[1]
    reach = tap.shape[0] // 2
    columns[...] = tap_columns(tap, square)
    line[:, :LANES] = jnp.zeros((rows, LANES), F32)
    line[:, LANES + count :] = jnp.zeros((rows, LANES), F32)

    @pl.loop(0, cells.shape[0] // rows, unroll=2)
    def _(block):
        at = pl.ds(pl.multiple_of(block * rows, rows), rows)
        line[:, LANES : LANES + count] = cells[at, :].astype(F32)
        whole = line[...]
        taps = columns[at, :]
        conv = jnp.zeros((rows, count), F32)
        for k in range(2 * reach + 1):
            shift = (reach - k) % whole.shape[1]
            moved = pltpu.roll(whole, shift, 1) if shift else whole
            conv = conv + taps[:, k : k + 1] * moved[:, LANES : LANES + count]
        value = (conv * jax.nn.sigmoid(conv)).astype(BF16)
        for chip in range(hidden.shape[0]):
            hidden[chip, at, :] = value


def forward(cells, tap, chips):
    rows, count = cells.shape
    return pl.pallas_call(
        forward_kernel,
        out_shape=jax.ShapeDtypeStruct((chips, rows, count), BF16),
        scratch_shapes=[
            pltpu.VMEM((16, count + 2 * LANES), F32),
            pltpu.VMEM((8, LANES), F32),
            pltpu.VMEM((LANES, 8), F32),
        ],
        compiler_params=pltpu.CompilerParams(vmem_limit_bytes=4 * 2**20),
        cost_estimate=pl.CostEstimate(
            flops=20 * rows * count, bytes_accessed=4 * rows * count, transcendentals=rows * count
        ),
        name="conv_silu",
    )(cells, tap)


def rim_kernel(cells, left, right, tap, given, hidden, line, square, columns, tiles, sems):
    del given
    width, count = cells.shape
    reach = left.shape[1]
    columns[...] = tap_columns(tap, square)
    taps = columns[:width, :]
    line[...] = jnp.zeros(line.shape, F32)
    writes = []
    for side, at in enumerate((0, count - LANES)):
        line[:, LANES : 2 * LANES] = cells[:, at : at + LANES].astype(F32)
        if side == 0:
            line[:, LANES - reach : LANES] = left[...].astype(F32)
            line[:, 2 * LANES :] = cells[:, at + LANES : at + 2 * LANES].astype(F32)
        else:
            line[:, :LANES] = cells[:, at - LANES : at].astype(F32)
            line[:, 2 * LANES : 2 * LANES + reach] = right[...].astype(F32)
        whole = line[...]
        conv = jnp.zeros((width, LANES), F32)
        for k in range(2 * reach + 1):
            shift = (reach - k) % whole.shape[1]
            moved = pltpu.roll(whole, shift, 1) if shift else whole
            conv = conv + taps[:, k : k + 1] * moved[:, LANES : 2 * LANES]
        tiles[side] = (conv * jax.nn.sigmoid(conv)).astype(BF16)
        for chip in range(hidden.shape[0]):
            spot = hidden.at[chip, :, pl.ds(at, LANES)]
            sem = sems.at[2 * chip + side]
            writes.append(pltpu.make_async_copy(tiles.at[side], spot, sem))
            writes[-1].start()
    for write in writes:
        write.wait()


def with_rim(cells, left, right, tap, hidden):
    width, _ = cells.shape
    return pl.pallas_call(
        rim_kernel,
        out_shape=jax.ShapeDtypeStruct(hidden.shape, hidden.dtype),
        in_specs=[pl.BlockSpec(memory_space=pltpu.VMEM)] * 4
        + [pl.BlockSpec(memory_space=pl.ANY)],
        out_specs=pl.BlockSpec(memory_space=pl.ANY),
        input_output_aliases={4: 0},
        scratch_shapes=[
            pltpu.VMEM((width, 3 * LANES), F32),
            pltpu.VMEM((8, LANES), F32),
            pltpu.VMEM((LANES, 8), F32),
            pltpu.VMEM((2, width, LANES), BF16),
            pltpu.SemaphoreType.DMA((2 * hidden.shape[0],)),
        ],
        compiler_params=pltpu.CompilerParams(vmem_limit_bytes=4 * 2**20),
        cost_estimate=pl.CostEstimate(
            flops=40 * width * LANES, bytes_accessed=8 * width * LANES, transcendentals=0
        ),
        name="outer_columns",
    )(cells, left, right, tap, hidden)


def pick_rows(weight, picked, blocks):
    width = picked.shape[0] // 4
    for chip, block in enumerate(blocks):
        at = pl.ds(pl.multiple_of(block * width, 16), width)
        picked[chip * width : (chip + 1) * width, :] = weight[at, :]


TURN = (((0,), (0,)), ((), ()))


def near_kernel(place, weight, hidden, targets, logits, counts, picked):
    pick_rows(weight, picked, [2 * chip + place[1] for chip in range(4)])
    logits[...] = lax.dot_general(picked[...], hidden[...], TURN, preferred_element_type=F32)
    counts[...] = jnp.broadcast_to(jnp.sum(targets[...], axis=1, keepdims=True), counts.shape)


def far_kernel(place, weight, hidden, near, counts, expo, stats, picked, table):
    tracks = near.shape[0]
    pick_rows(weight, picked, [2 * chip + 1 - place[1] for chip in range(4)])
    logits = lax.dot_general(picked[...], hidden[...], TURN, preferred_element_type=F32)
    logits = logits + near[...]
    top = jnp.max(logits, axis=1, keepdims=True)
    value = jnp.exp(logits - top)
    expo[...] = value
    total = jnp.sum(value, axis=1, keepdims=True)
    lane = lax.broadcasted_iota(jnp.int32, (tracks, LANES), 1)
    table[...] = jnp.zeros(table.shape, F32)
    table[:tracks, :] = jnp.where(lane == 0, top, jnp.where(lane == 1, total, counts[...]))
    stats[...] = table[...].T[: stats.shape[0]]


def kernel_call(body, name, outs, scratch, place, *operands, flops=0):
    size = sum(o.size * o.dtype.itemsize for o in operands)
    size += sum(o.size * o.dtype.itemsize for o in outs)
    return pl.pallas_call(
        body,
        out_shape=outs,
        in_specs=[pl.BlockSpec(memory_space=pltpu.SMEM)]
        + [pl.BlockSpec(memory_space=pltpu.VMEM)] * len(operands),
        scratch_shapes=scratch,
        compiler_params=pltpu.CompilerParams(vmem_limit_bytes=size + 4 * 2**20),
        cost_estimate=pl.CostEstimate(flops=flops, bytes_accessed=size, transcendentals=0),
        name=name,
    )(place, *operands)


def near_logits(place, weight, hidden, targets):
    tracks, count = targets.shape
    outs = (
        jax.ShapeDtypeStruct((tracks, count), F32),
        jax.ShapeDtypeStruct((tracks, LANES), F32),
    )
    scratch = [pltpu.VMEM((hidden.shape[0], tracks), BF16)]
    return kernel_call(
        near_kernel, "near_logits", outs, scratch, place, weight, hidden, targets,
        flops=2 * hidden.size * tracks,
    )


def far_logits(place, weight, hidden, near, counts):
    tracks = near.shape[0]
    outs = (
        jax.ShapeDtypeStruct(near.shape, F32),
        jax.ShapeDtypeStruct((8, LANES), F32),
    )
    scratch = [
        pltpu.VMEM((hidden.shape[0], tracks), BF16),
        pltpu.VMEM((LANES, LANES), F32),
    ]
    return kernel_call(
        far_kernel, "far_logits", outs, scratch, place, weight, hidden, near, counts,
        flops=2 * hidden.size * tracks,
    )


def grad_kernel(place, weight, scale, expo, targets, grad, sent, picked):
    tracks = expo.shape[0]
    column = scale[...].T[:tracks, 0:1]
    value = (column * expo[...] - targets[...]).astype(BF16)
    grad[...] = value
    blocks = [2 * lax.rem(place[0] + shift, 4) + 1 - place[1] for shift in range(4)]
    pick_rows(weight, picked, blocks)
    sent[...] = jnp.dot(picked[...], value, preferred_element_type=F32).astype(BF16)


def logit_gradient(place, weight, scale, expo, targets):
    tracks, count = expo.shape
    outs = (
        jax.ShapeDtypeStruct((tracks, count), BF16),
        jax.ShapeDtypeStruct((weight.shape[0] // 2, count), BF16),
    )
    scratch = [pltpu.VMEM((weight.shape[0] // 2, tracks), BF16)]
    return kernel_call(
        grad_kernel, "logit_grad", outs, scratch, place, weight, scale, expo, targets,
        flops=weight.size * count,
    )


def scatter_kernel(place, weight, grad, received, mine, one, two, three, picked):
    width = mine.shape[0]
    blocks = [2 * lax.rem(place[0] + shift, 4) + place[1] for shift in range(4)]
    pick_rows(weight, picked, blocks)
    part = jnp.dot(picked[...], grad[...], preferred_element_type=F32)
    for shift, out in enumerate((mine, one, two, three)):
        at = slice(shift * width, (shift + 1) * width)
        out[...] = (part[at] + received[at, :].astype(F32)).astype(out.dtype)


def scatter_blocks(place, weight, grad, received):
    tracks, count = grad.shape
    width = received.shape[0] // 4
    block = jax.ShapeDtypeStruct((width, count), BF16)
    outs = (jax.ShapeDtypeStruct((width, count), F32), block, block, block)
    scratch = [pltpu.VMEM((received.shape[0], tracks), BF16)]
    return kernel_call(
        scatter_kernel, "core_sum", outs, scratch, place, weight, grad, received,
        flops=weight.size * count,
    )


def outer_kernel(place, grad, mine, theirs, out, table):
    tracks = grad.shape[0]
    width = mine.shape[0] // 4
    along = (((1,), (1,)), ((), ()))
    for block, offset in ((mine, place[1]), (theirs, 1 - place[1])):
        part = lax.dot_general(block[...], grad[...], along, preferred_element_type=F32)
        for chip in range(4):
            row = (2 * chip + offset) * width
            at = pl.ds(pl.multiple_of(row, 16), width)
            table[at, :tracks] = part[chip * width : (chip + 1) * width]
    out[...] = table[...].T[:tracks]


def outer_product(place, grad, mine, theirs):
    tracks = grad.shape[0]
    features = 2 * mine.shape[0]
    return kernel_call(
        outer_kernel, "weight_part", (jax.ShapeDtypeStruct((tracks, features), F32),),
        [pltpu.VMEM((features, LANES), F32)], place, grad, mine, theirs,
        flops=2 * features * grad.size,
    )[0]


def rows_kernel(parts, out):
    wide = parts.shape[2] // LANES
    tiles = out.shape[2] // LANES
    for tile in range(parts.shape[1] // 8 * wide):
        row, lane = tile // wide * 8, tile % wide * LANES
        group, spot = tile // tiles, tile % tiles * LANES
        total = jnp.sum(parts[:, row : row + 8, lane : lane + LANES], axis=0)
        out[group * 8 : group * 8 + 8, 0, spot : spot + LANES] = total


def sum_to_rows(parts, rows):
    size = parts.shape[1] * parts.shape[2]
    return pl.pallas_call(
        rows_kernel,
        out_shape=jax.ShapeDtypeStruct((rows, 1, size // rows), F32),
        compiler_params=pltpu.CompilerParams(vmem_limit_bytes=8 * 2**20),
        cost_estimate=pl.CostEstimate(flops=4 * size, bytes_accessed=20 * size, transcendentals=0),
        name="sum_to_rows",
    )(parts)


def backward_kernel(
    mine, one, two, three, cells, left, right, tap, grad, rows_out, line, table, sides, sems,
    square, columns,
):
    reach = left.shape[1]
    count = cells.shape[1]
    rows = 16
    copies = [
        pltpu.make_async_copy(side, sides.at[i], sems.at[i])
        for i, side in enumerate((left, right))
    ]
    for copy in copies:
        copy.start()
    lane = lax.broadcasted_iota(jnp.int32, (rows, LANES), 1)
    columns[...] = tap_columns(tap, square)
    line[:, :LANES] = jnp.zeros((rows, LANES), F32)
    line[:, LANES + count :] = jnp.zeros((rows, LANES), F32)
    for copy in copies:
        copy.wait()

    @pl.loop(0, cells.shape[0] // rows, unroll=2)
    def _(block):
        at = pl.ds(pl.multiple_of(block * rows, rows), rows)
        line[:, LANES - reach : LANES] = sides[0, at, :].astype(F32)
        line[:, LANES + count : LANES + count + reach] = sides[1, at, :].astype(F32)
        line[:, LANES : LANES + count] = cells[at, :].astype(F32)
        whole = line[...]
        taps = columns[at, :]
        moved = []
        conv = jnp.zeros((rows, count), F32)
        for k in range(2 * reach + 1):
            shift = (reach - k) % whole.shape[1]
            turned = pltpu.roll(whole, shift, 1) if shift else whole
            moved.append(turned[:, LANES : LANES + count])
            conv = conv + taps[:, k : k + 1] * moved[k]
        sig = jax.nn.sigmoid(conv)
        total = mine[at, :] + one[at, :].astype(F32)
        total = total + two[at, :].astype(F32) + three[at, :].astype(F32)
        value = (total * (sig * (1.0 + conv * (1.0 - sig)))).astype(BF16)
        grad[at, :] = value
        value = value.astype(F32)
        found = jnp.zeros((rows, LANES), F32)
        for k in range(2 * reach + 1):
            found = jnp.where(lane == k, jnp.sum(moved[k] * value, axis=1, keepdims=True), found)
        for k in range(reach):
            found = jnp.where(lane == 8 + k, value[:, k : k + 1], found)
            last = count - reach + k
            found = jnp.where(lane == 8 + reach + k, value[:, last : last + 1], found)
        table[at, :] = found

    rows_out[...] = table[...].T[: rows_out.shape[0]]


def backward(mine, parts, cells, left, right, tap):
    rows, count = cells.shape
    return pl.pallas_call(
        backward_kernel,
        out_shape=(
            jax.ShapeDtypeStruct((rows, count), BF16),
            jax.ShapeDtypeStruct((16, rows), F32),
        ),
        in_specs=[pl.BlockSpec(memory_space=pltpu.VMEM)] * 5
        + [pl.BlockSpec(memory_space=pl.ANY)] * 2
        + [pl.BlockSpec(memory_space=pltpu.VMEM)],
        scratch_shapes=[
            pltpu.VMEM((16, count + 2 * LANES), F32),
            pltpu.VMEM((rows, LANES), F32),
            pltpu.VMEM((2,) + left.shape, left.dtype),
            pltpu.SemaphoreType.DMA((2,)),
            pltpu.VMEM((8, LANES), F32),
            pltpu.VMEM((LANES, 8), F32),
        ],
        compiler_params=pltpu.CompilerParams(vmem_limit_bytes=8 * 2**20),
        cost_estimate=pl.CostEstimate(
            flops=40 * rows * count, bytes_accessed=14 * rows * count, transcendentals=0
        ),
        name="conv_grad",
    )(mine, *parts, cells, left, right, tap)


def spread_kernel(grad, tap, embed, ends, line, square, columns):
    count = grad.shape[1]
    rows = 16
    reach = tap.shape[0] // 2
    columns[...] = tap_columns(tap, square)
    line[:, :LANES] = jnp.zeros((rows, LANES), F32)
    line[:, LANES + count :] = jnp.zeros((rows, LANES), F32)

    @pl.loop(0, grad.shape[0] // rows)
    def _(block):
        at = pl.ds(pl.multiple_of(block * rows, rows), rows)
        line[:, LANES : LANES + count] = grad[at, :].astype(F32)
        whole = line[...]
        taps = columns[at, :]
        total = jnp.zeros((rows, count), F32)
        for k in range(2 * reach + 1):
            shift = (k - reach) % whole.shape[1]
            moved = pltpu.roll(whole, shift, 1) if shift else whole
            total = total + taps[:, k : k + 1] * moved[:, LANES : LANES + count]
        embed[at, :] = total.astype(BF16)
        ends[at, :LANES] = total[:, :LANES]
        ends[at, LANES:] = total[:, count - LANES :]


def spread(grad, tap):
    rows, count = grad.shape
    return pl.pallas_call(
        spread_kernel,
        out_shape=(
            jax.ShapeDtypeStruct((rows, count), BF16),
            jax.ShapeDtypeStruct((rows, 2 * LANES), F32),
        ),
        scratch_shapes=[
            pltpu.VMEM((16, count + 2 * LANES), F32),
            pltpu.VMEM((8, LANES), F32),
            pltpu.VMEM((LANES, 8), F32),
        ],
        compiler_params=pltpu.CompilerParams(vmem_limit_bytes=8 * 2**20),
        cost_estimate=pl.CostEstimate(
            flops=10 * rows * count, bytes_accessed=4 * rows * count, transcendentals=0
        ),
        name="embed_grad",
    )(grad, tap)


def in_line(pieces, width, size, first=0):
    total = jnp.zeros((1, size), F32)
    for n, piece in enumerate(pieces):
        total = total + (pltpu.roll(piece, (first + n) * width, 1) if first + n else piece)
    return total


def high_and_low(line, ntaps, width):
    taps = lax.broadcasted_iota(jnp.int32, line.shape, 1) < ntaps * width
    line = jnp.where(taps, line, 0.0)
    high = line.astype(BF16).astype(F32)
    return high + pltpu.roll(line - high, ntaps * width, 1)


def message_kernel(place, slices, found, out, rows, mixed):
    z = place[0]
    devices, _, size = out.shape
    width = found.shape[1]
    ntaps, reach = place_taps(size, width)
    rows[...] = jnp.zeros(rows.shape, F32)
    rows[:, :width] = found[...]
    sides = [rows[8 + k : 9 + k, :] for k in range(2 * reach)]
    row = lax.broadcasted_iota(jnp.int32, (devices, size), 0)
    taps = in_line([rows[k : k + 1, :] for k in range(ntaps)], width, size)
    value = jnp.broadcast_to(high_and_low(taps, ntaps, width), (devices, size))
    head = in_line(sides[:reach], width, size, 2 * ntaps)
    tail = in_line(sides[reach:], width, size, 2 * ntaps)
    value = jnp.where(row == lax.rem(z + devices - 1, devices), value + head, value)
    value = jnp.where(row == lax.rem(z + 1, devices), value + tail, value)
    part = jnp.sum(slices[:, 0, :], axis=0, keepdims=True)
    mixed[:, 0, :] = jnp.broadcast_to(part, (devices, size))
    mixed[:, 1, :] = value
    out[...] = mixed[...].astype(BF16)


def place_taps(size, width):
    reach = (size // width - 2) // 5
    return 2 * reach + 1, reach


def last_message(place, slices, found, devices):
    size = slices.shape[2]
    return pl.pallas_call(
        message_kernel,
        out_shape=jax.ShapeDtypeStruct((devices, 2, size), BF16),
        in_specs=[pl.BlockSpec(memory_space=pltpu.SMEM)]
        + [pl.BlockSpec(memory_space=pltpu.VMEM)] * 2,
        scratch_shapes=[
            pltpu.VMEM((found.shape[0], size), F32),
            pltpu.VMEM((devices, 2, size), F32),
        ],
        compiler_params=pltpu.CompilerParams(vmem_limit_bytes=6 * 2**20),
        cost_estimate=pl.CostEstimate(
            flops=4 * devices * size, bytes_accessed=8 * devices * size, transcendentals=0
        ),
        name="message",
    )(place, slices, found)


def tap_line(total, ntaps, width):
    return total + pltpu.roll(total, total.shape[1] - ntaps * width, 1)


def onward_kernel(width, place, slab, out, plain, last):
    z, nz, x = place[0], place[1], place[2]
    devices, _, size = out.shape
    ntaps, _ = place_taps(size, width)
    count = slab.shape[0]
    plain[...] = slab[...].astype(F32)
    total = jnp.sum(plain[:, 1, :], axis=0, keepdims=True)
    value = high_and_low(tap_line(total, ntaps, width), ntaps, width)
    halo = lax.broadcasted_iota(jnp.int32, (1, size), 1) >= 2 * ntaps * width
    up = jnp.where(halo & (z == 0), plain[count - 1, 1:2, :], 0.0)
    down = jnp.where(halo & (z == nz - 1), plain[0, 1:2, :], 0.0)
    slices = plain[:, 0, :].astype(BF16)
    last[...] = jnp.zeros(last.shape, F32)
    for other in range(devices):
        out[other, :count, :] = slices
        passed = jnp.where(x + 1 == other, up, 0.0) + jnp.where(x - 1 == other, down, 0.0)
        last[0:1, :] = value + passed
        out[other, count:, :] = last[...].astype(BF16)


def onward(place, slab, devices, width):
    count, _, size = slab.shape
    return pl.pallas_call(
        functools.partial(onward_kernel, width),
        out_shape=jax.ShapeDtypeStruct((devices, count + 16, size), BF16),
        in_specs=[
            pl.BlockSpec(memory_space=pltpu.SMEM),
            pl.BlockSpec(memory_space=pltpu.VMEM),
        ],
        scratch_shapes=[
            pltpu.VMEM(slab.shape, F32),
            pltpu.VMEM((16, size), F32),
        ],
        compiler_params=pltpu.CompilerParams(vmem_limit_bytes=6 * 2**20),
        cost_estimate=pl.CostEstimate(
            flops=2 * slab.size, bytes_accessed=12 * slab.size, transcendentals=0
        ),
        name="onward",
    )(place, slab)


def finish_kernel(
    place, slab, wide, ends, tap, given, embed, weight, sums,
    square, columns, edges, tiles, plain, sems,
):
    del given
    ntaps, width = tap.shape
    reach = ntaps // 2
    nz, _, size = slab.shape
    nx = wide.shape[0]
    z, x = place[0], place[2]
    plain[...] = slab[...].astype(F32)
    columns[...] = tap_columns(tap, square)

    edges[...] = jnp.zeros(edges.shape, F32)
    start = 2 * ntaps * width
    lasts = [wide[n, nz:, :].astype(F32)[0:1, :] for n in range(nx)]
    for side, step in enumerate((-1, 1)):
        inner = (z + step >= 0) & (z + step < nz)
        row = jnp.zeros((1, size), F32)
        for n in range(nx):
            row = jnp.where(x + step == n, lasts[n], row)
        row = jnp.where(inner, plain[jnp.clip(z + step, 0, nz - 1), 1:2, :], row)
        for k in range(reach):
            turned = pltpu.roll(row, size - start - k * width, 1)
            edges[side * reach + k : side * reach + k + 1, :] = turned[:, :LANES]
    outer = edges[...].T[:width]

    lane = lax.broadcasted_iota(jnp.int32, (width, LANES), 1)
    first, last = ends[:, :LANES], ends[:, LANES:]
    for column in range(reach):
        for k in range(ntaps):
            source = column - k + reach
            if source < 0:
                mirror = ntaps - 1 - k
                before = outer[:, reach + source : reach + source + 1]
                after = outer[:, reach - 1 - source : reach - source]
                value = columns[:width, k : k + 1] * before
                first = first + jnp.where(lane == column, value, 0.0)
                value = columns[:width, mirror : mirror + 1] * after
                last = last + jnp.where(lane == LANES - 1 - column, value, 0.0)
    count = embed.shape[1]
    writes = []
    for n, (tile, at) in enumerate(((first, 0), (last, count - LANES))):
        tiles[n] = tile.astype(BF16)
        writes.append(
            pltpu.make_async_copy(tiles.at[n], embed.at[:, pl.ds(at, LANES)], sems.at[n])
        )
        writes[n].start()

    per_row, across = size // LANES, weight.shape[1] // LANES
    for n in range(nx):
        block = wide[n, :nz, :].astype(F32)
        for tile in range(nz // 8 * per_row):
            group, spot = tile // per_row, tile % per_row * LANES
            number = n * (nz // 8 * per_row) + tile
            row, col = number // across * 8, number % across * LANES
            weight[row : row + 8, col : col + LANES] = block[
                group * 8 : group * 8 + 8, spot : spot + LANES
            ]

    line = tap_line(sum(lasts), ntaps, width)
    for k in range(ntaps):
        found = pltpu.roll(line, size - k * width, 1) if k else line
        sums[k : k + 1, :] = found[:, :width]
    for write in writes:
        write.wait()


def finish(place, slab, wide, ends, tap, embed, weight_shape):
    ntaps, width = tap.shape
    return pl.pallas_call(
        finish_kernel,
        out_shape=(
            jax.ShapeDtypeStruct(embed.shape, embed.dtype),
            jax.ShapeDtypeStruct(weight_shape, F32),
            jax.ShapeDtypeStruct((ntaps, width), F32),
        ),
        in_specs=[pl.BlockSpec(memory_space=pltpu.SMEM)]
        + [pl.BlockSpec(memory_space=pltpu.VMEM)] * 4
        + [pl.BlockSpec(memory_space=pl.ANY)],
        out_specs=(
            pl.BlockSpec(memory_space=pl.ANY),
            pl.BlockSpec(memory_space=pltpu.VMEM),
            pl.BlockSpec(memory_space=pltpu.VMEM),
        ),
        input_output_aliases={5: 0},
        scratch_shapes=[
            pltpu.VMEM((8, LANES), F32),
            pltpu.VMEM((LANES, 8), F32),
            pltpu.VMEM((8, LANES), F32),
            pltpu.VMEM((2, width, LANES), BF16),
            pltpu.VMEM(slab.shape, F32),
            pltpu.SemaphoreType.DMA((2,)),
        ],
        compiler_params=pltpu.CompilerParams(vmem_limit_bytes=8 * 2**20),
        cost_estimate=pl.CostEstimate(
            flops=slab.size, bytes_accessed=8 * slab.size, transcendentals=0
        ),
        name="finish",
    )(place, slab, wide, ends, tap, embed)


def shards(embeddings, taps, head_weight, targets):
    width = embeddings.shape[0]
    count = embeddings.shape[1]
    tracks = head_weight.shape[0]
    ntaps = taps.shape[0]
    reach = ntaps // 2
    y = lax.axis_index("y")
    c = lax.axis_index("c")
    ny = lax.axis_size("y")
    features = ny * 2 * width

    place = jnp.stack([y, c])
    left, right = outer_columns(embeddings, reach)
    blocks = with_rim(embeddings, left, right, taps, forward(embeddings, taps, ny))

    mine = lax.all_to_all(blocks, "y", 0, 0, tiled=True).reshape(ny * width, count)
    theirs = other_core(mine)
    weight = head_weight.T
    near, counts = near_logits(place, weight, mine, targets)
    expo, stats = far_logits(place, weight, theirs, near, counts)
    every = share(stats[:3].reshape(-1), SEQ)
    tops = every[:, :LANES]
    peak = jnp.max(tops, axis=0)
    total = jnp.sum(every[:, LANES : 2 * LANES] * jnp.exp(tops - peak[None]), axis=0)
    counts = jnp.sum(every[:, 2 * LANES :], axis=0)
    scale = counts * jnp.exp(stats[0] - peak) / jnp.where(total > 0.0, total, 1.0)
    logit_grad, sent = logit_gradient(
        place, weight, jnp.broadcast_to(scale[None], (8, LANES)), expo, targets
    )
    received = other_core(sent)

    nx, nz = lax.axis_size("x"), lax.axis_size("z")
    late_grad, _ = lax.optimization_barrier((logit_grad, sent))
    local = outer_product(place, late_grad, mine, theirs)
    own, *blocks = scatter_blocks(place, weight, logit_grad, received)
    parts = [along_y(blocks[shift - 1], shift) for shift in (2, 1, 3)]

    local, own = lax.optimization_barrier((local, own))
    part = lax.all_to_all(local.reshape(nx, tracks // nx, features), "x", 0, 0, tiled=True)
    part, own = lax.optimization_barrier((sum_to_rows(part, nz), own))
    part = lax.all_to_all(part, "z", 0, 0, tiled=True)
    conv_grad, found = backward(own, parts, embeddings, left, right, taps)

    spot = jnp.stack([lax.axis_index("z"), nz, lax.axis_index("x")])
    message = last_message(spot, part, found, nz)
    slab = lax.all_to_all(message, "z", 0, 0, tiled=True)
    wide = lax.all_to_all(onward(spot, slab, nx, width), "x", 0, 0, tiled=True)
    embed_grad, ends = spread(conv_grad, taps)
    embed_grad, weight_grad, taps_grad = finish(
        spot, slab, wide, ends, taps, embed_grad, (tracks, features)
    )
    return embed_grad, weight_grad, taps_grad


def solution(mesh):
    fine = Mesh(np.asarray(mesh.devices).reshape(4, 16, 4, 2), ("x", "z", "y", "c"))
    track = ("y", "c")
    return jax.shard_map(
        shards,
        mesh=fine,
        in_specs=(P(track, SEQ), P(None, track), P(track, None), P(track, SEQ)),
        out_specs=(P(track, SEQ), P(track, None), P(None, track)),
        check_vma=False,
    )
```
